32 devices in a mesh: dp: 8 (over y, x, core), seq: 4 (over z).
Axes of the slice: x: 2, y: 2, z: 4, core: 2. Of those that a mesh axis runs over, the one named last changes fastest.
Arguments:
- tokens: bfloat16 [24, 1024, 768], P('dp', 'seq'), may hold values from -6 to 6
- segments: int32 [24, 1024], P('dp', 'seq'), may hold values from 0 to 7, as said below
- timesteps: int32 [24], P('dp'), may hold values from 0 to 999
- w_mod: bfloat16 [768, 4608], P(('dp', 'seq')), may hold values from -0.21875 to 0.21875
- b_mod: bfloat16 [4608], P(('dp', 'seq')), may hold values from -3 to 3
- gain_attn: bfloat16 [768], P(('dp', 'seq')), may hold values from 0.25 to 1.75
- w_qkv: bfloat16 [768, 2304], P(('dp', 'seq')), may hold values from -0.21875 to 0.21875
- w_out: bfloat16 [768, 768], P(('dp', 'seq')), may hold values from -1.75 to 1.75
- gain_mlp: bfloat16 [768], P(('dp', 'seq')), may hold values from 0.25 to 1.75
- w_up: bfloat16 [768, 3072], P(('dp', 'seq')), may hold values from -0.21875 to 0.21875
- w_down: bfloat16 [3072, 768], P(('dp', 'seq')), may hold values from -0.109375 to 0.109375
- cotangent: bfloat16 [24, 1024, 768], P('dp', 'seq'), may hold values from -6 to 6
Outputs:
- output: bfloat16 [24, 1024, 768], P('dp', 'seq')
- d_tokens: bfloat16 [24, 1024, 768], P('dp', 'seq')
- g_w_mod: float32 [768, 4608], P(('dp', 'seq'))
- g_b_mod: float32 [4608], P(('dp', 'seq'))
- g_gain_attn: float32 [768], P(('dp', 'seq'))
- g_w_qkv: float32 [768, 2304], P(('dp', 'seq'))
- g_w_out: float32 [768, 768], P(('dp', 'seq'))
- g_gain_mlp: float32 [768], P(('dp', 'seq'))
- g_w_up: float32 [768, 3072], P(('dp', 'seq'))
- g_w_down: float32 [3072, 768], P(('dp', 'seq'))
The draws below stay inside these ranges and needn't reach their ends.
Inputs may be any that keep to these rules, and one draw needn't show every extreme that they name: `segments`: in each row segment numbers start at 0 and never fall from one position to the next; a token attends only to tokens of its own segment.
All inputs are finite; a program needn't handle non-finite values.
Results may differ from the reference program's by a relative error of at most 0.018.
Values may be sent and summed in bfloat16 or wider, within the bound.
A program may use at most 192 MiB of HBM per device.

```python
import math
import jax
import jax.numpy as jnp
from jax import lax

D = 768
FF = 3072
HEAD_DIM = 64
SEQ = 1024
CUTS = 7
ROWS_DEV = 3
ROWS = 24


def draw_segments(key, part):
    key = jax.random.fold_in(key, 11)
    pick_key, cut_key, long_key = jax.random.split(key, 3)
    cut_points = jax.random.randint(cut_key, (ROWS, CUTS), 1, SEQ)
    near_ends = jax.random.randint(long_key, (ROWS, CUTS), 1, SEQ // 4)
    near_ends = jnp.where(near_ends < SEQ // 8, near_ends, near_ends + 3 * (SEQ // 4))
    chosen = jax.random.randint(pick_key, (ROWS // ROWS_DEV,), 0, ROWS_DEV)
    row_index = jnp.arange(ROWS, dtype=jnp.int32)
    spanning = row_index % ROWS_DEV == jnp.repeat(chosen, ROWS_DEV)
    cut_points = jnp.where(spanning[:, None], near_ends, cut_points)
    places = jnp.arange(SEQ, dtype=jnp.int32)
    passed = (cut_points[:, None, :] <= places[None, :, None]).astype(jnp.int32)
    return jnp.sum(passed, -1).astype(jnp.int32)


def set_ends(entries, key, smallest, high):
    spot = [jax.random.randint(jax.random.fold_in(key, axis), (), 0, length) for axis, length in enumerate(entries.shape)]
    main_axis = entries.shape.index(max(entries.shape))
    beside = spot[:main_axis] + [(spot[main_axis] + 1) % entries.shape[main_axis]] + spot[main_axis + 1:]
    return entries.at[tuple(spot)].set(smallest).at[tuple(beside)].set(high)


def spiked(values, rng, source, target, blocks, factor):
    owner, partner = [(jnp.arange(values.shape[axis_at]) // (values.shape[axis_at] // blocks)).reshape([-1 if axis == axis_at else 1 for axis in range(values.ndim)]) for axis_at in (source, target)]
    chosen = jax.random.permutation(rng, blocks)[partner]
    strong = (owner == chosen) | (owner == (partner + blocks // 2) % blocks)
    return jnp.where(strong, factor * values, values)


def levels(rng, dims, pieces, least, largest):
    def one(position, shards_of):
        steps = jax.random.uniform(jax.random.fold_in(jax.random.fold_in(rng, 6), position), (shards_of,), jnp.float32, least / len(pieces), largest / len(pieces))
        return jnp.repeat(jnp.exp(steps), dims[position] // shards_of).reshape((-1,) + (1,) * (len(dims) - position - 1))

    loudness = one(*pieces[0])
    for cut in pieces[1:]:
        loudness = loudness * one(*cut)
    return loudness


def bell_draw(stream_key, shape, deviation, reach, cuts=(), kind=jnp.bfloat16):
    result = deviation * jax.random.normal(stream_key, shape, jnp.float32)
    if cuts:
        result = result * levels(stream_key, shape, cuts, -0.22, 0.18)
    return jnp.clip(result, -reach, reach).astype(kind)


def noise_with(stream_key, extent, width, bound, cuts, heavy, kind=jnp.bfloat16):
    result = width * jax.random.normal(stream_key, extent, jnp.float32)
    if cuts:
        result = result * levels(stream_key, extent, cuts, -0.22, 0.18)
    return jnp.clip(spiked(result, jax.random.fold_in(stream_key, 3), *heavy), -bound, bound).astype(kind)


def setup_inputs(seed: int = 0) -> dict:
    splits = jax.random.split(jax.random.key(seed), 13)
    tokens = bell_draw(splits[0], (ROWS, SEQ, D), 1.0, 6.0, ((0, 8), (1, 4)))
    segments = draw_segments(jax.random.fold_in(splits[12], 71), 0)
    timesteps = set_ends(jax.random.randint(splits[2], (ROWS,), 0, 1000), jax.random.fold_in(splits[2], 1), 0, 999).astype(jnp.int32)
    w_mod = bell_draw(splits[3], (D, 6 * D), D ** -0.5, 0.21875, ((0, 32),))
    b_mod = bell_draw(splits[4], (6 * D,), 0.5, 3.0, ((0, 32),))
    gain_attn = jnp.clip(1.0 + 0.15 * jax.random.normal(splits[5], (D,), jnp.float32), 0.25, 1.75).astype(jnp.bfloat16)
    w_qkv = bell_draw(splits[6], (D, 3 * D), D ** -0.5, 0.21875, ((0, 32),))
    w_out = bell_draw(splits[7], (D, D), (max(D // 64, 4)) ** -0.5, 1.75, ((0, 32),))
    gain_mlp = jnp.clip(1.0 + 0.15 * jax.random.normal(splits[8], (D,), jnp.float32), 0.25, 1.75).astype(jnp.bfloat16)
    w_up = bell_draw(splits[9], (D, FF), D ** -0.5, 0.21875, ((0, 32),))
    w_down = bell_draw(splits[10], (FF, D), FF ** -0.5, 0.109375, ((0, 32),))
    cotangent = noise_with(splits[11], (ROWS, SEQ, D), 1.0, 6.0, ((0, 8), (1, 4)), (0, 2, 8, 2.0))
    return {"tokens": tokens, "segments": segments, "timesteps": timesteps, "w_mod": w_mod, "b_mod": b_mod, "gain_attn": gain_attn, "w_qkv": w_qkv, "w_out": w_out, "gain_mlp": gain_mlp, "w_up": w_up, "w_down": w_down, "cotangent": cotangent}


@jax.custom_vjp
def low(v):
    return lax.optimization_barrier(v.astype(jnp.bfloat16)).astype(jnp.float32)

@jax.custom_vjp
def low_back(v):
    return v

def low_keep(v):
    return (low(v), None)

def low_pass(kept, grad):
    return (grad,)

def back_keep(v):
    return (v, None)

def back_low(kept, grad):
    return (low(grad),)
low.defvjp(low_keep, low_pass)
low_back.defvjp(back_keep, back_low)
EPSILON = 1e-06
MASK_FILL = -1e+30

def multiply(left, right):
    return jnp.dot(left, right, precision=lax.Precision.HIGHEST, preferred_element_type=jnp.float32)

def time_embed(step_ids, model_dim):
    half_dim = model_dim // 2
    frequency = jnp.exp(-math.log(10000.0) * jnp.arange(half_dim, dtype=jnp.float32) / half_dim)
    angles = step_ids.astype(jnp.float32)[:, None] * frequency[None, :]
    return jnp.concatenate([jnp.cos(angles), jnp.sin(angles)], axis=-1)

def rotary_tables(positions, half_dim):
    frequency = jnp.exp(-math.log(10000.0) * jnp.arange(half_dim, dtype=jnp.float32) / half_dim)
    angles = positions.astype(jnp.float32)[:, None] * frequency[None, :]
    cosine = jnp.concatenate([jnp.cos(angles), jnp.cos(angles)], -1)[:, None, None, :]
    sine_table = jnp.concatenate([jnp.sin(angles), jnp.sin(angles)], -1)[:, None, None, :]
    return (cosine, sine_table)

def rotate(paired, positions):
    half_dim = paired.shape[-1] // 2
    cosine, sine_table = rotary_tables(positions, half_dim)
    front_half = paired[..., :half_dim]
    back_half = paired[..., half_dim:]
    turned = jnp.concatenate([-back_half, front_half], -1)
    return paired * cosine + turned * sine_table

def modulate(inputs, norm_gain, mod_scale, mod_shift):
    average = lax.optimization_barrier(jnp.mean(inputs, -1, keepdims=True))
    centred = inputs - average
    variance = lax.optimization_barrier(jnp.mean(centred * centred, -1, keepdims=True))
    return centred * lax.rsqrt(variance + EPSILON) * norm_gain * (1.0 + mod_scale) + mod_shift

def layer_row(stream, doc_ids, modulation, gain_attn, w_qkv, w_out, gain_mlp, w_up, w_down):
    shift_a, scale_a, gate_a, shift_m, scale_m, gate_m = jnp.split(modulation, 6)
    seq_len, model_dim = stream.shape
    head_count = model_dim // HEAD_DIM
    positions = jnp.arange(seq_len, dtype=jnp.int32)
    score_scale = 1.0 / math.sqrt(HEAD_DIM)
    normed_a = low(modulate(stream, gain_attn, scale_a, shift_a))
    qkv_proj = low_back(multiply(normed_a, w_qkv)).reshape(seq_len, 3, head_count, HEAD_DIM)
    turned = rotate(qkv_proj[:, :2], positions)
    packed = low(low_back(jnp.concatenate([turned, qkv_proj[:, 2:]], 1)))
    queries = packed[:, 0]
    keys_all = packed[:, 1]
    values = packed[:, 2]
    scores = jnp.einsum('qhd,khd->hqk', queries, keys_all, precision=lax.Precision.HIGHEST) * score_scale
    scores = low_back(scores)
    same_doc = doc_ids[:, None] == doc_ids[None, :]
    scores = jnp.where(same_doc[None], scores, MASK_FILL)
    row_max = lax.optimization_barrier(jnp.max(scores, -1, keepdims=True))
    raised = jnp.exp(scores - row_max)
    attn_probs = raised / lax.optimization_barrier(jnp.sum(raised, -1, keepdims=True))
    mixed = jnp.einsum('hqk,khd->qhd', low(attn_probs), values, precision=lax.Precision.HIGHEST)
    mixed = low(low_back(mixed.reshape(seq_len, model_dim)))
    attn_out = low_back(multiply(mixed, w_out))
    middle = stream + gate_a * attn_out
    normed_m = low(modulate(middle, gain_mlp, scale_m, shift_m))
    up_proj = low_back(multiply(normed_m, w_up))
    activated = low(jax.nn.gelu(up_proj))
    mlp_out = low_back(multiply(activated, w_down))
    return middle + gate_m * mlp_out

def reference(tokens, segments, timesteps, w_mod, b_mod, gain_attn, w_qkv, w_out, gain_mlp, w_up, w_down, cotangent):
    embedding = low(time_embed(timesteps, D))

    def forward(stream, wm, bm, g_attn, wq, wo, g_mlp, wu, wd):
        modulation = multiply(embedding, wm) + bm

        def one_row(element):
            row_stream, row_docs, row_mod = element
            return layer_row(row_stream, row_docs, row_mod, g_attn, wq, wo, g_mlp, wu, wd)
        return lax.map(jax.checkpoint(one_row), (stream, segments, modulation))
    output, pullback = jax.vjp(forward, tokens.astype(jnp.float32), w_mod.astype(jnp.float32), b_mod.astype(jnp.float32), gain_attn.astype(jnp.float32), w_qkv.astype(jnp.float32), w_out.astype(jnp.float32), gain_mlp.astype(jnp.float32), w_up.astype(jnp.float32), w_down.astype(jnp.float32))
    gradients = pullback(cotangent.astype(jnp.float32))
    return (output.astype(jnp.bfloat16), gradients[0].astype(jnp.bfloat16), gradients[1], gradients[2], gradients[3], gradients[4], gradients[5], gradients[6], gradients[7], gradients[8])
```

```python
import functools
import math

import jax
import jax.numpy as jnp
import numpy as np
from jax import lax
from jax.experimental import pallas as pl
from jax.experimental.pallas import tpu as pltpu
from jax.sharding import PartitionSpec as P

HEAD_DIM = 64
EPSILON = 1e-06
MASK_FILL = -1e30
MESH = pl.DeviceIdType.MESH
BF16 = jnp.bfloat16
F32 = jnp.float32
ANY = pl.BlockSpec(memory_space=pl.ANY)
VMEM = pl.BlockSpec(memory_space=pltpu.VMEM)
VMEM_LIMIT = 56 * 2**20


def place():
    return lax.axis_index("dp"), lax.axis_index("seq")


def xor(index, bits):
    return jnp.bitwise_xor(index, bits)


def remote(src, dst, send, recv, dp, seq):
    return pltpu.make_async_remote_copy(
        src_ref=src,
        dst_ref=dst,
        send_sem=send,
        recv_sem=recv,
        device_id=(dp, seq),
        device_id_type=MESH,
    )


def greet(n_dp, n_seq):
    d, s = place()
    barrier = pltpu.get_barrier_semaphore()
    for off in range(1, n_dp):
        pl.semaphore_signal(
            barrier, inc=1, device_id=(xor(d, off), s), device_id_type=MESH
        )
    for off in range(1, n_seq):
        pl.semaphore_signal(
            barrier, inc=1, device_id=(d, lax.rem(s + off, n_seq)), device_id_type=MESH
        )
    pl.semaphore_wait(barrier, n_dp - 1 + n_seq - 1)


def bit_orders(n_dp):
    high = [1 << b for b in range(1, n_dp.bit_length() - 1)]
    return (high + [1], high[::-1] + [1])


class WeightGather:
    def __init__(self, shard, full, own_sem, z_send, z_recv, x_send, x_recv, n_dp, n_seq):
        self.__dict__.update(locals())
        self.half = n_seq // 2
        self.orders = bit_orders(n_dp)
        self.groups = []
        for h in range(2):
            known = [(0, 0)]
            for step, bit in enumerate(self.orders[h]):
                known += [(off ^ bit, step + 1) for off, _ in known]
            self.groups.append(known)
        self.stages = len(self.orders[0]) + 1

    def own(self):
        d, s = place()
        return pltpu.make_async_copy(self.shard, self.full.at[d, s], self.own_sem)

    def z_copy(self, off):
        d, s = place()
        return remote(
            self.shard,
            self.full.at[d, s],
            self.z_send.at[off],
            self.z_recv.at[off],
            d,
            lax.rem(s + off, self.n_seq),
        )

    def z_wait(self, off):
        d, s = place()
        origin = lax.rem(s + self.n_seq - off, self.n_seq)
        remote(
            self.shard,
            self.full.at[d, origin],
            self.z_send.at[off],
            self.z_recv.at[off],
            d,
            origin,
        ).wait_recv()

    def x_copy(self, h, off, bit):
        d, s = place()
        part = self.full.at[xor(d, off), pl.ds(h * self.half, self.half)]
        return remote(
            part,
            part,
            self.x_send.at[h, off ^ bit],
            self.x_recv.at[h, off ^ bit],
            xor(d, bit),
            s,
        )

    def x_wait(self, h, off):
        d, s = place()
        part = self.full.at[xor(d, off), pl.ds(h * self.half, self.half)]
        remote(
            part, part, self.x_send.at[h, off], self.x_recv.at[h, off], d, s
        ).wait_recv()

    def start(self):
        self.own().start()
        for off in range(1, self.n_seq):
            self.z_copy(off).start()

    def stage(self, t):
        if t == 0:
            self.own().wait()
            for off in range(1, self.n_seq):
                self.z_wait(off)
        for h in range(2):
            for off, step in self.groups[h]:
                if step != t:
                    continue
                if t:
                    self.x_wait(h, off)
                for bit in self.orders[h][t:]:
                    self.x_copy(h, off, bit).start()

    def finish(self):
        for off in range(1, self.n_seq):
            self.z_copy(off).wait_send()
        for h in range(2):
            for off, step in self.groups[h]:
                for bit in self.orders[h][step:]:
                    self.x_copy(h, off, bit).wait_send()


def gather_kernel(n_dp, n_seq, rows, *refs):
    (tokens, cot, seg, part, *shards) = refs[:8]
    (tok_o, cot_o, seg_o, mod_o, *fulls) = refs[8:16]
    (
        zeros,
        zeros_seg,
        mod_in,
        mod_sum,
        mod_row,
        row_send,
        row_recv,
        mod_send,
        mod_recv,
        modz_send,
        modz_recv,
        own_sem,
        z_send,
        z_recv,
        x_send,
        x_recv,
    ) = refs[16:]
    d, s = place()
    first = lax.rem(d, 2)
    mine = s - first
    active = jnp.logical_and(mine >= 0, mine < rows)
    greet(n_dp, n_seq)

    def mod_copy(off):
        return remote(
            part.at[xor(d, off)],
            mod_in.at[d],
            mod_send.at[off],
            mod_recv.at[off],
            xor(d, off),
            s,
        )

    own_part = pltpu.make_async_copy(part.at[d], mod_in.at[d], mod_send.at[0])
    own_part.start()
    for off in range(1, n_dp):
        mod_copy(off).start()

    weights = [
        WeightGather(
            shards[w],
            fulls[w],
            own_sem.at[w],
            z_send.at[w],
            z_recv.at[w],
            x_send.at[w],
            x_recv.at[w],
            n_dp,
            n_seq,
        )
        for w in range(4)
    ]
    weights[0].start()

    trio = ((tokens, tok_o), (seg, seg_o), (cot, cot_o))

    def row_start(k):
        src, dst = trio[k]
        for i in range(rows):
            owner = first + i
            args = (src.at[i], dst.at[s], row_send.at[k, i])

            @pl.when(owner == s)
            def _():
                pltpu.make_async_copy(*args).start()

            @pl.when(owner != s)
            def _():
                remote(*args, row_recv.at[k, s], d, owner).start()

    def row_finish(k):
        src, dst = trio[k]
        for i in range(rows):
            owner = first + i
            args = (src.at[i], dst.at[s], row_send.at[k, i])

            @pl.when(owner == s)
            def _():
                pltpu.make_async_copy(*args).wait()

            @pl.when(owner != s)
            def _():
                remote(*args, row_recv.at[k, s], d, owner).wait_send()

        @pl.when(active)
        def _():
            for off in range(1, n_seq):
                origin = lax.rem(s + off, n_seq)
                remote(
                    src.at[0],
                    dst.at[origin],
                    row_send.at[k, 0],
                    row_recv.at[k, origin],
                    d,
                    origin,
                ).wait_recv()

        @pl.when(jnp.logical_not(active))
        def _():
            fill = zeros_seg if k == 1 else zeros
            copies = [
                pltpu.make_async_copy(fill, dst.at[z], row_recv.at[k, z])
                for z in range(n_seq)
            ]
            for c in copies:
                c.start()
            for c in copies:
                c.wait()

    zeros[...] = jnp.zeros_like(zeros)
    zeros_seg[...] = jnp.zeros_like(zeros_seg)
    row_start(0)
    row_start(1)
    for w in range(1, 4):
        weights[w].start()

    own_part.wait()
    for off in range(1, n_dp):
        remote(
            part.at[d],
            mod_in.at[xor(d, off)],
            mod_send.at[off],
            mod_recv.at[off],
            d,
            s,
        ).wait_recv()
    total = mod_in[0]
    for e in range(1, n_dp):
        total += mod_in[e]
    mod_sum[...] = total
    for i in range(rows):
        owner = first + i

        @pl.when(owner == s)
        def _():
            mod_row[s] = mod_sum[i]

        @pl.when(owner != s)
        def _():
            remote(
                mod_sum.at[i], mod_row.at[s], modz_send.at[i], modz_recv.at[s], d, owner
            ).start()

    row_start(2)
    stages = weights[0].stages
    for slot in range(stages + 3):
        for w in range(4):
            if 0 <= slot - w < stages:
                weights[w].stage(slot - w)

    @pl.when(active)
    def _():
        for off in range(1, n_seq):
            origin = lax.rem(s + off, n_seq)
            remote(
                mod_sum.at[0],
                mod_row.at[origin],
                modz_send.at[0],
                modz_recv.at[origin],
                d,
                origin,
            ).wait_recv()
        total = mod_row[0]
        for z in range(1, n_seq):
            total += mod_row[z]
        mod_o[...] = total

    @pl.when(jnp.logical_not(active))
    def _():
        mod_o[...] = jnp.zeros_like(mod_o)

    for i in range(rows):
        owner = first + i

        @pl.when(owner != s)
        def _():
            remote(
                mod_sum.at[i], mod_row.at[s], modz_send.at[i], modz_recv.at[s], d, owner
            ).wait_send()

    for off in range(1, n_dp):
        mod_copy(off).wait_send()
    for k in range(3):
        row_finish(k)
    for w in weights:
        w.finish()


def gather(n_dp, n_seq, tokens, cot, seg, part, shards):
    rows, length, width = tokens.shape
    dma = pltpu.SemaphoreType.DMA
    struct = jax.ShapeDtypeStruct
    outs = [
        struct((n_seq, length, width), BF16),
        struct((n_seq, length, width), BF16),
        struct((n_seq,) + seg.shape[1:], jnp.int32),
        struct((8, width), F32),
    ] + [struct((n_dp, n_seq) + w.shape, BF16) for w in shards]
    return pl.pallas_call(
        functools.partial(gather_kernel, n_dp, n_seq, rows),
        out_shape=outs,
        in_specs=[ANY] * 8,
        out_specs=[ANY, ANY, ANY, VMEM] + [ANY] * 4,
        scratch_shapes=[
            pltpu.VMEM((length, width), BF16),
            pltpu.VMEM(seg.shape[1:], jnp.int32),
            pltpu.VMEM((n_dp, rows, 8, width), F32),
            pltpu.VMEM((rows, 8, width), F32),
            pltpu.VMEM((n_seq, 8, width), F32),
            dma((3, rows)),
            dma((3, n_seq)),
            dma((n_dp,)),
            dma((n_dp,)),
            dma((rows,)),
            dma((n_seq,)),
            dma((4,)),
            dma((4, n_seq)),
            dma((4, n_seq)),
            dma((4, 2, n_dp)),
            dma((4, 2, n_dp)),
        ],
        compiler_params=pltpu.CompilerParams(
            collective_id=0, has_side_effects=True, vmem_limit_bytes=VMEM_LIMIT
        ),
    )(tokens, cot, seg, part, *shards)


class GradScatter:
    def __init__(self, grad, acc, core_in, step_in, z_in, out, sems, n_dp, n_seq):
        self.__dict__.update(locals())
        self.bits = n_dp.bit_length() - 1
        self.half = n_seq // 2
        self.high = list(range(self.bits - 1, 0, -1))
        self.orders = (list(range(len(self.high))), list(range(len(self.high)))[::-1])
        self.stages = len(self.high) + 2

    def my(self, dim):
        d, _ = place()
        return lax.rem(lax.div(d, 1 << self.high[dim]), 2)

    def index(self, h, done, flip=None):
        idx = []
        for dim in range(len(self.high)):
            if dim in done:
                idx.append(self.my(dim))
            elif dim == flip:
                idx.append(1 - self.my(dim))
            else:
                idx.append(slice(None))
        return tuple(idx) + (pl.ds(h * self.half, self.half),)

    def core_copies(self):
        d, s = place()
        core = lax.rem(d, 2)
        lead = (slice(None),) * len(self.high)
        send, recv, local = self.sems["core"]
        return (
            pltpu.make_async_copy(self.grad.at[lead + (core,)], self.acc, local),
            remote(
                self.grad.at[lead + (1 - core,)],
                self.core_in,
                send,
                recv,
                xor(d, 1),
                s,
            ),
        )

    def step_copy(self, h, step):
        d, s = place()
        done = self.orders[h][:step]
        dim = self.orders[h][step]
        send, recv = self.sems["step"]
        return remote(
            self.acc.at[self.index(h, done, dim)],
            self.step_in[h][step],
            send.at[h, step],
            recv.at[h, step],
            xor(d, 1 << self.high[dim]),
            s,
        )

    def z_copy(self, off):
        d, s = place()
        to = lax.rem(s + off, self.n_seq)
        send, recv = self.sems["z"]
        idx = tuple(self.my(dim) for dim in range(len(self.high)))
        return remote(
            self.acc.at[idx + (to,)],
            self.z_in.at[off],
            send.at[off],
            recv.at[off],
            d,
            to,
        )

    def start(self):
        for c in self.core_copies():
            c.start()

    def add(self, target, source, lead):
        count = math.prod(lead)

        @pl.loop(0, count)
        def _(k):
            idx = []
            for n in lead[::-1]:
                idx.append(lax.rem(k, n))
                k = lax.div(k, n)
            idx = tuple(idx[::-1])
            target[idx] = target[idx] + source[idx]

    def stage(self, t):
        if t == 0:
            for c in self.core_copies():
                c.wait()
            self.add(self.acc, self.core_in, self.acc.shape[:-2])
        for h in range(2):
            if t:
                if t > len(self.high):
                    continue
                done = self.orders[h][:t]
                self.step_copy(h, t - 1).wait()
                part = self.acc.at[self.index(h, done)]
                source = self.step_in[h][t - 1]
                self.add(part, source, source.shape[:-2])
            if t < len(self.high):
                self.step_copy(h, t).start()
        if t == len(self.high):
            for off in range(1, self.n_seq):
                self.z_copy(off).start()
        if t == len(self.high) + 1:
            _, s = place()
            idx = tuple(self.my(dim) for dim in range(len(self.high)))
            total = self.acc[idx + (s,)].astype(F32)
            for off in range(1, self.n_seq):
                self.z_copy(off).wait()
                total += self.z_in[off].astype(F32)
            self.out[...] = total


def scatter_kernel(n_dp, n_seq, rows, shapes, *refs):
    grads = refs[:4]
    out_row, dtok_row, gmod = refs[4:7]
    outs = refs[7:11]
    out_o, dtok_o, gmod_o = refs[11:14]
    refs = refs[14:]
    high = n_dp.bit_length() - 2
    weights = []
    for w in range(4):
        acc, core_in, z_in = refs[:3]
        steps = (refs[3 : 3 + high], refs[3 + high : 3 + 2 * high])
        refs = refs[3 + 2 * high :]
        weights.append((acc, core_in, steps, z_in))
    (
        row_send,
        row_recv,
        g_send,
        g_recv,
        gd_send,
        gd_recv,
        c_send,
        c_recv,
        c_local,
        s_send,
        s_recv,
        z_send,
        z_recv,
    ) = refs
    d, s = place()
    first = lax.rem(d, 2)
    mine = s - first
    active = jnp.logical_and(mine >= 0, mine < rows)
    greet(n_dp, n_seq)
    parts = [
        GradScatter(
            grads[w],
            weights[w][0],
            weights[w][1],
            weights[w][2],
            weights[w][3],
            outs[w],
            {
                "core": (c_send.at[w], c_recv.at[w], c_local.at[w]),
                "step": (s_send.at[w], s_recv.at[w]),
                "z": (z_send.at[w], z_recv.at[w]),
            },
            n_dp,
            n_seq,
        )
        for w in range(4)
    ]
    for p in parts:
        p.start()

    def group_copy(off):
        return remote(
            gmod,
            gmod_o.at[d, mine],
            g_send.at[off],
            g_recv.at[s],
            d,
            lax.rem(s + off, n_seq),
        )

    @pl.when(active)
    def _():
        pltpu.make_async_copy(gmod, gmod_o.at[d, mine], g_send.at[0]).start()
        for off in range(1, n_seq):
            group_copy(off).start()

    pair = ((out_row, out_o), (dtok_row, dtok_o))

    @pl.when(active)
    def _():
        for k in range(2):
            src, dst = pair[k]
            pltpu.make_async_copy(src.at[s], dst.at[mine], row_send.at[k, 0]).start()
            for off in range(1, n_seq):
                to = lax.rem(s + off, n_seq)
                remote(
                    src.at[to],
                    dst.at[mine],
                    row_send.at[k, off],
                    row_recv.at[k, mine],
                    d,
                    to,
                ).start()

    @pl.when(active)
    def _():
        pltpu.make_async_copy(gmod, gmod_o.at[d, mine], g_send.at[0]).wait()

    for i in range(rows):
        owner = first + i

        @pl.when(owner != s)
        def _():
            remote(
                gmod, gmod_o.at[d, i], g_send.at[0], g_recv.at[owner], d, owner
            ).wait_recv()

    def dp_copy(off):
        return remote(
            gmod_o.at[d], gmod_o.at[d], gd_send.at[off], gd_recv.at[off], xor(d, off), s
        )

    for off in range(1, n_dp):
        dp_copy(off).start()

    stages = parts[0].stages
    for slot in range(stages + 3):
        for w in range(4):
            if 0 <= slot - w < stages:
                parts[w].stage(slot - w)

    for off in range(1, n_dp):
        e = xor(d, off)
        dp_copy(off).wait_send()
        remote(
            gmod_o.at[e], gmod_o.at[e], gd_send.at[off], gd_recv.at[off], e, s
        ).wait_recv()

    @pl.when(active)
    def _():
        for off in range(1, n_seq):
            group_copy(off).wait_send()
        for k in range(2):
            src, dst = pair[k]
            pltpu.make_async_copy(src.at[s], dst.at[mine], row_send.at[k, 0]).wait()
            for off in range(1, n_seq):
                to = lax.rem(s + off, n_seq)
                remote(
                    src.at[to],
                    dst.at[mine],
                    row_send.at[k, off],
                    row_recv.at[k, mine],
                    d,
                    to,
                ).wait_send()

    for k in range(2):
        src, dst = pair[k]
        for i in range(rows):
            owner = first + i

            @pl.when(owner != s)
            def _():
                remote(
                    src.at[0],
                    dst.at[i],
                    row_send.at[k, 0],
                    row_recv.at[k, i],
                    d,
                    owner,
                ).wait_recv()


def scatter(n_dp, n_seq, rows, grads, out_row, dtok_row, gmod):
    dma = pltpu.SemaphoreType.DMA
    struct = jax.ShapeDtypeStruct
    high = n_dp.bit_length() - 2
    half = n_seq // 2
    scratch = []
    outs = []
    lead = (2,) * high
    views = []
    for g in grads:
        slab = g.shape[2:]
        views.append(g.reshape(lead + (2, n_seq) + slab))
        scratch += [
            pltpu.VMEM(lead + (n_seq,) + slab, BF16),
            pltpu.VMEM(lead + (n_seq,) + slab, BF16),
            pltpu.VMEM((n_seq,) + slab, BF16),
        ]
        for _ in range(2):
            for step in range(high):
                scratch.append(pltpu.VMEM((2,) * (high - 1 - step) + (half,) + slab, BF16))
        outs.append(struct(slab, F32))
    length, width = out_row.shape[1:]
    outs += [
        struct((rows, length, width), BF16),
        struct((rows, length, width), BF16),
        struct((n_dp, rows) + gmod.shape, F32),
    ]
    scratch += [
        dma((2, n_seq)),
        dma((2, rows)),
        dma((n_seq,)),
        dma((n_seq,)),
        dma((n_dp,)),
        dma((n_dp,)),
        dma((4,)),
        dma((4,)),
        dma((4,)),
        dma((4, 2, max(high, 1))),
        dma((4, 2, max(high, 1))),
        dma((4, n_seq)),
        dma((4, n_seq)),
    ]
    return pl.pallas_call(
        functools.partial(scatter_kernel, n_dp, n_seq, rows, None),
        out_shape=outs,
        in_specs=[ANY] * 7,
        out_specs=[VMEM] * 4 + [ANY] * 3,
        scratch_shapes=scratch,
        compiler_params=pltpu.CompilerParams(
            collective_id=1, has_side_effects=True, vmem_limit_bytes=VMEM_LIMIT
        ),
    )(*views, out_row, dtok_row, gmod)


def dot(a, b, dims):
    return lax.dot_general(a, b, (dims, ((), ())), preferred_element_type=F32)


def rotary_tables(seq_len):
    half = HEAD_DIM // 2
    freq = np.exp(np.float32(-math.log(10000.0)) * np.arange(half, dtype=np.float32) / np.float32(half))
    angles = np.arange(seq_len, dtype=np.float32)[:, None] * freq.astype(np.float32)[None, :]
    cos = np.tile(np.cos(angles), (1, 4)).astype(np.float32)
    sin = np.sin(angles)
    sin = np.concatenate([-sin, sin, -sin, sin], 1).astype(np.float32)
    return jnp.asarray(cos), jnp.asarray(sin)


def swap_halves(x):
    quarter = HEAD_DIM // 2
    lane = lax.broadcasted_iota(jnp.int32, x.shape, 1)
    return jnp.where(
        lax.rem(lane, HEAD_DIM) < quarter,
        pltpu.roll(x, 128 - quarter, axis=1),
        pltpu.roll(x, quarter, axis=1),
    )


def qkv_kernel(tok, mod, w, cos, sin, normed_o, packed_o):
    x = tok[...].astype(F32)
    mean = jnp.mean(x, -1, keepdims=True)
    centred = x - mean
    var = jnp.mean(centred * centred, -1, keepdims=True)
    z = centred * lax.rsqrt(var + EPSILON)
    gain = mod[6:7, :] * (1.0 + mod[1:2, :])
    normed = (z * gain + mod[0:1, :]).astype(BF16)
    normed_o[...] = normed
    width = x.shape[1]
    for c in range(3 * width // 256):
        y = dot(normed, w[:, c * 256 : (c + 1) * 256], ((1,), (0,)))
        for j in range(2):
            col = c * 256 + j * 128
            p = y[:, j * 128 : (j + 1) * 128]
            if col < 2 * width:
                p = p * cos[...] + swap_halves(p) * sin[...]
            if col < width:
                p = p * (1.0 / math.sqrt(HEAD_DIM))
            packed_o[:, col : col + 128] = p.astype(BF16)


def qkv_call(tok, mod, w, cos, sin):
    seq_len, width = tok.shape
    block = 256
    return pl.pallas_call(
        qkv_kernel,
        grid=(seq_len // block,),
        in_specs=[
            pl.BlockSpec((block, width), lambda i: (i, 0)),
            pl.BlockSpec((8, width), lambda i: (0, 0)),
            pl.BlockSpec((width, 3 * width), lambda i: (0, 0)),
            pl.BlockSpec((block, 128), lambda i: (i, 0)),
            pl.BlockSpec((block, 128), lambda i: (i, 0)),
        ],
        out_specs=[
            pl.BlockSpec((block, width), lambda i: (i, 0)),
            pl.BlockSpec((block, 3 * width), lambda i: (i, 0)),
        ],
        out_shape=[
            jax.ShapeDtypeStruct((seq_len, width), BF16),
            jax.ShapeDtypeStruct((seq_len, 3 * width), BF16),
        ],
        compiler_params=pltpu.CompilerParams(vmem_limit_bytes=VMEM_LIMIT),
    )(tok, mod, w, cos, sin)


def head_mask(x, j):
    lane = lax.broadcasted_iota(jnp.int32, x.shape, 1)
    return jnp.where(lax.div(lane, HEAD_DIM) == j, x, jnp.zeros_like(x))


def attend_kernel(q, k, v, seg_col, seg_row, out, lse_o):
    seq_len = q.shape[0]
    block = 256
    keys = k[...]
    values = v[...]
    for i in range(seq_len // block):
        rows = pl.ds(i * block, block)
        bias = jnp.where(seg_col[rows, 0:1] == seg_row[0:1, :], 0.0, MASK_FILL)
        qb = q[rows, :]
        both = []
        stats = []
        for j in range(2):
            sc = dot(head_mask(qb, j), keys, ((1,), (1,))) + bias
            top = jnp.max(sc, -1, keepdims=True)
            e = jnp.exp(sc - top)
            total = jnp.sum(e, -1, keepdims=True)
            o = dot(e.astype(BF16), values, ((1,), (0,)))
            both.append(o / total)
            stats.append(top + jnp.log(total))
        lane = lax.broadcasted_iota(jnp.int32, both[0].shape, 1)
        out[rows, :] = jnp.where(lane < HEAD_DIM, both[0], both[1]).astype(BF16)
        lse_o[rows, :] = jnp.where(lane < HEAD_DIM, stats[0], stats[1])


def attend_call(packed, seg_col, seg_row):
    seq_len, width3 = packed.shape
    width = width3 // 3
    pairs = width // 128
    return pl.pallas_call(
        attend_kernel,
        grid=(pairs,),
        in_specs=[
            pl.BlockSpec((seq_len, 128), lambda i: (0, i)),
            pl.BlockSpec((seq_len, 128), lambda i: (0, i + pairs)),
            pl.BlockSpec((seq_len, 128), lambda i: (0, i + 2 * pairs)),
            pl.BlockSpec((seq_len, 128), lambda i: (0, 0)),
            pl.BlockSpec((8, seq_len), lambda i: (0, 0)),
        ],
        out_specs=[
            pl.BlockSpec((seq_len, 128), lambda i: (0, i)),
            pl.BlockSpec((seq_len, 128), lambda i: (0, i)),
        ],
        out_shape=[
            jax.ShapeDtypeStruct((seq_len, width), BF16),
            jax.ShapeDtypeStruct((seq_len, width), F32),
        ],
        compiler_params=pltpu.CompilerParams(vmem_limit_bytes=VMEM_LIMIT),
    )(packed, packed, packed, seg_col, seg_row)


def attend_back_kernel(
    q, k, v, o, do, lse, seg_col, seg_row, cos, sin, dq_o, dk_o, dv_o, dq_acc
):
    seq_len = q.shape[0]
    block = 256
    grads = do[...]
    inner = jnp.transpose(grads.astype(F32) * o[...].astype(F32))
    lse_t = jnp.transpose(lse[...])
    queries = q[...]
    scale = 1.0 / math.sqrt(HEAD_DIM)
    inners, lses, qs, gs = [], [], [], []
    for j in range(2):
        inners.append(
            jnp.sum(inner[j * HEAD_DIM : (j + 1) * HEAD_DIM], 0, keepdims=True)
        )
        lses.append(lse_t[j * HEAD_DIM : j * HEAD_DIM + 1])
        qs.append(head_mask(queries, j))
        gs.append(head_mask(grads, j))
    for i in range(seq_len // block):
        rows = pl.ds(i * block, block)
        bias = jnp.where(seg_col[rows, 0:1] == seg_row[0:1, :], 0.0, MASK_FILL)
        kb = k[rows, :]
        vb = v[rows, :]
        dk = None
        for j in range(2):
            sc = dot(kb, qs[j], ((1,), (1,))) + bias
            p = jnp.exp(sc - lses[j])
            dp = dot(vb, gs[j], ((1,), (1,)))
            ds = (p * (dp - inners[j])).astype(BF16)
            dv_j = dot(p.astype(BF16), gs[j], ((1,), (0,)))
            dk_j = dot(ds, qs[j], ((1,), (0,)))
            dq_j = dot(ds, head_mask(kb, j), ((0,), (0,)))
            if j == 0:
                dv, dk, dq = dv_j, dk_j, dq_j
            else:
                dv, dk, dq = dv + dv_j, dk + dk_j, dq + dq_j
        if i == 0:
            dq_acc[...] = dq
        else:
            dq_acc[...] += dq
        dv_o[rows, :] = dv.astype(BF16)
        dk_o[rows, :] = (dk * cos[rows, :] + swap_halves(dk * sin[rows, :]) * 1.0).astype(BF16)
    dq = dq_acc[...] * scale
    dq_o[...] = (dq * cos[...] + swap_halves(dq * sin[...])).astype(BF16)


def attend_back_call(packed, mixed, grad_mixed, lse, seg_col, seg_row, cos, sin):
    seq_len, width3 = packed.shape
    width = width3 // 3
    pairs = width // 128
    pair = pl.BlockSpec((seq_len, 128), lambda i: (0, i))
    whole = pl.BlockSpec((seq_len, 128), lambda i: (0, 0))
    return pl.pallas_call(
        attend_back_kernel,
        grid=(pairs,),
        in_specs=[
            pair,
            pl.BlockSpec((seq_len, 128), lambda i: (0, i + pairs)),
            pl.BlockSpec((seq_len, 128), lambda i: (0, i + 2 * pairs)),
            pair,
            pair,
            pair,
            whole,
            pl.BlockSpec((8, seq_len), lambda i: (0, 0)),
            whole,
            whole,
        ],
        out_specs=[pair] * 3,
        out_shape=[jax.ShapeDtypeStruct((seq_len, width), BF16)] * 3,
        scratch_shapes=[pltpu.VMEM((seq_len, 128), F32)],
        compiler_params=pltpu.CompilerParams(vmem_limit_bytes=VMEM_LIMIT),
    )(packed, packed, packed, mixed, grad_mixed, lse, seg_col, seg_row, cos, sin)


def time_embed(step_ids, model_dim):
    half_dim = model_dim // 2
    frequency = jnp.exp(-math.log(10000.0) * jnp.arange(half_dim, dtype=jnp.float32) / half_dim)
    angles = step_ids.astype(jnp.float32)[:, None] * frequency[None, :]
    return jnp.concatenate([jnp.cos(angles), jnp.sin(angles)], axis=-1)


def modulate(inputs, norm_gain, mod_scale, mod_shift):
    average = jnp.mean(inputs, -1, keepdims=True)
    centred = inputs - average
    variance = jnp.mean(centred * centred, -1, keepdims=True)
    return centred * lax.rsqrt(variance + EPSILON) * norm_gain * (1.0 + mod_scale) + mod_shift


def matmul(a, b, spec):
    return jnp.einsum(spec, a, b, preferred_element_type=F32)


def placed_at(vector, index, length):
    whole = jnp.zeros((length,), F32)
    return lax.dynamic_update_slice(whole, vector.astype(F32), (index * vector.shape[0],))


def shards(
    n_dp,
    n_seq,
    tokens,
    segments,
    timesteps,
    w_mod,
    b_mod,
    gain_attn,
    w_qkv,
    w_out,
    gain_mlp,
    w_up,
    w_down,
    cotangent,
):
    rows, length, width = tokens.shape
    seq_len = length * n_seq
    hidden = w_up.shape[1]
    d, s = place()
    me = d * n_seq + s
    depth = w_mod.shape[0]
    cos, sin = rotary_tables(seq_len)

    steps = lax.all_gather(timesteps, "dp", axis=0, tiled=True)
    embedding = lax.dynamic_slice_in_dim(
        time_embed(steps, width).astype(BF16), me * depth, depth, 1
    )
    part = matmul(embedding, w_mod, "rk,kn->rn") + placed_at(b_mod, me, 6 * width)
    gains = jnp.concatenate(
        [placed_at(gain_attn, me, width), placed_at(gain_mlp, me, width)]
    )
    part = jnp.concatenate([part, jnp.broadcast_to(gains, (part.shape[0], 2 * width))], 1)
    part = part.reshape(n_dp, rows, 8, width)
    seg = jnp.broadcast_to(segments[:, None, :], (rows, 8, length))

    tok, cot, seg, mod, wq, wo, wu, wd = gather(
        n_dp, n_seq, tokens, cotangent, seg, part, (w_qkv, w_out, w_up, w_down)
    )
    tok = tok.reshape(seq_len, width)
    cot = cot.reshape(seq_len, width).astype(F32)
    seg_row = seg.transpose(1, 0, 2).reshape(8, seq_len)
    seg_col = jnp.broadcast_to(seg_row[0][:, None], (seq_len, 128))
    wq = wq.reshape(width, 3 * width)
    wo = wo.reshape(width, width)
    wu = wu.reshape(width, hidden)
    wd = wd.reshape(hidden, width)
    shift_a, scale_a, gate_a, shift_m, scale_m, gate_m, gain_a, gain_m = (
        mod[j : j + 1] for j in range(8)
    )

    normed_a, packed = qkv_call(tok, mod, wq, cos, sin)
    mixed, lse = attend_call(packed, seg_col, seg_row)

    stream = tok.astype(F32)
    attn_out = matmul(mixed, wo, "td,de->te")
    middle = stream + gate_a * attn_out
    normed_m, norm_back_m = jax.vjp(modulate, middle, gain_m, scale_m, shift_m)
    normed_m = normed_m.astype(BF16)
    up_proj = matmul(normed_m, wu, "td,df->tf")
    activated, gelu_back = jax.vjp(jax.nn.gelu, up_proj)
    activated = activated.astype(BF16)
    mlp_out = matmul(activated, wd, "tf,fd->td")
    output = (middle + gate_m * mlp_out).astype(BF16)

    grad_mlp = (cot * gate_m).astype(BF16)
    grad_gate_m = jnp.sum(cot * mlp_out, 0, keepdims=True)
    grad_down = matmul(activated, grad_mlp, "tf,td->fd").astype(BF16)
    grad_act = matmul(grad_mlp, wd, "td,fd->tf")
    grad_up = gelu_back(grad_act)[0].astype(BF16)
    grad_wup = matmul(normed_m, grad_up, "td,tf->df").astype(BF16)
    grad_hm = matmul(grad_up, wu, "tf,df->td")
    grad_mid_norm, grad_gain_m, grad_scale_m, grad_shift_m = norm_back_m(grad_hm)
    grad_mid = cot + grad_mid_norm
    grad_gate_a = jnp.sum(grad_mid * attn_out, 0, keepdims=True)
    grad_attn = (grad_mid * gate_a).astype(BF16)
    grad_wout = matmul(mixed, grad_attn, "td,te->de").astype(BF16)
    grad_mixed = matmul(grad_attn, wo, "te,de->td").astype(BF16)

    dq, dk, dv = attend_back_call(
        packed, mixed, grad_mixed, lse, seg_col, seg_row, cos, sin
    )
    grad_qkv = jnp.concatenate([dq, dk, dv], 1)
    grad_wqkv = matmul(normed_a, grad_qkv, "td,te->de").astype(BF16)
    grad_ha = matmul(grad_qkv, wq, "te,de->td")
    _, norm_back_a = jax.vjp(modulate, stream, gain_a, scale_a, shift_a)
    grad_in_norm, grad_gain_a, grad_scale_a, grad_shift_a = norm_back_a(grad_ha)
    grad_input = (grad_mid + grad_in_norm).astype(BF16)
    gmod = jnp.concatenate(
        [
            grad_shift_a,
            grad_scale_a,
            grad_gate_a,
            grad_shift_m,
            grad_scale_m,
            grad_gate_m,
            grad_gain_a,
            grad_gain_m,
        ],
        0,
    )

    def cut(g, shard):
        return g.reshape((n_dp, n_seq) + shard.shape)

    g_wqkv, g_wout, g_wup, g_wdown, out, d_tok, gmods = scatter(
        n_dp,
        n_seq,
        rows,
        (
            cut(grad_wqkv, w_qkv),
            cut(grad_wout, w_out),
            cut(grad_wup, w_up),
            cut(grad_down, w_down),
        ),
        output.reshape(n_seq, length, width),
        grad_input.reshape(n_seq, length, width),
        gmod,
    )
    gmods = gmods.reshape(n_dp * rows, 8 * width)
    g_w_mod = jnp.dot(
        embedding.astype(F32).T,
        gmods[:, : 6 * width],
        precision=lax.Precision.HIGHEST,
        preferred_element_type=F32,
    )
    summed = jnp.sum(gmods, 0)

    def own_part(vector, n):
        return lax.dynamic_slice_in_dim(vector, me * n, n, 0)

    return (
        out,
        d_tok,
        g_w_mod,
        own_part(summed[: 6 * width], b_mod.shape[0]),
        own_part(summed[6 * width : 7 * width], gain_attn.shape[0]),
        g_wqkv,
        g_wout,
        own_part(summed[7 * width :], gain_mlp.shape[0]),
        g_wup,
        g_wdown,
    )


def solution(mesh):
    both = P(("dp", "seq"))
    wide = P(("dp", "seq"), None)
    tokens = P("dp", "seq", None)
    return jax.shard_map(
        functools.partial(shards, mesh.shape["dp"], mesh.shape["seq"]),
        mesh=mesh,
        in_specs=(
            tokens,
            P("dp", "seq"),
            P("dp"),
            wide,
            both,
            both,
            wide,
            wide,
            both,
            wide,
            wide,
            tokens,
        ),
        out_specs=(tokens, tokens, wide, both, both, wide, wide, both, wide, wide),
        check_vma=False,
    )
```

```python
import functools
import math

import jax
import jax.numpy as jnp
import numpy as np
from jax import lax
from jax.experimental import pallas as pl
from jax.experimental.pallas import tpu as pltpu
from jax.sharding import PartitionSpec as P

HEAD_DIM = 64
EPSILON = 1e-06
MASK_FILL = -1e30
MESH = pl.DeviceIdType.MESH
BF16 = jnp.bfloat16
F32 = jnp.float32
ANY = pl.BlockSpec(memory_space=pl.ANY)
VMEM = pl.BlockSpec(memory_space=pltpu.VMEM)
VMEM_LIMIT = 60 * 2**20
LOG2E = math.log2(math.e)


def place():
    return lax.axis_index("dp"), lax.axis_index("seq")


def xor(index, bits):
    return jnp.bitwise_xor(index, bits)


def remote(src, dst, send, recv, dp, seq):
    return pltpu.make_async_remote_copy(
        src_ref=src,
        dst_ref=dst,
        send_sem=send,
        recv_sem=recv,
        device_id=(dp, seq),
        device_id_type=MESH,
    )


def greet(n_dp, n_seq):
    d, s = place()
    barrier = pltpu.get_barrier_semaphore()
    for off in range(1, n_dp):
        pl.semaphore_signal(
            barrier, inc=1, device_id=(xor(d, off), s), device_id_type=MESH
        )
    for off in range(1, n_seq):
        pl.semaphore_signal(
            barrier, inc=1, device_id=(d, lax.rem(s + off, n_seq)), device_id_type=MESH
        )
    pl.semaphore_wait(barrier, n_dp - 1 + n_seq - 1)


def bit_orders(n_dp):
    high = [1 << b for b in range(1, n_dp.bit_length() - 1)]
    return (high + [1], high[::-1] + [1])


def signed(value, sign):
    return value if sign > 0 else -value


class WeightGather:
    def __init__(self, shard, full, own_sem, z_send, z_recv, x_send, x_recv, n_dp, n_seq):
        self.shard, self.full, self.own_sem = shard, full, own_sem
        self.z_send, self.z_recv = z_send, z_recv
        self.x_send, self.x_recv = x_send, x_recv
        self.n_seq = n_seq
        self.cols = shard.shape[1] // 2
        self.orders = bit_orders(n_dp)
        self.steps = len(self.orders[0])
        self.groups = []
        for h in range(2):
            known = [(0, 0)]
            for step, bit in enumerate(self.orders[h]):
                known += [(off ^ bit, step + 1) for off, _ in known]
            self.groups.append(known)

    def own(self):
        d, s = place()
        return pltpu.make_async_copy(self.shard, self.full.at[d, s], self.own_sem)

    def z_copy(self, way, k):
        d, s = place()
        origin = s - signed(k - 1, way)
        side = 0 if way > 0 else 1
        src = self.shard if k == 1 else self.full.at[d, origin]
        return remote(
            src,
            self.full.at[d, origin],
            self.z_send.at[side, k],
            self.z_recv.at[side, k],
            d,
            s + way,
        )

    def direct_copy(self, way, k):
        d, s = place()
        side = 0 if way > 0 else 1
        return remote(
            self.shard,
            self.full.at[d, s],
            self.z_send.at[side, k],
            self.z_recv.at[side, k],
            d,
            s + signed(k, way),
        )

    def direct_each(self, body):
        d, s = place()
        for k in range(1, self.n_seq):
            for way in (1, -1):
                to = s + signed(k, way)

                @pl.when((to >= 0) & (to < self.n_seq))
                def _():
                    body(self.direct_copy(way, k))

    def z_valid(self, way, k):
        d, s = place()
        origin = s - signed(k - 1, way)
        to = s + way
        return (origin >= 0) & (origin < self.n_seq) & (to >= 0) & (to < self.n_seq)

    def x_copy(self, origin, h, off, bit, own=False):
        d, s = place()
        cols = pl.ds(h * self.cols, self.cols)
        dst = self.full.at[xor(d, off), origin, :, cols]
        src = self.shard.at[:, cols] if own else dst
        return remote(
            src,
            dst,
            self.x_send.at[origin, h, off ^ bit],
            self.x_recv.at[origin, h, off ^ bit],
            xor(d, bit),
            s,
        )

    def each(self, k, body):
        d, s = place()
        if k == 0:
            body(s, 0)
            return
        for way in (1, -1):
            origin = s - signed(k, way)

            @pl.when((origin >= 0) & (origin < self.n_seq))
            def _():
                body(origin, way)

    def z_start(self, k):
        for way in (1, -1):

            @pl.when(self.z_valid(way, k))
            def _():
                self.z_copy(way, k).start()

    def own_start(self):
        self.own().start()
        d, s = place()
        for h in range(2):
            for bit in self.orders[h]:
                self.x_copy(s, h, 0, bit, True).start()

    def event(self, k, t, forward=True):
        if t == 0:
            d, s = place()

            def arrival(origin, way):
                side = 0 if way > 0 else 1
                remote(
                    self.shard,
                    self.full.at[d, origin],
                    self.z_send.at[side, k],
                    self.z_recv.at[side, k],
                    d,
                    s,
                ).wait_recv()
                for h in range(2):
                    for bit in self.orders[h]:
                        self.x_copy(origin, h, 0, bit).start()

            self.each(k, arrival)
            if forward and k + 1 < self.n_seq:
                self.z_start(k + 1)
            return

        def passing(origin, way):
            for h in range(2):
                for off, step in self.groups[h]:
                    if step != t:
                        continue
                    self.x_copy(origin, h, off, 0).wait_recv()
                    for bit in self.orders[h][t:]:
                        self.x_copy(origin, h, off, bit).start()

        self.each(k, passing)

    def finish(self, direct=False):
        if direct:
            self.direct_each(lambda copy: copy.wait_send())
        for k in range(1, self.n_seq if not direct else 1):
            for way in (1, -1):

                @pl.when(self.z_valid(way, k))
                def _():
                    self.z_copy(way, k).wait_send()

        for k in range(self.n_seq):

            def sent(origin, way):
                for h in range(2):
                    for off, step in self.groups[h]:
                        for bit in self.orders[h][step:]:
                            self.x_copy(origin, h, off, bit).wait_send()

            self.each(k, sent)


def dot(a, b, dims):
    return lax.dot_general(a, b, (dims, ((), ())), preferred_element_type=F32)


def swap_halves(x):
    quarter = HEAD_DIM // 2
    lane = lax.broadcasted_iota(jnp.int32, x.shape, 1)
    return jnp.where(
        lax.rem(lane, HEAD_DIM) < quarter,
        pltpu.roll(x, 128 - quarter, axis=1),
        pltpu.roll(x, quarter, axis=1),
    )


def normalise(x):
    mean = jnp.mean(x, -1, keepdims=True)
    centred = x - mean
    var = jnp.mean(centred * centred, -1, keepdims=True)
    rstd = lax.rsqrt(var + EPSILON)
    return centred * rstd, rstd


def join_slabs(slabs, whole):
    depth = slabs.shape[-2]
    count = math.prod(slabs.shape[:-2])
    group = 16 // math.gcd(16, depth)

    @pl.loop(0, count // group)
    def _(i):
        parts = []
        for j in range(group):
            k, idx = i * group + j, []
            for n in slabs.shape[:-2][::-1]:
                idx.append(lax.rem(k, n))
                k = lax.div(k, n)
            parts.append(slabs[tuple(idx[::-1])])
        rows = group * depth
        whole[pl.ds(pl.multiple_of(i * rows, rows), rows), :] = jnp.concatenate(parts, 0)


def lanes_of(j, shape):
    lane = lax.broadcasted_iota(jnp.int32, shape, 1)
    return lax.div(lane, HEAD_DIM) == j


def front_kernel(n_dp, n_seq, rows, *refs):
    tokens, cot, seg, part, *shards = refs[:6]
    cos, sin = refs[6:8]
    tok_o, cot_o, doc_o, norm_o, pack_o, *fulls = refs[8:15]
    mod_o, mixed_o, lse_o = refs[15:18]
    (
        tok,
        segs,
        docs,
        normed,
        packed,
        w_in,
        w,
        values,
        keys,
        mod_in,
        mod_sum,
        mod_row,
        out_sem,
        row_send,
        row_recv,
        mod_send,
        mod_recv,
        modz_send,
        modz_recv,
        own_sem,
        z_send,
        z_recv,
        x_send,
        x_recv,
    ) = refs[18:]
    d, s = place()
    length, width = tokens.shape[1:]
    seq_len = length * n_seq
    first = lax.rem(d, 2)
    mine = s - first
    active = (mine >= 0) & (mine < rows)
    greet(n_dp, n_seq)

    def mod_copy(off):
        return remote(
            part.at[xor(d, off)],
            mod_in.at[d],
            mod_send.at[off],
            mod_recv.at[off],
            xor(d, off),
            s,
        )

    own_part = pltpu.make_async_copy(part.at[d], mod_in.at[d], mod_send.at[0])
    own_part.start()
    for off in range(1, n_dp):
        mod_copy(off).start()

    qkv, rest = [
        WeightGather(
            shards[i],
            fulls[i],
            own_sem.at[i],
            z_send.at[i],
            z_recv.at[i],
            x_send.at[i],
            x_recv.at[i],
            n_dp,
            n_seq,
        )
        for i in range(2)
    ]
    qkv.direct_each(lambda copy: copy.start())
    rest.z_start(1)
    qkv.own_start()

    trio = ((tokens, tok), (seg, segs), (cot, cot_o))

    def row_local(k, i):
        src, dst = trio[k]
        return pltpu.make_async_copy(src.at[i], dst.at[s], row_send.at[k, i])

    def row_remote(k, i):
        src, dst = trio[k]
        return remote(
            src.at[i], dst.at[s], row_send.at[k, i], row_recv.at[k, s], d, first + i
        )

    def row_start(k):
        for i in range(rows):

            @pl.when(first + i == s)
            def _():
                row_local(k, i).start()

            @pl.when(first + i != s)
            def _():
                row_remote(k, i).start()

    def row_sent(k):
        for i in range(rows):

            @pl.when(first + i != s)
            def _():
                row_remote(k, i).wait_send()

    def row_arrival(k, origin):
        src, dst = trio[k]
        remote(
            src.at[0],
            dst.at[origin],
            row_send.at[k, 0],
            row_recv.at[k, origin],
            d,
            origin,
        ).wait_recv()

    def row_own(k):
        for i in range(rows):

            @pl.when(first + i == s)
            def _():
                row_local(k, i).wait()

    def mod_exchange():
        own_part.wait()
        for off in range(1, n_dp):
            remote(
                part.at[d],
                mod_in.at[xor(d, off)],
                mod_send.at[off],
                mod_recv.at[off],
                d,
                s,
            ).wait_recv()
        total = mod_in[0]
        for e in range(1, n_dp):
            total += mod_in[e]
        mod_sum[...] = total
        for i in range(rows):

            @pl.when(first + i == s)
            def _():
                mod_row[s] = mod_sum[i]

            @pl.when(first + i != s)
            def _():
                remote(
                    mod_sum.at[i],
                    mod_row.at[s],
                    modz_send.at[i],
                    modz_recv.at[s],
                    d,
                    first + i,
                ).start()

    @pl.when(jnp.logical_not(active))
    def _():
        tok[...] = jnp.zeros_like(tok)
        segs[...] = jnp.zeros_like(segs)

    row_start(1)
    mod_exchange()
    row_start(0)
    for k in range(1, n_seq):
        qkv.event(k, 0, forward=False)
    for k in range(n_seq):
        qkv.event(k, 1)
    rest.own_start()
    rest.event(1, 0)
    for t in range(2, qkv.steps + 1):
        for k in range(n_seq):
            qkv.event(k, t)
    stage = pltpu.make_async_copy(fulls[0], w_in, out_sem.at[0])
    qkv.own().wait()
    stage.start()

    @pl.when(active)
    def _():
        for off in range(1, n_seq):
            row_arrival(1, lax.rem(s + off, n_seq))

    row_own(1)
    lane = lax.broadcasted_iota(jnp.int32, (length, 128), 1)
    lane = lax.rem(lane, HEAD_DIM).astype(F32)
    for z in range(n_seq):
        ids = jnp.transpose(
            jnp.broadcast_to(segs[z, 0:1, :].astype(F32), (128, length))
        )
        same = ids == lane
        at = pl.ds(z * length, length)
        docs[0, at, :] = jnp.where(
            same | ((lane >= 8.0) & (lane < 11.0)), 1.0, 0.0
        ).astype(BF16)
        docs[1, at, :] = jnp.where(same | (lane >= 8.0), 0.0, MASK_FILL).astype(BF16)
    doc_copy = pltpu.make_async_copy(docs, doc_o, out_sem.at[1])
    doc_copy.start()

    stage.wait()
    depth = w_in.shape[2]

    join_slabs(w_in, w)

    @pl.when(active)
    def _():
        for off in range(1, n_seq):
            origin = lax.rem(s + off, n_seq)
            remote(
                mod_sum.at[0],
                mod_row.at[origin],
                modz_send.at[0],
                modz_recv.at[origin],
                d,
                origin,
            ).wait_recv()
        total = mod_row[0]
        for z in range(1, n_seq):
            total += mod_row[z]
        mod_o[...] = total

    @pl.when(jnp.logical_not(active))
    def _():
        mod_o[...] = jnp.zeros_like(mod_o)

    rest.event(0, 1)

    gain = mod_o[6:7, :] * (1.0 + mod_o[1:2, :])
    shift = mod_o[0:1, :]
    row_own(0)
    for off in range(n_seq):
        z = lax.rem(s + off, n_seq)
        if off:

            @pl.when(active)
            def _():
                row_arrival(0, z)

        normal, _ = normalise(tok[z].astype(F32))
        at = pl.ds(pl.multiple_of(z * length, length), length)
        normed[at, :] = (normal * gain + shift).astype(BF16)
    outs = [
        pltpu.make_async_copy(tok, tok_o, out_sem.at[2]),
        pltpu.make_async_copy(normed, norm_o, out_sem.at[3]),
    ]
    for c in outs:
        c.start()

    for kind in range(3):

        @pl.loop(0, width // 256)
        def _(c):
            col = kind * width + c * 256
            wc = w[:, pl.ds(pl.multiple_of(col, 256), 256)]
            for r in range(seq_len // 256):
                at = pl.ds(r * 256, 256)
                y = dot(normed[at, :], wc, ((1,), (0,)))
                for j in range(2):
                    p = y[:, j * 128 : (j + 1) * 128]
                    if kind < 2:
                        p = p * cos[at, :] + swap_halves(p) * sin[at, :]
                    if kind == 0:
                        p = p * (LOG2E / math.sqrt(HEAD_DIM))
                    packed[kind * (width // 128) + c * 2 + j, at, :] = p.astype(BF16)

    pack_copy = pltpu.make_async_copy(packed, pack_o, out_sem.at[4])
    pack_copy.start()
    early = [(0, 2), (1, 1), (0, 3), (2, 0)]
    for e in early:
        rest.event(*e)
    row_start(2)
    pairs = width // 128
    slots = {
        1: [(1, 2)],
        2: [(3, 0), (2, 1), (1, 3)],
        4: [(2, 2)],
        5: [(3, 1)],
    }
    done = {e for v in slots.values() for e in v}
    done |= set(early) | {(1, 0), (0, 1)}

    values[:, 128:] = jnp.ones((seq_len, 128), BF16)
    block = 128
    lse_o[...] = jnp.zeros_like(lse_o)

    @pl.loop(0, pairs)
    def _(p):
        k = packed[pairs + p]
        values[:, :128] = packed[2 * pairs + p]
        for j in range(2):
            keys[j] = jnp.where(lanes_of(j, k.shape), k, docs[0])
        for i in range(seq_len // block):
            at = pl.ds(i * block, block)
            q = packed[p, at, :]
            both = []
            stats = lse_o[at, :]
            lane = lax.broadcasted_iota(jnp.int32, (block, 128), 1)
            for j in range(2):
                own = lanes_of(j, q.shape)
                scores = dot(jnp.where(own, q, docs[1, at, :]), keys[j], ((1,), (1,)))
                top = jnp.max(scores, -1, keepdims=True)
                e = jnp.exp2(scores - top).astype(BF16)
                o = dot(e, values[...], ((1,), (0,)))
                total = o[:, 128:]
                both.append(o[:, :128] / total)
                stats = jnp.where(lane == 2 * p + j, top + jnp.log2(total), stats)
            lse_o[at, :] = stats
            mixed_o[at, pl.ds(pl.multiple_of(p * 128, 128), 128)] = jnp.where(
                lane < HEAD_DIM, both[0], both[1]
            ).astype(BF16)
        for slot, events in slots.items():

            @pl.when(p == slot)
            def _():
                for k, t in events:
                    rest.event(k, t)

    for t in range(1, rest.steps + 1):
        for k in range(n_seq):
            if (k, t) not in done:
                rest.event(k, t)

    for i in range(rows):

        @pl.when(first + i != s)
        def _():
            remote(
                mod_sum.at[i], mod_row.at[s], modz_send.at[i], modz_recv.at[s], d, first + i
            ).wait_send()

    for off in range(1, n_dp):
        mod_copy(off).wait_send()
    rest.own().wait()
    for c in outs + [doc_copy, pack_copy]:
        c.wait()

    row_own(2)

    @pl.when(active)
    def _():
        for off in range(1, n_seq):
            row_arrival(2, lax.rem(s + off, n_seq))

    @pl.when(jnp.logical_not(active))
    def _():
        copies = [
            pltpu.make_async_copy(tok.at[z], cot_o.at[z], row_recv.at[2, z])
            for z in range(n_seq)
        ]
        for c in copies:
            c.start()
        for c in copies:
            c.wait()

    for k in range(3):
        row_sent(k)
    qkv.finish(direct=True)
    rest.finish()


def front(n_dp, n_seq, tokens, cot, seg, part, shards, cos, sin):
    rows, length, width = tokens.shape
    seq_len = length * n_seq
    dma = pltpu.SemaphoreType.DMA
    struct = jax.ShapeDtypeStruct
    pairs = width // 128
    outs = [
        struct((n_seq, length, width), BF16),
        struct((n_seq, length, width), BF16),
        struct((2, seq_len, 128), BF16),
        struct((seq_len, width), BF16),
        struct((3 * pairs, seq_len, 128), BF16),
    ]
    outs += [struct((n_dp, n_seq) + w.shape, BF16) for w in shards]
    outs += [
        struct((8, width), F32),
        struct((seq_len, width), BF16),
        struct((seq_len, 128), F32),
    ]
    return pl.pallas_call(
        functools.partial(front_kernel, n_dp, n_seq, rows),
        out_shape=outs,
        in_specs=[ANY] * 6 + [VMEM] * 2,
        out_specs=[ANY] * 7 + [VMEM] * 3,
        scratch_shapes=[
            pltpu.VMEM((n_seq, length, width), BF16),
            pltpu.VMEM((n_seq,) + seg.shape[1:], jnp.int32),
            pltpu.VMEM((2, seq_len, 128), BF16),
            pltpu.VMEM((seq_len, width), BF16),
            pltpu.VMEM((3 * pairs, seq_len, 128), BF16),
            pltpu.VMEM((n_dp, n_seq) + shards[0].shape, BF16),
            pltpu.VMEM((width, 3 * width), BF16),
            pltpu.VMEM((seq_len, 256), BF16),
            pltpu.VMEM((2, seq_len, 128), BF16),
            pltpu.VMEM((n_dp, rows, 8, width), F32),
            pltpu.VMEM((rows, 8, width), F32),
            pltpu.VMEM((n_seq, 8, width), F32),
            dma((5,)),
            dma((3, rows)),
            dma((3, n_seq)),
            dma((n_dp,)),
            dma((n_dp,)),
            dma((rows,)),
            dma((n_seq,)),
            dma((2,)),
            dma((2, 2, n_seq)),
            dma((2, 2, n_seq)),
            dma((2, n_seq, 2, n_dp)),
            dma((2, n_seq, 2, n_dp)),
        ],
        compiler_params=pltpu.CompilerParams(
            collective_id=0, has_side_effects=True, vmem_limit_bytes=VMEM_LIMIT
        ),
    )(tokens, cot, seg, part, *shards, cos, sin)


def split3(x):
    high = x.astype(BF16)
    x = x - high.astype(F32)
    middle = x.astype(BF16)
    low = (x - middle.astype(F32)).astype(BF16)
    return high, middle, low


class GradReduce:
    def __init__(self, grad, own, local, core_in, step_in, z_in, sems, n_dp, n_seq):
        self.grad, self.own, self.local = grad, own, local
        self.core_in, self.step_in, self.z_in = core_in, step_in, z_in
        self.sems, self.n_seq = sems, n_seq
        self.bits = list(range(n_dp.bit_length() - 2, 0, -1))
        self.m = len(self.bits)
        self.orders = (list(range(self.m)), list(range(self.m))[::-1])
        self.cols = core_in.shape[-1] // 2

    def my(self, dim):
        d, _ = place()
        return lax.rem(lax.div(d, 1 << self.bits[dim]), 2)

    def mine(self):
        return tuple(self.my(dim) for dim in range(self.m))

    def index(self, done, flip=None):
        return tuple(
            self.my(dim)
            if dim in done
            else 1 - self.my(dim)
            if dim == flip
            else slice(None)
            for dim in range(self.m)
        )

    def core_copies(self, z):
        d, s = place()
        core = lax.rem(d, 2)
        lead = (slice(None),) * self.m
        send, recv, local = self.sems["core"]
        copies = [
            remote(
                self.grad.at[lead + (1 - core, z)],
                self.core_in.at[lead + (z,)],
                send.at[z],
                recv.at[z],
                xor(d, 1),
                s,
            )
        ]
        if self.local:
            copies.append(
                pltpu.make_async_copy(
                    self.grad.at[lead + (core, z)],
                    self.own(lead, z, slice(None)),
                    local.at[z],
                )
            )
        return copies

    def core_start(self, z):
        for c in self.core_copies(z):
            c.start()

    def core_add(self, z):
        for c in self.core_copies(z):
            c.wait()

        @pl.loop(0, 1 << self.m)
        def _(n):
            lead = tuple(
                lax.rem(lax.div(n, 1 << (self.m - 1 - dim)), 2) for dim in range(self.m)
            )
            target = self.own(lead, z, slice(None))
            target[...] = target[...] + self.core_in[lead + (z,)]

    def step_copy(self, z, h, step):
        d, s = place()
        order = self.orders[h]
        send, recv = self.sems["step"]
        cols = pl.ds(h * self.cols, self.cols)
        return remote(
            self.own(self.index(order[:step], order[step]), z, cols),
            self.step_in[h][step].at[z],
            send.at[z, h, step],
            recv.at[z, h, step],
            xor(d, 1 << self.bits[order[step]]),
            s,
        )

    def z_copy(self, z):
        d, s = place()
        send, recv = self.sems["z"]
        return remote(
            self.own(self.mine(), z, slice(None)),
            self.z_in.at[s],
            send.at[z],
            recv.at[s],
            d,
            z,
        )

    def event(self, z, t):
        for h in range(2):
            if t:
                self.step_copy(z, h, t - 1).wait()
                order = self.orders[h]
                cols = pl.ds(h * self.cols, self.cols)
                free = [dim for dim in range(self.m) if dim not in order[:t]]
                for n in range(1 << len(free)):
                    bits = [(n >> (len(free) - 1 - i)) & 1 for i in range(len(free))]
                    lead = tuple(
                        bits[free.index(dim)] if dim in free else self.my(dim)
                        for dim in range(self.m)
                    )
                    target = self.own(lead, z, cols)
                    target[...] = target[...] + self.step_in[h][t - 1][(z, *bits)]
            if t < self.m:
                self.step_copy(z, h, t).start()
        if t == self.m:
            _, s = place()

            @pl.when(z != s)
            def _():
                self.z_copy(z).start()

    def total(self):
        d, s = place()
        send, recv = self.sems["z"]
        for off in range(1, self.n_seq):
            origin = lax.rem(s + off, self.n_seq)
            remote(
                self.own(self.mine(), s, slice(None)),
                self.z_in.at[origin],
                send.at[origin],
                recv.at[origin],
                d,
                origin,
            ).wait_recv()
        total = self.own(self.mine(), s, slice(None))[...].astype(F32)
        for off in range(1, self.n_seq):
            total += self.z_in[lax.rem(s + off, self.n_seq)].astype(F32)
        return total

    def sent(self):
        _, s = place()
        for z in range(self.n_seq):

            @pl.when(z != s)
            def _():
                self.z_copy(z).wait_send()


def back_kernel(n_dp, n_seq, rows, hidden, *refs):
    grad_rest, out_row, wq_full, packed_h, mixed_h, grad_mixed_h, normed_h = refs[:7]
    lse, docs, cos, sin, tok, grad_mid, mod, gm_in = refs[7:15]
    gq_o, go_o, gu_o, gd_o = refs[15:19]
    out_o, dtok_o, gmod_o = refs[19:22]
    refs = refs[22:]
    m = n_dp.bit_length() - 2
    acc_r, core_r, zin_r = refs[:3]
    step_r = (refs[3 : 3 + m], refs[3 + m : 3 + 2 * m])
    refs = refs[3 + 2 * m :]
    w_in, core_q, zin_q = refs[:3]
    step_q = (refs[3 : 3 + m], refs[3 + m : 3 + 2 * m])
    refs = refs[3 + 2 * m :]
    (
        w,
        qkv,
        normed_t,
        grad_qkv,
        dtok,
        q2,
        k2,
        v2,
        g2,
        dq2,
        gmod,
        qkv_sem,
        w_sem,
        row_send,
        row_recv,
        g_send,
        g_recv,
        gd_send,
        gd_recv,
        c_send,
        c_recv,
        c_local,
        s_send,
        s_recv,
        z_send,
        z_recv,
    ) = refs
    d, s = place()
    length, width = out_row.shape[1:]
    seq_len = length * n_seq
    pairs = width // 128
    first = lax.rem(d, 2)
    mine = s - first
    active = (mine >= 0) & (mine < rows)
    core = lax.rem(d, 2)

    def pair_copies(p, slot):
        return [
            pltpu.make_async_copy(
                packed_h.at[kind * pairs + p], qkv.at[slot, kind], qkv_sem.at[slot, kind]
            )
            for kind in range(3)
        ] + [
            pltpu.make_async_copy(
                src.at[:, pl.ds(pl.multiple_of(p * 128, 128), 128)],
                qkv.at[slot, kind],
                qkv_sem.at[slot, kind],
            )
            for kind, src in ((3, mixed_h), (4, grad_mixed_h))
        ]

    for c in pair_copies(0, 0):
        c.start()
    w_copy = pltpu.make_async_copy(wq_full, w_in, w_sem.at[0])
    w_copy.start()
    normed_copy = pltpu.make_async_copy(normed_h, dtok, w_sem.at[1])
    normed_copy.start()
    greet(n_dp, n_seq)

    def sems(i):
        return {
            "core": (c_send.at[i], c_recv.at[i], c_local.at[i]),
            "step": (s_send.at[i], s_recv.at[i]),
            "z": (z_send.at[i], z_recv.at[i]),
        }

    rest = GradReduce(
        grad_rest,
        lambda lead, z, cols: acc_r.at[tuple(lead) + (z, slice(None), cols)],
        True,
        core_r,
        step_r,
        zin_r,
        sems(0),
        n_dp,
        n_seq,
    )
    stage = w_in
    last = GradReduce(
        stage,
        lambda lead, z, cols: stage.at[tuple(lead) + (core, z, slice(None), cols)],
        False,
        core_q,
        step_q,
        zin_q,
        sems(1),
        n_dp,
        n_seq,
    )
    for z in range(n_seq):
        rest.core_start(z)

    pair = ((out_row, out_o), (dtok, dtok_o))

    def row_local(k):
        src, dst = pair[k]
        return pltpu.make_async_copy(src.at[s], dst.at[mine], row_send.at[k, 0])

    def row_remote(k, off):
        src, dst = pair[k]
        to = lax.rem(s + off, n_seq)
        return remote(
            src.at[to], dst.at[mine], row_send.at[k, off], row_recv.at[k, mine], d, to
        )

    def row_start(k):
        @pl.when(active)
        def _():
            row_local(k).start()
            for off in range(1, n_seq):
                row_remote(k, off).start()

    def row_sent(k):
        @pl.when(active)
        def _():
            row_local(k).wait()
            for off in range(1, n_seq):
                row_remote(k, off).wait_send()

    def row_arrivals(k):
        src, dst = pair[k]
        for i in range(rows):

            @pl.when(first + i != s)
            def _():
                remote(
                    src.at[0],
                    dst.at[i],
                    row_send.at[k, 0],
                    row_recv.at[k, i],
                    d,
                    first + i,
                ).wait_recv()

    row_start(0)

    w_copy.wait()
    depth = w_in.shape[-2]
    lead_dims = w_in.shape[:-2]

    join_slabs(w_in, w)
    normed_copy.wait()
    for r in range(n_seq):
        normed_t[:, pl.ds(r * length, length)] = jnp.transpose(dtok[r])

    rest.core_add(0)
    rest.event(0, 0)
    rest.core_add(1)
    rest.event(1, 0)
    slots = {
        0: [("c", 2), ("c", 3)],
        2: [(0, 1)],
        3: [(2, 0)],
        4: [(1, 1)],
        5: [(0, 2), (3, 0)],
        7: [(2, 1)],
        8: [(1, 2)],
        10: [(3, 1)],
        11: [(2, 2)],
    }
    done = {e for v in slots.values() for e in v} | {(0, 0), (1, 0)}
    block = seq_len // 2
    lane = lax.broadcasted_iota(jnp.int32, (seq_len, 128), 1)

    @pl.loop(0, pairs)
    def _(p):
        now = lax.rem(p, 2)

        @pl.when(p + 1 < pairs)
        def _():
            for c in pair_copies(p + 1, 1 - now):
                c.start()

        for c in pair_copies(p, now):
            c.wait()
        queries, keys, values = qkv[now, 0], qkv[now, 1], qkv[now, 2]
        at_p = pl.ds(pl.multiple_of(p * 128, 128), 128)
        grads = qkv[now, 4]
        product = grads.astype(F32) * qkv[now, 3].astype(F32)
        nothing = jnp.zeros_like(grads)
        for j in range(2):
            own = lanes_of(j, grads.shape)
            base = HEAD_DIM * (1 - j) + 8

            def with_terms(x, other, column):
                for n, term in enumerate(split3(column)):
                    other = jnp.where(lane == base + n, term, other)
                return jnp.where(own, x, other)

            inner = jnp.sum(jnp.where(own, product, 0.0), -1, keepdims=True)
            stat = jnp.sum(jnp.where(lane == 2 * p + j, lse[...], 0.0), -1, keepdims=True)
            g2[j] = with_terms(grads, nothing, -inner)
            q2[j] = with_terms(queries, docs[1], -stat)
            k2[j] = jnp.where(own, keys, docs[0])
            v2[j] = jnp.where(own, values, docs[0])
        for i in range(seq_len // block):
            at = pl.ds(i * block, block)
            dvs, dks = [], []
            for j in range(2):
                probs = jnp.exp2(dot(k2[j, at, :], q2[j], ((1,), (1,))))
                ds = probs * dot(v2[j, at, :], g2[j], ((1,), (1,)))
                ds = ds.astype(BF16)
                dvs.append(dot(probs.astype(BF16), grads, ((1,), (0,))))
                dks.append(dot(ds, queries, ((1,), (0,))))
                dq = dot(ds, qkv[now, 1, at, :], ((0,), (0,)))
                if i == 0:
                    dq2[j] = dq
                else:
                    dq2[j] += dq
            here = lanes_of(0, dvs[0].shape)
            dk = jnp.where(here, dks[0], dks[1]) * (1.0 / LOG2E)
            grad_qkv[at, pl.ds(pl.multiple_of(width + p * 128, 128), 128)] = (
                dk * cos[at, :] + swap_halves(dk * sin[at, :])
            ).astype(BF16)
            grad_qkv[at, pl.ds(pl.multiple_of(2 * width + p * 128, 128), 128)] = jnp.where(
                here, dvs[0], dvs[1]
            ).astype(BF16)
            for slot, events in slots.items():
                if slot % 2 != i:
                    continue

                @pl.when(p == slot // 2)
                def _():
                    for z, t in events:
                        if z == "c":
                            rest.core_add(t)
                        else:
                            rest.event(z, t)

        dq = jnp.where(lanes_of(0, dq2.shape[1:]), dq2[0], dq2[1])
        dq = dq * (1.0 / math.sqrt(HEAD_DIM))
        grad_qkv[:, at_p] = (dq * cos[...] + swap_halves(dq * sin[...])).astype(BF16)

    gain = mod[6:7, :]
    scale = 1.0 + mod[1:2, :]
    gmod[...] = gm_in[...]
    for r in range(n_seq):
        at = pl.ds(r * length, length)
        e = dot(grad_qkv[at, :], w[...], ((1,), (1,)))
        normal, rstd = normalise(tok[at, :].astype(F32))
        gmod[0:1, :] += jnp.sum(e, 0, keepdims=True)
        weighted = jnp.sum(e * normal, 0, keepdims=True)
        gmod[1:2, :] += weighted * gain
        gmod[6:7, :] += weighted * scale
        h = e * (gain * scale)
        mean_h = jnp.mean(h, -1, keepdims=True)
        mean_hz = jnp.mean(h * normal, -1, keepdims=True)
        dtok[r] = (grad_mid[at, :] + (h - mean_h - normal * mean_hz) * rstd).astype(BF16)

    own_row = pltpu.make_async_copy(gmod, gmod_o.at[d, mine], g_send.at[0])

    def group_copy(off):
        return remote(
            gmod,
            gmod_o.at[d, mine],
            g_send.at[off],
            g_recv.at[s],
            d,
            lax.rem(s + off, n_seq),
        )

    @pl.when(active)
    def _():
        own_row.start()
        for off in range(1, n_seq):
            group_copy(off).start()

    row_start(1)

    for c in range(3 * width // 256):
        cols = pl.ds(c * 256, 256)
        g = dot(normed_t[...], grad_qkv[:, cols], ((1,), (0,)))
        for i in range(n_dp * n_seq):
            k, idx = i, []
            for n in lead_dims[::-1]:
                idx.append(k % n)
                k //= n
            stage[tuple(idx[::-1]) + (slice(None), cols)] = g[
                i * depth : (i + 1) * depth
            ].astype(BF16)
    for z in range(n_seq):
        last.core_start(z)
    for z in range(n_seq):
        for t in range(m + 1):
            if (z, t) not in done:
                rest.event(z, t)
    for z in range(n_seq):
        last.core_add(z)
        last.event(z, 0)

    @pl.when(active)
    def _():
        own_row.wait()

    for i in range(rows):
        owner = first + i

        @pl.when(owner != s)
        def _():
            remote(
                gmod, gmod_o.at[d, i], g_send.at[0], g_recv.at[owner], d, owner
            ).wait_recv()

    def dp_copy(off):
        return remote(
            gmod_o.at[d], gmod_o.at[d], gd_send.at[off], gd_recv.at[off], xor(d, off), s
        )

    for off in range(1, n_dp):
        dp_copy(off).start()
    for t in range(1, m + 1):
        for z in range(n_seq):
            last.event(z, t)
    total = rest.total()
    go_o[...] = total[:, :width]
    gu_o[...] = total[:, width : width + hidden]
    for i in range(hidden // width):
        col = width + hidden + i * width
        gd_o[i * depth : (i + 1) * depth, :] = total[:, col : col + width]
    gq_o[...] = last.total()

    for off in range(1, n_dp):
        e = xor(d, off)
        dp_copy(off).wait_send()
        remote(
            gmod_o.at[e], gmod_o.at[e], gd_send.at[off], gd_recv.at[off], e, s
        ).wait_recv()

    @pl.when(active)
    def _():
        for off in range(1, n_seq):
            group_copy(off).wait_send()

    for k in range(2):
        row_sent(k)
        row_arrivals(k)
    rest.sent()
    last.sent()


def back(n_dp, n_seq, rows, hidden, grad_rest, out_row, wq, hbm_args, vmem_args):
    dma = pltpu.SemaphoreType.DMA
    struct = jax.ShapeDtypeStruct
    m = n_dp.bit_length() - 2
    lead = (2,) * m
    length, width = out_row.shape[1:]
    seq_len = length * n_seq
    depth = wq.shape[-2]
    wide = grad_rest.shape[-1]
    gmod = vmem_args[-1]
    outs = [
        struct((depth, 3 * width), F32),
        struct((depth, width), F32),
        struct((depth, hidden), F32),
        struct((depth * hidden // width, width), F32),
        struct((rows, length, width), BF16),
        struct((rows, length, width), BF16),
        struct((n_dp, rows) + gmod.shape, F32),
    ]

    def reduce_scratch(n, acc):
        slabs = [
            pltpu.VMEM(acc + (n_seq, depth, n), BF16),
            pltpu.VMEM(lead + (n_seq, depth, n), BF16),
            pltpu.VMEM((n_seq, depth, n), BF16),
        ]
        for _ in range(2):
            for step in range(m):
                slabs.append(
                    pltpu.VMEM(
                        (n_seq,) + (2,) * (m - 1 - step) + (depth, n // 2), BF16
                    )
                )
        return slabs

    scratch = (
        reduce_scratch(wide, lead)
        + reduce_scratch(3 * width, lead + (2,))
        + [
            pltpu.VMEM((width, 3 * width), BF16),
            pltpu.VMEM((2, 5, seq_len, 128), BF16),
            pltpu.VMEM((width, seq_len), BF16),
            pltpu.VMEM((seq_len, 3 * width), BF16),
            pltpu.VMEM((n_seq, length, width), BF16),
        ]
        + [pltpu.VMEM((2, seq_len, 128), BF16)] * 4
        + [
            pltpu.VMEM((2, seq_len, 128), F32),
            pltpu.VMEM(gmod.shape, F32),
            dma((2, 5)),
            dma((2,)),
            dma((2, n_seq)),
            dma((2, rows)),
            dma((n_seq,)),
            dma((n_seq,)),
            dma((n_dp,)),
            dma((n_dp,)),
            dma((2, n_seq)),
            dma((2, n_seq)),
            dma((2, n_seq)),
            dma((2, n_seq, 2, m)),
            dma((2, n_seq, 2, m)),
            dma((2, n_seq)),
            dma((2, n_seq)),
        ]
    )
    split = lead + (2, n_seq)
    return pl.pallas_call(
        functools.partial(back_kernel, n_dp, n_seq, rows, hidden),
        out_shape=outs,
        in_specs=[ANY] * 7 + [VMEM] * len(vmem_args),
        out_specs=[VMEM] * 4 + [ANY] * 3,
        scratch_shapes=scratch,
        compiler_params=pltpu.CompilerParams(
            collective_id=1, has_side_effects=True, vmem_limit_bytes=VMEM_LIMIT
        ),
    )(
        grad_rest.reshape(split + grad_rest.shape[-2:]),
        out_row,
        wq.reshape(split + wq.shape[-2:]),
        *hbm_args,
        *vmem_args,
    )


def rotary_tables(seq_len):
    half = HEAD_DIM // 2
    freq = np.exp(np.float32(-math.log(10000.0)) * np.arange(half, dtype=np.float32) / np.float32(half))
    angles = np.arange(seq_len, dtype=np.float32)[:, None] * freq.astype(np.float32)[None, :]
    cos = np.tile(np.cos(angles), (1, 4)).astype(np.float32)
    sin = np.sin(angles)
    sin = np.concatenate([-sin, sin, -sin, sin], 1).astype(np.float32)
    return jnp.asarray(cos), jnp.asarray(sin)


def time_embed(step_ids, model_dim):
    half_dim = model_dim // 2
    frequency = jnp.exp(-math.log(10000.0) * jnp.arange(half_dim, dtype=jnp.float32) / half_dim)
    angles = step_ids.astype(jnp.float32)[:, None] * frequency[None, :]
    return jnp.concatenate([jnp.cos(angles), jnp.sin(angles)], axis=-1)


def modulate(inputs, norm_gain, mod_scale, mod_shift):
    average = jnp.mean(inputs, -1, keepdims=True)
    centred = inputs - average
    variance = jnp.mean(centred * centred, -1, keepdims=True)
    return centred * lax.rsqrt(variance + EPSILON) * norm_gain * (1.0 + mod_scale) + mod_shift


def matmul(a, b, spec):
    return jnp.einsum(spec, a, b, preferred_element_type=F32)


def placed_at(vector, index, length):
    whole = jnp.zeros((length,), F32)
    return lax.dynamic_update_slice(whole, vector.astype(F32), (index * vector.shape[0],))


def shards(
    n_dp,
    n_seq,
    tokens,
    segments,
    timesteps,
    w_mod,
    b_mod,
    gain_attn,
    w_qkv,
    w_out,
    gain_mlp,
    w_up,
    w_down,
    cotangent,
):
    rows, length, width = tokens.shape
    seq_len = length * n_seq
    hidden = w_up.shape[1]
    d, s = place()
    me = d * n_seq + s
    depth = w_mod.shape[0]
    cos, sin = rotary_tables(seq_len)

    steps = lax.all_gather(timesteps, "dp", axis=0, tiled=True)
    embedding = lax.dynamic_slice_in_dim(
        time_embed(steps, width).astype(BF16), me * depth, depth, 1
    )
    part = matmul(embedding, w_mod, "rk,kn->rn") + placed_at(b_mod, me, 6 * width)
    gains = jnp.concatenate(
        [placed_at(gain_attn, me, width), placed_at(gain_mlp, me, width)]
    )
    part = jnp.concatenate([part, jnp.broadcast_to(gains, (part.shape[0], 2 * width))], 1)
    part = part.reshape(n_dp, rows, 8, width)
    seg = jnp.broadcast_to(segments[:, None, :], (rows, 8, length))

    packed_rest = jnp.concatenate(
        [w_out, w_up]
        + [w_down[i * depth : (i + 1) * depth] for i in range(hidden // width)],
        1,
    )
    tok, cot, docs, normed_a, packed, wq, rest, mod, mixed, lse = front(
        n_dp, n_seq, tokens, cotangent, seg, part, (w_qkv, packed_rest), cos, sin
    )
    tok = tok.reshape(seq_len, width)
    cot = cot.reshape(seq_len, width).astype(F32)
    wo = rest[..., :width].reshape(width, width)
    wu = rest[..., width : width + hidden].reshape(width, hidden)
    wd = jnp.stack(
        [
            rest[..., width + hidden + i * width : width + hidden + (i + 1) * width]
            for i in range(hidden // width)
        ],
        2,
    ).reshape(hidden, width)
    shift_a, scale_a, gate_a, shift_m, scale_m, gate_m, gain_a, gain_m = (
        mod[j : j + 1] for j in range(8)
    )

    stream = tok.astype(F32)
    attn_out = matmul(mixed, wo, "td,de->te")
    middle = stream + gate_a * attn_out
    normed_m, norm_back_m = jax.vjp(modulate, middle, gain_m, scale_m, shift_m)
    normed_m = normed_m.astype(BF16)
    up_proj = matmul(normed_m, wu, "td,df->tf")
    activated, gelu_back = jax.vjp(jax.nn.gelu, up_proj)
    activated = activated.astype(BF16)
    mlp_out = matmul(activated, wd, "tf,fd->td")
    output = (middle + gate_m * mlp_out).astype(BF16)

    grad_mlp = (cot * gate_m).astype(BF16)
    grad_gate_m = jnp.sum(cot * mlp_out, 0, keepdims=True)
    grad_down = matmul(activated, grad_mlp, "tf,td->fd").astype(BF16)
    grad_act = matmul(grad_mlp, wd, "td,fd->tf")
    grad_up = gelu_back(grad_act)[0].astype(BF16)
    grad_wup = matmul(normed_m, grad_up, "td,tf->df").astype(BF16)
    grad_hm = matmul(grad_up, wu, "tf,df->td")
    grad_mid_norm, grad_gain_m, grad_scale_m, grad_shift_m = norm_back_m(grad_hm)
    grad_mid = cot + grad_mid_norm
    grad_gate_a = jnp.sum(grad_mid * attn_out, 0, keepdims=True)
    grad_attn = (grad_mid * gate_a).astype(BF16)
    grad_wout = matmul(mixed, grad_attn, "td,te->de").astype(BF16)
    grad_mixed = matmul(grad_attn, wo, "te,de->td").astype(BF16)

    gm_in = jnp.concatenate(
        [
            jnp.zeros((2, width), F32),
            grad_gate_a,
            grad_shift_m,
            grad_scale_m,
            grad_gate_m,
            jnp.zeros((1, width), F32),
            grad_gain_m,
        ],
        0,
    )

    def cut(g, n):
        return g.reshape((n_dp, n_seq, n * depth, -1))

    down = cut(grad_down, hidden // width)
    grad_rest = jnp.concatenate(
        [cut(grad_wout, 1), cut(grad_wup, 1)]
        + [down[:, :, i * depth : (i + 1) * depth] for i in range(hidden // width)],
        -1,
    )
    g_wqkv, g_wout, g_wup, g_wdown, out, d_tok, gmods = back(
        n_dp,
        n_seq,
        rows,
        hidden,
        grad_rest,
        output.reshape(n_seq, length, width),
        wq,
        (packed, mixed, grad_mixed, normed_a.reshape(n_seq, length, width)),
        (
            lse,
            docs,
            cos,
            sin,
            tok,
            grad_mid.astype(BF16),
            mod,
            gm_in,
        ),
    )
    gmods = gmods.reshape(n_dp * rows, 8 * width)
    g_w_mod = jnp.dot(
        embedding.astype(F32).T,
        gmods[:, : 6 * width],
        precision=lax.Precision.HIGHEST,
        preferred_element_type=F32,
    )
    summed = jnp.sum(gmods, 0)

    def own_part(vector, n):
        return lax.dynamic_slice_in_dim(vector, me * n, n, 0)

    return (
        out,
        d_tok,
        g_w_mod,
        own_part(summed[: 6 * width], b_mod.shape[0]),
        own_part(summed[6 * width : 7 * width], gain_attn.shape[0]),
        g_wqkv,
        g_wout,
        own_part(summed[7 * width :], gain_mlp.shape[0]),
        g_wup,
        g_wdown,
    )


def solution(mesh):
    both = P(("dp", "seq"))
    wide = P(("dp", "seq"), None)
    tokens = P("dp", "seq", None)
    return jax.shard_map(
        functools.partial(shards, mesh.shape["dp"], mesh.shape["seq"]),
        mesh=mesh,
        in_specs=(
            tokens,
            P("dp", "seq"),
            P("dp"),
            wide,
            both,
            both,
            wide,
            wide,
            both,
            wide,
            wide,
            tokens,
        ),
        out_specs=(tokens, tokens, wide, both, both, wide, wide, both, wide, wide),
        check_vma=False,
    )
```

```python
import functools
import math

import jax
import jax.numpy as jnp
import numpy as np
from jax import lax
from jax.experimental import pallas as pl
from jax.experimental.pallas import tpu as pltpu
from jax.sharding import PartitionSpec as P

HEAD_DIM = 64
EPSILON = 1e-06
MASK_FILL = -1e30
MESH = pl.DeviceIdType.MESH
BF16 = jnp.bfloat16
F32 = jnp.float32
ANY = pl.BlockSpec(memory_space=pl.ANY)
VMEM = pl.BlockSpec(memory_space=pltpu.VMEM)
VMEM_LIMIT = 60 * 2**20
LOG2E = math.log2(math.e)


def place():
    return lax.axis_index("dp"), lax.axis_index("seq")


def xor(index, bits):
    return jnp.bitwise_xor(index, bits)


def remote(src, dst, send, recv, dp, seq):
    return pltpu.make_async_remote_copy(
        src_ref=src,
        dst_ref=dst,
        send_sem=send,
        recv_sem=recv,
        device_id=(dp, seq),
        device_id_type=MESH,
    )


def greet(n_dp, n_seq):
    d, s = place()
    barrier = pltpu.get_barrier_semaphore()
    for off in range(1, n_dp):
        pl.semaphore_signal(
            barrier, inc=1, device_id=(xor(d, off), s), device_id_type=MESH
        )
    for off in range(1, n_seq):
        pl.semaphore_signal(
            barrier, inc=1, device_id=(d, lax.rem(s + off, n_seq)), device_id_type=MESH
        )
    pl.semaphore_wait(barrier, n_dp - 1 + n_seq - 1)


def bit_orders(n_dp):
    high = [1 << b for b in range(1, n_dp.bit_length() - 1)]
    return (high + [1], high[::-1] + [1])


def signed(value, sign):
    return value if sign > 0 else -value


class WeightGather:
    def __init__(self, shard, full, own_sem, z_send, z_recv, x_send, x_recv, n_dp, n_seq):
        self.shard, self.full, self.own_sem = shard, full, own_sem
        self.z_send, self.z_recv = z_send, z_recv
        self.x_send, self.x_recv = x_send, x_recv
        self.n_seq = n_seq
        self.cols = shard.shape[1] // 2
        self.orders = bit_orders(n_dp)
        self.steps = len(self.orders[0])
        self.groups = []
        for h in range(2):
            known = [(0, 0)]
            for step, bit in enumerate(self.orders[h]):
                known += [(off ^ bit, step + 1) for off, _ in known]
            self.groups.append(known)

    def own(self):
        d, s = place()
        return pltpu.make_async_copy(self.shard, self.full.at[d, s], self.own_sem)

    def z_copy(self, way, k):
        d, s = place()
        origin = s - signed(k - 1, way)
        side = 0 if way > 0 else 1
        src = self.shard if k == 1 else self.full.at[d, origin]
        return remote(
            src,
            self.full.at[d, origin],
            self.z_send.at[side, k],
            self.z_recv.at[side, k],
            d,
            s + way,
        )

    def direct_copy(self, way, k):
        d, s = place()
        side = 0 if way > 0 else 1
        return remote(
            self.shard,
            self.full.at[d, s],
            self.z_send.at[side, k],
            self.z_recv.at[side, k],
            d,
            s + signed(k, way),
        )

    def direct_each(self, body):
        d, s = place()
        for k in range(1, self.n_seq):
            for way in (1, -1):
                to = s + signed(k, way)

                @pl.when((to >= 0) & (to < self.n_seq))
                def _():
                    body(self.direct_copy(way, k))

    def z_valid(self, way, k):
        d, s = place()
        origin = s - signed(k - 1, way)
        to = s + way
        return (origin >= 0) & (origin < self.n_seq) & (to >= 0) & (to < self.n_seq)

    def x_copy(self, origin, h, off, bit, own=False):
        d, s = place()
        cols = pl.ds(h * self.cols, self.cols)
        dst = self.full.at[xor(d, off), origin, :, cols]
        src = self.shard.at[:, cols] if own else dst
        return remote(
            src,
            dst,
            self.x_send.at[origin, h, off ^ bit],
            self.x_recv.at[origin, h, off ^ bit],
            xor(d, bit),
            s,
        )

    def each(self, k, body):
        d, s = place()
        if k == 0:
            body(s, 0)
            return
        for way in (1, -1):
            origin = s - signed(k, way)

            @pl.when((origin >= 0) & (origin < self.n_seq))
            def _():
                body(origin, way)

    def z_start(self, k):
        for way in (1, -1):

            @pl.when(self.z_valid(way, k))
            def _():
                self.z_copy(way, k).start()

    def own_start(self):
        self.own().start()
        d, s = place()
        for h in range(2):
            for bit in self.orders[h]:
                self.x_copy(s, h, 0, bit, True).start()

    def event(self, k, t, forward=True):
        if t == 0:
            d, s = place()

            def arrival(origin, way):
                side = 0 if way > 0 else 1
                remote(
                    self.shard,
                    self.full.at[d, origin],
                    self.z_send.at[side, k],
                    self.z_recv.at[side, k],
                    d,
                    s,
                ).wait_recv()
                for h in range(2):
                    for bit in self.orders[h]:
                        self.x_copy(origin, h, 0, bit).start()

            self.each(k, arrival)
            if forward and k + 1 < self.n_seq:
                self.z_start(k + 1)
            return

        def passing(origin, way):
            for h in range(2):
                for off, step in self.groups[h]:
                    if step != t:
                        continue
                    self.x_copy(origin, h, off, 0).wait_recv()
                    for bit in self.orders[h][t:]:
                        self.x_copy(origin, h, off, bit).start()

        self.each(k, passing)

    def finish(self, direct=False):
        if direct:
            self.direct_each(lambda copy: copy.wait_send())
        for k in range(1, self.n_seq if not direct else 1):
            for way in (1, -1):

                @pl.when(self.z_valid(way, k))
                def _():
                    self.z_copy(way, k).wait_send()

        for k in range(self.n_seq):

            def sent(origin, way):
                for h in range(2):
                    for off, step in self.groups[h]:
                        for bit in self.orders[h][step:]:
                            self.x_copy(origin, h, off, bit).wait_send()

            self.each(k, sent)


def dot(a, b, dims):
    return lax.dot_general(a, b, (dims, ((), ())), preferred_element_type=F32)


def swap_halves(x):
    quarter = HEAD_DIM // 2
    lane = lax.broadcasted_iota(jnp.int32, x.shape, 1)
    return jnp.where(
        lax.rem(lane, HEAD_DIM) < quarter,
        pltpu.roll(x, 128 - quarter, axis=1),
        pltpu.roll(x, quarter, axis=1),
    )


def normalise(x):
    mean = jnp.mean(x, -1, keepdims=True)
    centred = x - mean
    var = jnp.mean(centred * centred, -1, keepdims=True)
    rstd = lax.rsqrt(var + EPSILON)
    return centred * rstd, rstd


def join_slabs(slabs, whole):
    depth = slabs.shape[-2]
    count = math.prod(slabs.shape[:-2])
    group = 16 // math.gcd(16, depth)

    @pl.loop(0, count // group)
    def _(i):
        parts = []
        for j in range(group):
            k, idx = i * group + j, []
            for n in slabs.shape[:-2][::-1]:
                idx.append(lax.rem(k, n))
                k = lax.div(k, n)
            parts.append(slabs[tuple(idx[::-1])])
        rows = group * depth
        whole[pl.ds(pl.multiple_of(i * rows, rows), rows), :] = jnp.concatenate(parts, 0)


def lanes_of(j, shape):
    lane = lax.broadcasted_iota(jnp.int32, shape, 1)
    return lax.div(lane, HEAD_DIM) == j


def front_kernel(n_dp, n_seq, rows, *refs):
    tokens, cot, seg, part, *shards = refs[:6]
    cos, sin = refs[6:8]
    tok_o, cot_o, doc_o, norm_o, pack_o, *fulls = refs[8:15]
    mod_o, mixed_o, lse_o = refs[15:18]
    (
        tok,
        segs,
        docs,
        normed,
        packed,
        w_in,
        w,
        values,
        keys,
        mod_in,
        mod_sum,
        mod_row,
        out_sem,
        row_send,
        row_recv,
        mod_send,
        mod_recv,
        modz_send,
        modz_recv,
        own_sem,
        z_send,
        z_recv,
        x_send,
        x_recv,
    ) = refs[18:]
    d, s = place()
    length, width = tokens.shape[1:]
    seq_len = length * n_seq
    first = lax.rem(d, 2)
    mine = s - first
    active = (mine >= 0) & (mine < rows)
    greet(n_dp, n_seq)

    def mod_copy(off):
        return remote(
            part.at[xor(d, off)],
            mod_in.at[d],
            mod_send.at[off],
            mod_recv.at[off],
            xor(d, off),
            s,
        )

    own_part = pltpu.make_async_copy(part.at[d], mod_in.at[d], mod_send.at[0])
    own_part.start()
    for off in range(1, n_dp):
        mod_copy(off).start()

    qkv, rest = [
        WeightGather(
            shards[i],
            fulls[i],
            own_sem.at[i],
            z_send.at[i],
            z_recv.at[i],
            x_send.at[i],
            x_recv.at[i],
            n_dp,
            n_seq,
        )
        for i in range(2)
    ]
    qkv.direct_each(lambda copy: copy.start())
    rest.z_start(1)
    qkv.own_start()

    trio = ((tokens, tok), (seg, segs), (cot, cot_o))

    def row_local(k, i):
        src, dst = trio[k]
        return pltpu.make_async_copy(src.at[i], dst.at[s], row_send.at[k, i])

    def row_remote(k, i):
        src, dst = trio[k]
        return remote(
            src.at[i], dst.at[s], row_send.at[k, i], row_recv.at[k, s], d, first + i
        )

    def row_start(k):
        for i in range(rows):

            @pl.when(first + i == s)
            def _():
                row_local(k, i).start()

            @pl.when(first + i != s)
            def _():
                row_remote(k, i).start()

    def row_sent(k):
        for i in range(rows):

            @pl.when(first + i != s)
            def _():
                row_remote(k, i).wait_send()

    def row_arrival(k, origin):
        src, dst = trio[k]
        remote(
            src.at[0],
            dst.at[origin],
            row_send.at[k, 0],
            row_recv.at[k, origin],
            d,
            origin,
        ).wait_recv()

    def row_own(k):
        for i in range(rows):

            @pl.when(first + i == s)
            def _():
                row_local(k, i).wait()

    def mod_exchange():
        own_part.wait()
        for off in range(1, n_dp):
            remote(
                part.at[d],
                mod_in.at[xor(d, off)],
                mod_send.at[off],
                mod_recv.at[off],
                d,
                s,
            ).wait_recv()
        total = mod_in[0]
        for e in range(1, n_dp):
            total += mod_in[e]
        mod_sum[...] = total
        for i in range(rows):

            @pl.when(first + i == s)
            def _():
                mod_row[s] = mod_sum[i]

            @pl.when(first + i != s)
            def _():
                remote(
                    mod_sum.at[i],
                    mod_row.at[s],
                    modz_send.at[i],
                    modz_recv.at[s],
                    d,
                    first + i,
                ).start()

    @pl.when(jnp.logical_not(active))
    def _():
        tok[...] = jnp.zeros_like(tok)
        segs[...] = jnp.zeros_like(segs)

    row_start(1)
    mod_exchange()
    row_start(0)
    for k in range(1, n_seq):
        qkv.event(k, 0, forward=False)
    for k in range(n_seq):
        qkv.event(k, 1)
    rest.own_start()
    rest.event(1, 0)
    for t in range(2, qkv.steps + 1):
        for k in range(n_seq):
            qkv.event(k, t)
    stage = pltpu.make_async_copy(fulls[0], w_in, out_sem.at[0])
    qkv.own().wait()
    stage.start()

    @pl.when(active)
    def _():
        for off in range(1, n_seq):
            row_arrival(1, lax.rem(s + off, n_seq))

    row_own(1)
    lane = lax.broadcasted_iota(jnp.int32, (length, 128), 1)
    lane = lax.rem(lane, HEAD_DIM).astype(F32)
    for z in range(n_seq):
        ids = jnp.transpose(
            jnp.broadcast_to(segs[z, 0:1, :].astype(F32), (128, length))
        )
        same = ids == lane
        at = pl.ds(z * length, length)
        docs[0, at, :] = jnp.where(
            same | ((lane >= 8.0) & (lane < 11.0)), 1.0, 0.0
        ).astype(BF16)
        docs[1, at, :] = jnp.where(same | (lane >= 8.0), 0.0, MASK_FILL).astype(BF16)
    doc_copy = pltpu.make_async_copy(docs, doc_o, out_sem.at[1])
    doc_copy.start()

    stage.wait()
    depth = w_in.shape[2]

    join_slabs(w_in, w)

    @pl.when(active)
    def _():
        for off in range(1, n_seq):
            origin = lax.rem(s + off, n_seq)
            remote(
                mod_sum.at[0],
                mod_row.at[origin],
                modz_send.at[0],
                modz_recv.at[origin],
                d,
                origin,
            ).wait_recv()
        total = mod_row[0]
        for z in range(1, n_seq):
            total += mod_row[z]
        mod_o[...] = total

    @pl.when(jnp.logical_not(active))
    def _():
        mod_o[...] = jnp.zeros_like(mod_o)

    rest.event(0, 1)

    gain = mod_o[6:7, :] * (1.0 + mod_o[1:2, :])
    shift = mod_o[0:1, :]
    row_own(0)
    for off in range(n_seq):
        z = lax.rem(s + off, n_seq)
        if off:

            @pl.when(active)
            def _():
                row_arrival(0, z)

        normal, _ = normalise(tok[z].astype(F32))
        at = pl.ds(pl.multiple_of(z * length, length), length)
        normed[at, :] = (normal * gain + shift).astype(BF16)
    outs = [
        pltpu.make_async_copy(tok, tok_o, out_sem.at[2]),
        pltpu.make_async_copy(normed, norm_o, out_sem.at[3]),
    ]
    for c in outs:
        c.start()

    for kind in range(3):

        @pl.loop(0, width // 256)
        def _(c):
            col = kind * width + c * 256
            wc = w[:, pl.ds(pl.multiple_of(col, 256), 256)]
            for r in range(seq_len // 256):
                at = pl.ds(r * 256, 256)
                y = dot(normed[at, :], wc, ((1,), (0,)))
                for j in range(2):
                    p = y[:, j * 128 : (j + 1) * 128]
                    if kind < 2:
                        p = p * cos[at, :] + swap_halves(p) * sin[at, :]
                    if kind == 0:
                        p = p * (LOG2E / math.sqrt(HEAD_DIM))
                    packed[kind * (width // 128) + c * 2 + j, at, :] = p.astype(BF16)

    pack_copy = pltpu.make_async_copy(packed, pack_o, out_sem.at[4])
    pack_copy.start()
    early = [(0, 2), (1, 1), (0, 3), (2, 0)]
    for e in early:
        rest.event(*e)
    row_start(2)
    pairs = width // 128
    slots = {
        1: [(1, 2)],
        2: [(3, 0), (2, 1), (1, 3)],
        4: [(2, 2)],
        5: [(3, 1)],
    }
    done = {e for v in slots.values() for e in v}
    done |= set(early) | {(1, 0), (0, 1)}

    values[:, 128:] = jnp.ones((seq_len, 128), BF16)
    block = 128
    lse_o[...] = jnp.zeros_like(lse_o)

    @pl.loop(0, pairs)
    def _(p):
        k = packed[pairs + p]
        values[:, :128] = packed[2 * pairs + p]
        for j in range(2):
            keys[j] = jnp.where(lanes_of(j, k.shape), k, docs[0])
        for i in range(seq_len // block):
            at = pl.ds(i * block, block)
            q = packed[p, at, :]
            both = []
            stats = lse_o[at, :]
            lane = lax.broadcasted_iota(jnp.int32, (block, 128), 1)
            for j in range(2):
                own = lanes_of(j, q.shape)
                scores = dot(jnp.where(own, q, docs[1, at, :]), keys[j], ((1,), (1,)))
                top = jnp.max(scores, -1, keepdims=True)
                e = jnp.exp2(scores - top).astype(BF16)
                o = dot(e, values[...], ((1,), (0,)))
                total = o[:, 128:]
                both.append(o[:, :128] / total)
                stats = jnp.where(lane == 2 * p + j, top + jnp.log2(total), stats)
            lse_o[at, :] = stats
            mixed_o[at, pl.ds(pl.multiple_of(p * 128, 128), 128)] = jnp.where(
                lane < HEAD_DIM, both[0], both[1]
            ).astype(BF16)
        for slot, events in slots.items():

            @pl.when(p == slot)
            def _():
                for k, t in events:
                    rest.event(k, t)

    for t in range(1, rest.steps + 1):
        for k in range(n_seq):
            if (k, t) not in done:
                rest.event(k, t)

    for i in range(rows):

        @pl.when(first + i != s)
        def _():
            remote(
                mod_sum.at[i], mod_row.at[s], modz_send.at[i], modz_recv.at[s], d, first + i
            ).wait_send()

    for off in range(1, n_dp):
        mod_copy(off).wait_send()
    rest.own().wait()
    for c in outs + [doc_copy, pack_copy]:
        c.wait()

    row_own(2)

    @pl.when(active)
    def _():
        for off in range(1, n_seq):
            row_arrival(2, lax.rem(s + off, n_seq))

    @pl.when(jnp.logical_not(active))
    def _():
        copies = [
            pltpu.make_async_copy(tok.at[z], cot_o.at[z], row_recv.at[2, z])
            for z in range(n_seq)
        ]
        for c in copies:
            c.start()
        for c in copies:
            c.wait()

    for k in range(3):
        row_sent(k)
    qkv.finish(direct=True)
    rest.finish()


def front(n_dp, n_seq, tokens, cot, seg, part, shards, cos, sin):
    rows, length, width = tokens.shape
    seq_len = length * n_seq
    dma = pltpu.SemaphoreType.DMA
    struct = jax.ShapeDtypeStruct
    pairs = width // 128
    outs = [
        struct((n_seq, length, width), BF16),
        struct((n_seq, length, width), BF16),
        struct((2, seq_len, 128), BF16),
        struct((seq_len, width), BF16),
        struct((3 * pairs, seq_len, 128), BF16),
    ]
    outs += [struct((n_dp, n_seq) + w.shape, BF16) for w in shards]
    outs += [
        struct((8, width), F32),
        struct((seq_len, width), BF16),
        struct((seq_len, 128), F32),
    ]
    return pl.pallas_call(
        functools.partial(front_kernel, n_dp, n_seq, rows),
        out_shape=outs,
        in_specs=[ANY] * 6 + [VMEM] * 2,
        out_specs=[ANY] * 7 + [VMEM] * 3,
        scratch_shapes=[
            pltpu.VMEM((n_seq, length, width), BF16),
            pltpu.VMEM((n_seq,) + seg.shape[1:], jnp.int32),
            pltpu.VMEM((2, seq_len, 128), BF16),
            pltpu.VMEM((seq_len, width), BF16),
            pltpu.VMEM((3 * pairs, seq_len, 128), BF16),
            pltpu.VMEM((n_dp, n_seq) + shards[0].shape, BF16),
            pltpu.VMEM((width, 3 * width), BF16),
            pltpu.VMEM((seq_len, 256), BF16),
            pltpu.VMEM((2, seq_len, 128), BF16),
            pltpu.VMEM((n_dp, rows, 8, width), F32),
            pltpu.VMEM((rows, 8, width), F32),
            pltpu.VMEM((n_seq, 8, width), F32),
            dma((5,)),
            dma((3, rows)),
            dma((3, n_seq)),
            dma((n_dp,)),
            dma((n_dp,)),
            dma((rows,)),
            dma((n_seq,)),
            dma((2,)),
            dma((2, 2, n_seq)),
            dma((2, 2, n_seq)),
            dma((2, n_seq, 2, n_dp)),
            dma((2, n_seq, 2, n_dp)),
        ],
        compiler_params=pltpu.CompilerParams(
            collective_id=0, has_side_effects=True, vmem_limit_bytes=VMEM_LIMIT
        ),
    )(tokens, cot, seg, part, *shards, cos, sin)


GELU_A = math.sqrt(2.0 / math.pi)
GELU_B = 0.044715 * GELU_A


def gelu_both(u):
    square = u * u
    half = 0.5 * jnp.tanh(u * (GELU_B * square + GELU_A)) + 0.5
    value = u * half
    slope = half + value * (1.0 - half) * (6.0 * GELU_B * square + 2.0 * GELU_A)
    return value, slope


def middle_kernel(block, *refs):
    mixed_h, tok_h, cot_h, rest_h, slabs_h, mod = refs[:6]
    out_h, mid_h, gmixed_h, grad_h, gm = refs[6:11]
    (
        wo,
        wu,
        wd,
        slabs,
        mixed,
        tok,
        cot,
        act,
        slope,
        normed,
        g_mlp,
        g_attn,
        turned,
        out,
        mid,
        g_mixed,
        sems,
    ) = refs[11:]
    seq_len, width = mixed.shape
    hidden = wu.shape[1]
    depth = slabs.shape[1]
    count = slabs.shape[0]
    ways = hidden // width
    down = width + hidden
    ins = [
        pltpu.make_async_copy(*args, sems.at[i])
        for i, args in enumerate(
            (
                (rest_h.at[:, pl.ds(0, width)], wo),
                (mixed_h, mixed),
                (tok_h, tok),
                (slabs_h.at[:, :, pl.ds(down, hidden)], slabs.at[:, :, pl.ds(down, hidden)]),
                (rest_h.at[:, pl.ds(width, hidden)], wu),
                (cot_h, cot),
            )
        )
    ]
    for c in ins:
        c.start()
    for c in ins[:4]:
        c.wait()

    group = 16 // math.gcd(16, depth * ways)

    @pl.loop(0, count // group)
    def _(i):
        parts = [
            slabs[i * group + j, :, down + k * width : down + (k + 1) * width]
            for j in range(group)
            for k in range(ways)
        ]
        n = group * depth * ways
        wd[pl.ds(pl.multiple_of(i * n, n), n), :] = jnp.concatenate(parts, 0)

    for c in ins[4:]:
        c.wait()
    shift = mod[3:4, :]
    gain = mod[7:8, :]
    scale = 1.0 + mod[4:5, :]
    gate_a = mod[2:3, :]
    gate_m = mod[5:6, :]
    gm[...] = jnp.zeros_like(gm)
    chunk = 512

    @pl.loop(0, seq_len // block)
    def _(r):
        at = pl.ds(pl.multiple_of(r * block, block), block)
        attn_out = dot(mixed[at, :], wo[...], ((1,), (0,)))
        middle = tok[at, :].astype(F32) + gate_a * attn_out
        normal, rstd = normalise(middle)
        normed[at, :] = (normal * (gain * scale) + shift).astype(BF16)

        @pl.loop(0, hidden // chunk)
        def _(c):
            cols = pl.ds(pl.multiple_of(c * chunk, chunk), chunk)
            value, steep = gelu_both(dot(normed[at, :], wu[:, cols], ((1,), (0,))))
            act[at, cols] = value.astype(BF16)
            slope[at, cols] = steep.astype(BF16)

        mlp_out = dot(act[at, :], wd[...], ((1,), (0,)))
        out[at, :] = (middle + gate_m * mlp_out).astype(BF16)
        grad = cot[at, :].astype(F32)
        g_mlp[at, :] = (grad * gate_m).astype(BF16)
        gm[5:6, :] += jnp.sum(grad * mlp_out, 0, keepdims=True)

        @pl.loop(0, hidden // chunk)
        def _(c):
            cols = pl.ds(pl.multiple_of(c * chunk, chunk), chunk)
            g_act = dot(g_mlp[at, :], wd[cols, :], ((1,), (1,)))
            slope[at, cols] = (g_act * slope[at, cols].astype(F32)).astype(BF16)

        e = dot(slope[at, :], wu[...], ((1,), (1,)))
        gm[3:4, :] += jnp.sum(e, 0, keepdims=True)
        weighted = jnp.sum(e * normal, 0, keepdims=True)
        gm[4:5, :] += weighted * gain
        gm[7:8, :] += weighted * scale
        h = e * (gain * scale)
        mean_h = jnp.mean(h, -1, keepdims=True)
        mean_hz = jnp.mean(h * normal, -1, keepdims=True)
        g_mid = grad + (h - mean_h - normal * mean_hz) * rstd
        mid[at, :] = g_mid.astype(BF16)
        gm[2:3, :] += jnp.sum(g_mid * attn_out, 0, keepdims=True)
        g_attn[at, :] = (g_mid * gate_a).astype(BF16)
        g_mixed[at, :] = dot(g_attn[at, :], wo[...], ((1,), (1,))).astype(BF16)

    outs = [
        pltpu.make_async_copy(*args, sems.at[i])
        for i, args in enumerate(((out, out_h), (mid, mid_h), (g_mixed, gmixed_h)))
    ]
    for c in outs:
        c.start()

    def ship(i, col, n):
        part = slabs.at[:, :, pl.ds(col, n)]
        copy = pltpu.make_async_copy(part, grad_h.at[:, :, pl.ds(col, n)], sems.at[i])
        copy.start()
        outs.append(copy)

    tile = 256

    several = math.lcm(128, depth * ways) // (depth * ways)

    @pl.loop(0, count // several)
    def _(i):
        n = several * depth * ways
        at = pl.ds(pl.multiple_of(i * n, n), n)
        g = dot(act[:, at], g_mlp[...], ((0,), (0,)))
        for j in range(several):
            for k in range(ways):
                row = (j * ways + k) * depth
                cols = slice(down + k * width, down + (k + 1) * width)
                slabs[i * several + j, :, cols] = g[row : row + depth].astype(BF16)

    ship(3, down, hidden)

    def weight_grad(left, right, start, n):
        for r in range(seq_len // 256):
            at = pl.ds(r * 256, 256)
            turned[:, at] = jnp.transpose(left[at, :])

        @pl.loop(0, n // tile)
        def _(c):
            col = pl.multiple_of(c * tile, tile)
            g = dot(turned[...], right[:, pl.ds(col, tile)], ((1,), (0,)))
            for i in range(count):
                slabs[i, :, pl.ds(start + col, tile)] = g[
                    i * depth : (i + 1) * depth
                ].astype(BF16)

    weight_grad(normed, slope, width, hidden)
    ship(4, width, hidden)
    weight_grad(mixed, g_attn, 0, width)
    ship(5, 0, width)
    for c in outs:
        c.wait()


def middle_call(mixed, tok, cot, rest, mod, width, hidden):
    seq_len = mixed.shape[0]
    lead, slab = rest.shape[:-2], rest.shape[-2:]
    count = math.prod(lead)
    slabs = rest.reshape((count,) + slab)
    struct = jax.ShapeDtypeStruct
    row = pltpu.VMEM((seq_len, width), BF16)
    full = pltpu.VMEM((seq_len, hidden), BF16)
    res = pl.pallas_call(
        functools.partial(middle_kernel, 512),
        out_shape=[struct((seq_len, width), BF16)] * 3
        + [struct(slabs.shape, BF16), struct(mod.shape, F32)],
        in_specs=[ANY] * 5 + [VMEM],
        out_specs=[ANY] * 4 + [VMEM],
        scratch_shapes=[
            pltpu.VMEM((width, width), BF16),
            pltpu.VMEM((width, hidden), BF16),
            pltpu.VMEM((hidden, width), BF16),
            pltpu.VMEM(slabs.shape, BF16),
            row,
            row,
            row,
            full,
            full,
            row,
            row,
            row,
            pltpu.VMEM((width, seq_len), BF16),
            row,
            row,
            row,
            pltpu.SemaphoreType.DMA((6,)),
        ],
        compiler_params=pltpu.CompilerParams(vmem_limit_bytes=VMEM_LIMIT),
    )(mixed, tok, cot, rest.reshape(width, slab[1]), slabs, mod)
    return (*res[:3], res[3].reshape(rest.shape), res[4])


def split3(x):
    high = x.astype(BF16)
    x = x - high.astype(F32)
    middle = x.astype(BF16)
    low = (x - middle.astype(F32)).astype(BF16)
    return high, middle, low


class GradReduce:
    def __init__(self, grad, own, local, core_in, step_in, z_in, sems, n_dp, n_seq):
        self.grad, self.own, self.local = grad, own, local
        self.core_in, self.step_in, self.z_in = core_in, step_in, z_in
        self.sems, self.n_seq = sems, n_seq
        self.bits = list(range(n_dp.bit_length() - 2, 0, -1))
        self.m = len(self.bits)
        self.orders = (list(range(self.m)), list(range(self.m))[::-1])
        self.cols = core_in.shape[-1] // 2

    def my(self, dim):
        d, _ = place()
        return lax.rem(lax.div(d, 1 << self.bits[dim]), 2)

    def mine(self):
        return tuple(self.my(dim) for dim in range(self.m))

    def index(self, done, flip=None):
        return tuple(
            self.my(dim)
            if dim in done
            else 1 - self.my(dim)
            if dim == flip
            else slice(None)
            for dim in range(self.m)
        )

    def core_copies(self, z):
        d, s = place()
        core = lax.rem(d, 2)
        lead = (slice(None),) * self.m
        send, recv, local = self.sems["core"]
        copies = [
            remote(
                self.grad.at[lead + (1 - core, z)],
                self.core_in.at[lead + (z,)],
                send.at[z],
                recv.at[z],
                xor(d, 1),
                s,
            )
        ]
        if self.local:
            copies.append(
                pltpu.make_async_copy(
                    self.grad.at[lead + (core, z)],
                    self.own(lead, z, slice(None)),
                    local.at[z],
                )
            )
        return copies

    def core_start(self, z):
        for c in self.core_copies(z):
            c.start()

    def core_add(self, z):
        for c in self.core_copies(z):
            c.wait()

        @pl.loop(0, 1 << self.m)
        def _(n):
            lead = tuple(
                lax.rem(lax.div(n, 1 << (self.m - 1 - dim)), 2) for dim in range(self.m)
            )
            target = self.own(lead, z, slice(None))
            target[...] = target[...] + self.core_in[lead + (z,)]

    def step_copy(self, z, h, step):
        d, s = place()
        order = self.orders[h]
        send, recv = self.sems["step"]
        cols = pl.ds(h * self.cols, self.cols)
        return remote(
            self.own(self.index(order[:step], order[step]), z, cols),
            self.step_in[h][step].at[z],
            send.at[z, h, step],
            recv.at[z, h, step],
            xor(d, 1 << self.bits[order[step]]),
            s,
        )

    def z_copy(self, z):
        d, s = place()
        send, recv = self.sems["z"]
        return remote(
            self.own(self.mine(), z, slice(None)),
            self.z_in.at[s],
            send.at[z],
            recv.at[s],
            d,
            z,
        )

    def event(self, z, t):
        for h in range(2):
            if t:
                self.step_copy(z, h, t - 1).wait()
                order = self.orders[h]
                cols = pl.ds(h * self.cols, self.cols)
                free = [dim for dim in range(self.m) if dim not in order[:t]]
                for n in range(1 << len(free)):
                    bits = [(n >> (len(free) - 1 - i)) & 1 for i in range(len(free))]
                    lead = tuple(
                        bits[free.index(dim)] if dim in free else self.my(dim)
                        for dim in range(self.m)
                    )
                    target = self.own(lead, z, cols)
                    target[...] = target[...] + self.step_in[h][t - 1][(z, *bits)]
            if t < self.m:
                self.step_copy(z, h, t).start()
        if t == self.m:
            _, s = place()

            @pl.when(z != s)
            def _():
                self.z_copy(z).start()

    def total(self):
        d, s = place()
        send, recv = self.sems["z"]
        for off in range(1, self.n_seq):
            origin = lax.rem(s + off, self.n_seq)
            remote(
                self.own(self.mine(), s, slice(None)),
                self.z_in.at[origin],
                send.at[origin],
                recv.at[origin],
                d,
                origin,
            ).wait_recv()
        total = self.own(self.mine(), s, slice(None))[...].astype(F32)
        for off in range(1, self.n_seq):
            total += self.z_in[lax.rem(s + off, self.n_seq)].astype(F32)
        return total

    def sent(self):
        _, s = place()
        for z in range(self.n_seq):

            @pl.when(z != s)
            def _():
                self.z_copy(z).wait_send()


def back_kernel(n_dp, n_seq, rows, hidden, *refs):
    grad_rest, out_row, wq_full, packed_h, mixed_h, grad_mixed_h, normed_h = refs[:7]
    lse, docs, cos, sin, tok, grad_mid, mod, gm_in = refs[7:15]
    gq_o, go_o, gu_o, gd_o = refs[15:19]
    out_o, dtok_o, gmod_o = refs[19:22]
    refs = refs[22:]
    m = n_dp.bit_length() - 2
    acc_r, core_r, zin_r = refs[:3]
    step_r = (refs[3 : 3 + m], refs[3 + m : 3 + 2 * m])
    refs = refs[3 + 2 * m :]
    w_in, core_q, zin_q = refs[:3]
    step_q = (refs[3 : 3 + m], refs[3 + m : 3 + 2 * m])
    refs = refs[3 + 2 * m :]
    (
        w,
        qkv,
        normed_t,
        grad_qkv,
        dtok,
        q2,
        k2,
        v2,
        g2,
        dq2,
        gmod,
        qkv_sem,
        w_sem,
        row_send,
        row_recv,
        g_send,
        g_recv,
        gd_send,
        gd_recv,
        c_send,
        c_recv,
        c_local,
        s_send,
        s_recv,
        z_send,
        z_recv,
    ) = refs
    d, s = place()
    length, width = out_row.shape[1:]
    seq_len = length * n_seq
    pairs = width // 128
    first = lax.rem(d, 2)
    mine = s - first
    active = (mine >= 0) & (mine < rows)
    core = lax.rem(d, 2)

    def pair_copies(p, slot):
        return [
            pltpu.make_async_copy(
                packed_h.at[kind * pairs + p], qkv.at[slot, kind], qkv_sem.at[slot, kind]
            )
            for kind in range(3)
        ] + [
            pltpu.make_async_copy(
                src.at[:, pl.ds(pl.multiple_of(p * 128, 128), 128)],
                qkv.at[slot, kind],
                qkv_sem.at[slot, kind],
            )
            for kind, src in ((3, mixed_h), (4, grad_mixed_h))
        ]

    for c in pair_copies(0, 0):
        c.start()
    w_copy = pltpu.make_async_copy(wq_full, w_in, w_sem.at[0])
    w_copy.start()
    normed_copy = pltpu.make_async_copy(normed_h, dtok, w_sem.at[1])
    normed_copy.start()
    greet(n_dp, n_seq)

    def sems(i):
        return {
            "core": (c_send.at[i], c_recv.at[i], c_local.at[i]),
            "step": (s_send.at[i], s_recv.at[i]),
            "z": (z_send.at[i], z_recv.at[i]),
        }

    rest = GradReduce(
        grad_rest,
        lambda lead, z, cols: acc_r.at[tuple(lead) + (z, slice(None), cols)],
        True,
        core_r,
        step_r,
        zin_r,
        sems(0),
        n_dp,
        n_seq,
    )
    stage = w_in
    last = GradReduce(
        stage,
        lambda lead, z, cols: stage.at[tuple(lead) + (core, z, slice(None), cols)],
        False,
        core_q,
        step_q,
        zin_q,
        sems(1),
        n_dp,
        n_seq,
    )
    for z in range(n_seq):
        rest.core_start(z)

    pair = ((out_row, out_o), (dtok, dtok_o))

    def row_local(k):
        src, dst = pair[k]
        return pltpu.make_async_copy(src.at[s], dst.at[mine], row_send.at[k, 0])

    def row_remote(k, off):
        src, dst = pair[k]
        to = lax.rem(s + off, n_seq)
        return remote(
            src.at[to], dst.at[mine], row_send.at[k, off], row_recv.at[k, mine], d, to
        )

    def row_start(k):
        @pl.when(active)
        def _():
            row_local(k).start()
            for off in range(1, n_seq):
                row_remote(k, off).start()

    def row_sent(k):
        @pl.when(active)
        def _():
            row_local(k).wait()
            for off in range(1, n_seq):
                row_remote(k, off).wait_send()

    def row_arrivals(k):
        src, dst = pair[k]
        for i in range(rows):

            @pl.when(first + i != s)
            def _():
                remote(
                    src.at[0],
                    dst.at[i],
                    row_send.at[k, 0],
                    row_recv.at[k, i],
                    d,
                    first + i,
                ).wait_recv()

    row_start(0)

    w_copy.wait()
    depth = w_in.shape[-2]
    lead_dims = w_in.shape[:-2]

    join_slabs(w_in, w)
    normed_copy.wait()
    for r in range(n_seq):
        normed_t[:, pl.ds(r * length, length)] = jnp.transpose(dtok[r])

    rest.core_add(0)
    rest.event(0, 0)
    rest.core_add(1)
    rest.event(1, 0)
    slots = {
        0: [("c", 2), ("c", 3)],
        2: [(0, 1)],
        3: [(2, 0)],
        4: [(1, 1)],
        5: [(0, 2), (3, 0)],
        7: [(2, 1)],
        8: [(1, 2)],
        10: [(3, 1)],
        11: [(2, 2)],
    }
    done = {e for v in slots.values() for e in v} | {(0, 0), (1, 0)}
    block = seq_len // 2
    lane = lax.broadcasted_iota(jnp.int32, (seq_len, 128), 1)

    @pl.loop(0, pairs)
    def _(p):
        now = lax.rem(p, 2)

        @pl.when(p + 1 < pairs)
        def _():
            for c in pair_copies(p + 1, 1 - now):
                c.start()

        for c in pair_copies(p, now):
            c.wait()
        queries, keys, values = qkv[now, 0], qkv[now, 1], qkv[now, 2]
        at_p = pl.ds(pl.multiple_of(p * 128, 128), 128)
        grads = qkv[now, 4]
        product = grads.astype(F32) * qkv[now, 3].astype(F32)
        nothing = jnp.zeros_like(grads)
        for j in range(2):
            own = lanes_of(j, grads.shape)
            base = HEAD_DIM * (1 - j) + 8

            def with_terms(x, other, column):
                for n, term in enumerate(split3(column)):
                    other = jnp.where(lane == base + n, term, other)
                return jnp.where(own, x, other)

            inner = jnp.sum(jnp.where(own, product, 0.0), -1, keepdims=True)
            stat = jnp.sum(jnp.where(lane == 2 * p + j, lse[...], 0.0), -1, keepdims=True)
            g2[j] = with_terms(grads, nothing, -inner)
            q2[j] = with_terms(queries, docs[1], -stat)
            k2[j] = jnp.where(own, keys, docs[0])
            v2[j] = jnp.where(own, values, docs[0])
        for i in range(seq_len // block):
            at = pl.ds(i * block, block)
            dvs, dks = [], []
            for j in range(2):
                probs = jnp.exp2(dot(k2[j, at, :], q2[j], ((1,), (1,))))
                ds = probs * dot(v2[j, at, :], g2[j], ((1,), (1,)))
                ds = ds.astype(BF16)
                dvs.append(dot(probs.astype(BF16), grads, ((1,), (0,))))
                dks.append(dot(ds, queries, ((1,), (0,))))
                dq = dot(ds, qkv[now, 1, at, :], ((0,), (0,)))
                if i == 0:
                    dq2[j] = dq
                else:
                    dq2[j] += dq
            here = lanes_of(0, dvs[0].shape)
            dk = jnp.where(here, dks[0], dks[1]) * (1.0 / LOG2E)
            grad_qkv[at, pl.ds(pl.multiple_of(width + p * 128, 128), 128)] = (
                dk * cos[at, :] + swap_halves(dk * sin[at, :])
            ).astype(BF16)
            grad_qkv[at, pl.ds(pl.multiple_of(2 * width + p * 128, 128), 128)] = jnp.where(
                here, dvs[0], dvs[1]
            ).astype(BF16)
            for slot, events in slots.items():
                if slot % 2 != i:
                    continue

                @pl.when(p == slot // 2)
                def _():
                    for z, t in events:
                        if z == "c":
                            rest.core_add(t)
                        else:
                            rest.event(z, t)

        dq = jnp.where(lanes_of(0, dq2.shape[1:]), dq2[0], dq2[1])
        dq = dq * (1.0 / math.sqrt(HEAD_DIM))
        grad_qkv[:, at_p] = (dq * cos[...] + swap_halves(dq * sin[...])).astype(BF16)

    gain = mod[6:7, :]
    scale = 1.0 + mod[1:2, :]
    gmod[...] = gm_in[...]
    for r in range(n_seq):
        at = pl.ds(r * length, length)
        e = dot(grad_qkv[at, :], w[...], ((1,), (1,)))
        normal, rstd = normalise(tok[at, :].astype(F32))
        gmod[0:1, :] += jnp.sum(e, 0, keepdims=True)
        weighted = jnp.sum(e * normal, 0, keepdims=True)
        gmod[1:2, :] += weighted * gain
        gmod[6:7, :] += weighted * scale
        h = e * (gain * scale)
        mean_h = jnp.mean(h, -1, keepdims=True)
        mean_hz = jnp.mean(h * normal, -1, keepdims=True)
        dtok[r] = (grad_mid[at, :] + (h - mean_h - normal * mean_hz) * rstd).astype(BF16)

    own_row = pltpu.make_async_copy(gmod, gmod_o.at[d, mine], g_send.at[0])

    def group_copy(off):
        return remote(
            gmod,
            gmod_o.at[d, mine],
            g_send.at[off],
            g_recv.at[s],
            d,
            lax.rem(s + off, n_seq),
        )

    @pl.when(active)
    def _():
        own_row.start()
        for off in range(1, n_seq):
            group_copy(off).start()

    row_start(1)

    for c in range(3 * width // 256):
        cols = pl.ds(c * 256, 256)
        g = dot(normed_t[...], grad_qkv[:, cols], ((1,), (0,)))
        for i in range(n_dp * n_seq):
            k, idx = i, []
            for n in lead_dims[::-1]:
                idx.append(k % n)
                k //= n
            stage[tuple(idx[::-1]) + (slice(None), cols)] = g[
                i * depth : (i + 1) * depth
            ].astype(BF16)
    for z in range(n_seq):
        last.core_start(z)
    for z in range(n_seq):
        for t in range(m + 1):
            if (z, t) not in done:
                rest.event(z, t)
    for z in range(n_seq):
        last.core_add(z)
        last.event(z, 0)

    @pl.when(active)
    def _():
        own_row.wait()

    for i in range(rows):
        owner = first + i

        @pl.when(owner != s)
        def _():
            remote(
                gmod, gmod_o.at[d, i], g_send.at[0], g_recv.at[owner], d, owner
            ).wait_recv()

    def dp_copy(off):
        return remote(
            gmod_o.at[d], gmod_o.at[d], gd_send.at[off], gd_recv.at[off], xor(d, off), s
        )

    for off in range(1, n_dp):
        dp_copy(off).start()
    for t in range(1, m + 1):
        for z in range(n_seq):
            last.event(z, t)
    total = rest.total()
    go_o[...] = total[:, :width]
    gu_o[...] = total[:, width : width + hidden]
    for i in range(hidden // width):
        col = width + hidden + i * width
        gd_o[i * depth : (i + 1) * depth, :] = total[:, col : col + width]
    gq_o[...] = last.total()

    for off in range(1, n_dp):
        e = xor(d, off)
        dp_copy(off).wait_send()
        remote(
            gmod_o.at[e], gmod_o.at[e], gd_send.at[off], gd_recv.at[off], e, s
        ).wait_recv()

    @pl.when(active)
    def _():
        for off in range(1, n_seq):
            group_copy(off).wait_send()

    for k in range(2):
        row_sent(k)
        row_arrivals(k)
    rest.sent()
    last.sent()


def back(n_dp, n_seq, rows, hidden, grad_rest, out_row, wq, hbm_args, vmem_args):
    dma = pltpu.SemaphoreType.DMA
    struct = jax.ShapeDtypeStruct
    m = n_dp.bit_length() - 2
    lead = (2,) * m
    length, width = out_row.shape[1:]
    seq_len = length * n_seq
    depth = wq.shape[-2]
    wide = grad_rest.shape[-1]
    gmod = vmem_args[-1]
    outs = [
        struct((depth, 3 * width), F32),
        struct((depth, width), F32),
        struct((depth, hidden), F32),
        struct((depth * hidden // width, width), F32),
        struct((rows, length, width), BF16),
        struct((rows, length, width), BF16),
        struct((n_dp, rows) + gmod.shape, F32),
    ]

    def reduce_scratch(n, acc):
        slabs = [
            pltpu.VMEM(acc + (n_seq, depth, n), BF16),
            pltpu.VMEM(lead + (n_seq, depth, n), BF16),
            pltpu.VMEM((n_seq, depth, n), BF16),
        ]
        for _ in range(2):
            for step in range(m):
                slabs.append(
                    pltpu.VMEM(
                        (n_seq,) + (2,) * (m - 1 - step) + (depth, n // 2), BF16
                    )
                )
        return slabs

    scratch = (
        reduce_scratch(wide, lead)
        + reduce_scratch(3 * width, lead + (2,))
        + [
            pltpu.VMEM((width, 3 * width), BF16),
            pltpu.VMEM((2, 5, seq_len, 128), BF16),
            pltpu.VMEM((width, seq_len), BF16),
            pltpu.VMEM((seq_len, 3 * width), BF16),
            pltpu.VMEM((n_seq, length, width), BF16),
        ]
        + [pltpu.VMEM((2, seq_len, 128), BF16)] * 4
        + [
            pltpu.VMEM((2, seq_len, 128), F32),
            pltpu.VMEM(gmod.shape, F32),
            dma((2, 5)),
            dma((2,)),
            dma((2, n_seq)),
            dma((2, rows)),
            dma((n_seq,)),
            dma((n_seq,)),
            dma((n_dp,)),
            dma((n_dp,)),
            dma((2, n_seq)),
            dma((2, n_seq)),
            dma((2, n_seq)),
            dma((2, n_seq, 2, m)),
            dma((2, n_seq, 2, m)),
            dma((2, n_seq)),
            dma((2, n_seq)),
        ]
    )
    split = lead + (2, n_seq)
    return pl.pallas_call(
        functools.partial(back_kernel, n_dp, n_seq, rows, hidden),
        out_shape=outs,
        in_specs=[ANY] * 7 + [VMEM] * len(vmem_args),
        out_specs=[VMEM] * 4 + [ANY] * 3,
        scratch_shapes=scratch,
        compiler_params=pltpu.CompilerParams(
            collective_id=1, has_side_effects=True, vmem_limit_bytes=VMEM_LIMIT
        ),
    )(
        grad_rest.reshape(split + grad_rest.shape[-2:]),
        out_row,
        wq.reshape(split + wq.shape[-2:]),
        *hbm_args,
        *vmem_args,
    )


def rotary_tables(seq_len):
    half = HEAD_DIM // 2
    freq = np.exp(np.float32(-math.log(10000.0)) * np.arange(half, dtype=np.float32) / np.float32(half))
    angles = np.arange(seq_len, dtype=np.float32)[:, None] * freq.astype(np.float32)[None, :]
    cos = np.tile(np.cos(angles), (1, 4)).astype(np.float32)
    sin = np.sin(angles)
    sin = np.concatenate([-sin, sin, -sin, sin], 1).astype(np.float32)
    return jnp.asarray(cos), jnp.asarray(sin)


def time_embed(step_ids, model_dim):
    half_dim = model_dim // 2
    frequency = jnp.exp(-math.log(10000.0) * jnp.arange(half_dim, dtype=jnp.float32) / half_dim)
    angles = step_ids.astype(jnp.float32)[:, None] * frequency[None, :]
    return jnp.concatenate([jnp.cos(angles), jnp.sin(angles)], axis=-1)


def matmul(a, b, spec):
    return jnp.einsum(spec, a, b, preferred_element_type=F32)


def placed_at(vector, index, length):
    whole = jnp.zeros((length,), F32)
    return lax.dynamic_update_slice(whole, vector.astype(F32), (index * vector.shape[0],))


def shards(
    n_dp,
    n_seq,
    tokens,
    segments,
    timesteps,
    w_mod,
    b_mod,
    gain_attn,
    w_qkv,
    w_out,
    gain_mlp,
    w_up,
    w_down,
    cotangent,
):
    rows, length, width = tokens.shape
    seq_len = length * n_seq
    hidden = w_up.shape[1]
    d, s = place()
    me = d * n_seq + s
    depth = w_mod.shape[0]
    cos, sin = rotary_tables(seq_len)

    steps = lax.all_gather(timesteps, "dp", axis=0, tiled=True)
    embedding = lax.dynamic_slice_in_dim(
        time_embed(steps, width).astype(BF16), me * depth, depth, 1
    )
    part = matmul(embedding, w_mod, "rk,kn->rn") + placed_at(b_mod, me, 6 * width)
    gains = jnp.concatenate(
        [placed_at(gain_attn, me, width), placed_at(gain_mlp, me, width)]
    )
    part = jnp.concatenate([part, jnp.broadcast_to(gains, (part.shape[0], 2 * width))], 1)
    part = part.reshape(n_dp, rows, 8, width)
    seg = jnp.broadcast_to(segments[:, None, :], (rows, 8, length))

    packed_rest = jnp.concatenate(
        [w_out, w_up]
        + [w_down[i * depth : (i + 1) * depth] for i in range(hidden // width)],
        1,
    )
    tok, cot, docs, normed_a, packed, wq, rest, mod, mixed, lse = front(
        n_dp, n_seq, tokens, cotangent, seg, part, (w_qkv, packed_rest), cos, sin
    )
    tok = tok.reshape(seq_len, width)
    cot = cot.reshape(seq_len, width)
    output, grad_mid, grad_mixed, grad_rest, gm_in = middle_call(
        mixed, tok, cot, rest, mod, width, hidden
    )
    g_wqkv, g_wout, g_wup, g_wdown, out, d_tok, gmods = back(
        n_dp,
        n_seq,
        rows,
        hidden,
        grad_rest,
        output.reshape(n_seq, length, width),
        wq,
        (packed, mixed, grad_mixed, normed_a.reshape(n_seq, length, width)),
        (
            lse,
            docs,
            cos,
            sin,
            tok,
            grad_mid,
            mod,
            gm_in,
        ),
    )
    gmods = gmods.reshape(n_dp * rows, 8 * width)
    g_w_mod = jnp.dot(
        embedding.astype(F32).T,
        gmods[:, : 6 * width],
        precision=lax.Precision.HIGHEST,
        preferred_element_type=F32,
    )
    summed = jnp.sum(gmods, 0)

    def own_part(vector, n):
        return lax.dynamic_slice_in_dim(vector, me * n, n, 0)

    return (
        out,
        d_tok,
        g_w_mod,
        own_part(summed[: 6 * width], b_mod.shape[0]),
        own_part(summed[6 * width : 7 * width], gain_attn.shape[0]),
        g_wqkv,
        g_wout,
        own_part(summed[7 * width :], gain_mlp.shape[0]),
        g_wup,
        g_wdown,
    )


def solution(mesh):
    both = P(("dp", "seq"))
    wide = P(("dp", "seq"), None)
    tokens = P("dp", "seq", None)
    return jax.shard_map(
        functools.partial(shards, mesh.shape["dp"], mesh.shape["seq"]),
        mesh=mesh,
        in_specs=(
            tokens,
            P("dp", "seq"),
            P("dp"),
            wide,
            both,
            both,
            wide,
            wide,
            both,
            wide,
            wide,
            tokens,
        ),
        out_specs=(tokens, tokens, wide, both, both, wide, wide, both, wide, wide),
        check_vma=False,
    )
```

```python
import functools
import math

import jax
import jax.numpy as jnp
import numpy as np
from jax import lax
from jax.experimental import pallas as pl
from jax.experimental.pallas import tpu as pltpu
from jax.sharding import PartitionSpec as P

HEAD_DIM = 64
EPSILON = 1e-06
MASK_FILL = -1e30
MESH = pl.DeviceIdType.MESH
BF16 = jnp.bfloat16
F32 = jnp.float32
ANY = pl.BlockSpec(memory_space=pl.ANY)
VMEM = pl.BlockSpec(memory_space=pltpu.VMEM)
VMEM_LIMIT = 60 * 2**20
LOG2E = math.log2(math.e)


def place():
    return lax.axis_index("dp"), lax.axis_index("seq")


def xor(index, bits):
    return jnp.bitwise_xor(index, bits)


def remote(src, dst, send, recv, dp, seq):
    return pltpu.make_async_remote_copy(
        src_ref=src,
        dst_ref=dst,
        send_sem=send,
        recv_sem=recv,
        device_id=(dp, seq),
        device_id_type=MESH,
    )


def greet(n_dp, n_seq):
    d, s = place()
    barrier = pltpu.get_barrier_semaphore()
    for off in range(1, n_dp):
        pl.semaphore_signal(
            barrier, inc=1, device_id=(xor(d, off), s), device_id_type=MESH
        )
    for off in range(1, n_seq):
        pl.semaphore_signal(
            barrier, inc=1, device_id=(d, lax.rem(s + off, n_seq)), device_id_type=MESH
        )
    pl.semaphore_wait(barrier, n_dp - 1 + n_seq - 1)


def bit_orders(n_dp):
    high = [1 << b for b in range(1, n_dp.bit_length() - 1)]
    return (high + [1], high[::-1] + [1])


def signed(value, sign):
    return value if sign > 0 else -value


class WeightGather:
    def __init__(self, shard, at, own_sem, z_sems, x_sems, cols, n_dp, n_seq):
        self.shard, self.at, self.own_sem = shard, at, own_sem
        self.z_sems, self.x_sems = z_sems, x_sems
        self.n_seq = n_seq
        self.cols = cols // 2
        self.orders = bit_orders(n_dp)
        self.steps = len(self.orders[0])
        self.groups = []
        for h in range(2):
            known = [(0, 0)]
            for step, bit in enumerate(self.orders[h]):
                known += [(off ^ bit, step + 1) for off, _ in known]
            self.groups.append(known)

    def own(self):
        d, s = place()
        return pltpu.make_async_copy(self.shard, self.at(d, s), self.own_sem)

    def z_copy(self, way, k):
        d, s = place()
        origin = s - signed(k - 1, way)
        side = 0 if way > 0 else 1
        send, recv = self.z_sems
        return remote(
            self.shard if k == 1 else self.at(d, origin),
            self.at(d, origin),
            send.at[side, k],
            recv.at[side, k],
            d,
            s + way,
        )

    def direct_copy(self, way, k):
        d, s = place()
        side = 0 if way > 0 else 1
        send, recv = self.z_sems
        return remote(
            self.shard,
            self.at(d, s),
            send.at[side, k],
            recv.at[side, k],
            d,
            s + signed(k, way),
        )

    def direct_each(self, body):
        d, s = place()
        for k in range(1, self.n_seq):
            for way in (1, -1):
                to = s + signed(k, way)

                @pl.when((to >= 0) & (to < self.n_seq))
                def _():
                    body(self.direct_copy(way, k))

    def z_valid(self, way, k):
        d, s = place()
        origin = s - signed(k - 1, way)
        to = s + way
        return (origin >= 0) & (origin < self.n_seq) & (to >= 0) & (to < self.n_seq)

    def half(self, ref, h):
        return ref.at[:, pl.ds(h * self.cols, self.cols)]

    def x_copy(self, origin, h, off, bit, src=None):
        d, s = place()
        dst = self.half(self.at(xor(d, off), origin), h)
        send, recv = self.x_sems
        return remote(
            dst if src is None else self.half(src, h),
            dst,
            send.at[origin, h, off ^ bit],
            recv.at[origin, h, off ^ bit],
            xor(d, bit),
            s,
        )

    def each(self, k, body):
        d, s = place()
        if k == 0:
            body(s, 0)
            return
        for way in (1, -1):
            origin = s - signed(k, way)

            @pl.when((origin >= 0) & (origin < self.n_seq))
            def _():
                body(origin, way)

    def z_start(self, k):
        for way in (1, -1):

            @pl.when(self.z_valid(way, k))
            def _():
                self.z_copy(way, k).start()

    def x_start(self, origin, src=None):
        for h in range(2):
            for bit in self.orders[h]:
                self.x_copy(origin, h, 0, bit, src).start()

    def own_start(self):
        d, s = place()
        self.own().start()
        self.x_start(s, self.shard)

    def passing(self, origin, t):
        for h in range(2):
            for off, step in self.groups[h]:
                if step != t:
                    continue
                self.x_copy(origin, h, off, 0).wait_recv()
                for bit in self.orders[h][t:]:
                    self.x_copy(origin, h, off, bit).start()

    def x_sent(self, origin):
        for h in range(2):
            for off, step in self.groups[h]:
                for bit in self.orders[h][step:]:
                    self.x_copy(origin, h, off, bit).wait_send()

    def event(self, k, t, forward=True, across=True):
        if t:
            self.each(k, lambda origin, way: self.passing(origin, t))
            return
        d, s = place()
        send, recv = self.z_sems

        def arrival(origin, way):
            side = 0 if way > 0 else 1
            remote(
                self.shard,
                self.at(d, origin),
                send.at[side, k],
                recv.at[side, k],
                d,
                s,
            ).wait_recv()
            if across:
                self.x_start(origin)

        self.each(k, arrival)
        if forward and k + 1 < self.n_seq:
            self.z_start(k + 1)

    def finish(self, direct=False, across=True):
        if direct:
            self.direct_each(lambda copy: copy.wait_send())
        else:
            for k in range(1, self.n_seq):
                for way in (1, -1):

                    @pl.when(self.z_valid(way, k))
                    def _():
                        self.z_copy(way, k).wait_send()

        if across:
            for k in range(self.n_seq):
                self.each(k, lambda origin, way: self.x_sent(origin))


def dot(a, b, dims):
    return lax.dot_general(a, b, (dims, ((), ())), preferred_element_type=F32)


def swap_halves(x):
    quarter = HEAD_DIM // 2
    lane = lax.broadcasted_iota(jnp.int32, x.shape, 1)
    return jnp.where(
        lax.rem(lane, HEAD_DIM) < quarter,
        pltpu.roll(x, 128 - quarter, axis=1),
        pltpu.roll(x, quarter, axis=1),
    )


def normalise(x):
    mean = jnp.mean(x, -1, keepdims=True)
    centred = x - mean
    var = jnp.mean(centred * centred, -1, keepdims=True)
    rstd = lax.rsqrt(var + EPSILON)
    return centred * rstd, rstd


def join_slabs(slabs, whole):
    depth = slabs.shape[-2]
    count = math.prod(slabs.shape[:-2])
    group = 16 // math.gcd(16, depth)

    @pl.loop(0, count // group)
    def _(i):
        parts = []
        for j in range(group):
            k, idx = i * group + j, []
            for n in slabs.shape[:-2][::-1]:
                idx.append(lax.rem(k, n))
                k = lax.div(k, n)
            parts.append(slabs[tuple(idx[::-1])])
        rows = group * depth
        whole[pl.ds(pl.multiple_of(i * rows, rows), rows), :] = jnp.concatenate(parts, 0)


def lanes_of(j, shape):
    lane = lax.broadcasted_iota(jnp.int32, shape, 1)
    return lax.div(lane, HEAD_DIM) == j


def front_kernel(n_dp, n_seq, rows, *refs):
    tokens, seg, emb_h, *shards = refs[:6]
    w_mod, base, cos, sin = refs[6:10]
    tok_o, doc_o, norm_o, pack_o, *fulls = refs[10:17]
    mod_o, emb, mixed_o, lse_o = refs[17:21]
    (
        tok,
        segs,
        docs,
        normed,
        packed,
        w_in,
        w,
        values,
        keys,
        mod_in,
        mod_sum,
        mod_row,
        out_sem,
        row_send,
        row_recv,
        mod_send,
        mod_recv,
        modz_send,
        modz_recv,
        own_sem,
        z_send,
        z_recv,
        x_send,
        x_recv,
        part,
        emb_send,
        emb_recv,
    ) = refs[21:]
    d, s = place()
    length, width = tokens.shape[1:]
    seq_len = length * n_seq
    first = lax.rem(d, 2)
    mine = s - first
    active = (mine >= 0) & (mine < rows)
    greet(n_dp, n_seq)

    def mod_copy(off):
        return remote(
            part.at[xor(d, off)],
            mod_in.at[d],
            mod_send.at[off],
            mod_recv.at[off],
            xor(d, off),
            s,
        )

    def emb_copy(off):
        return remote(
            emb_h.at[xor(d, off)],
            emb.at[d],
            emb_send.at[off],
            emb_recv.at[off],
            xor(d, off),
            s,
        )

    emb_own = pltpu.make_async_copy(emb_h.at[d], emb.at[d], emb_send.at[0])
    emb_own.start()
    for off in range(1, n_dp):
        emb_copy(off).start()

    ats = [
        lambda e, z: fulls[0].at[e, z],
        lambda e, z: fulls[1].at[e, z],
        lambda e, z: fulls[2].at[z],
    ]
    qkv, rest, down = [
        WeightGather(
            shards[i],
            ats[i],
            own_sem.at[i],
            (z_send.at[i], z_recv.at[i]),
            (x_send.at[i], x_recv.at[i]) if i < 2 else None,
            shards[i].shape[1],
            n_dp,
            n_seq,
        )
        for i in range(3)
    ]
    qkv.direct_each(lambda copy: copy.start())
    rest.z_start(1)
    down.z_start(1)
    down.own().start()
    qkv.own_start()

    emb_own.wait()
    for off in range(1, n_dp):
        e = xor(d, off)
        remote(
            emb_h.at[d], emb.at[e], emb_send.at[off], emb_recv.at[off], d, s
        ).wait_recv()
    features = emb[...].reshape(n_dp * 8, 128)[:, : w_mod.shape[0]].astype(BF16)
    for k in range(8):
        if k < 6:
            terms = dot(features, w_mod[:, k * width : (k + 1) * width], ((1,), (0,)))
            terms = terms + base[k : k + 1, :]
        for e in range(n_dp):
            for i in range(rows):
                part[e, i, k : k + 1, :] = (
                    terms[e * 8 + i : e * 8 + i + 1] if k < 6 else base[k : k + 1, :]
                )
    for off in range(1, n_dp):
        mod_copy(off).start()

    trio = ((tokens, tok), (seg, segs))

    def row_local(k, i):
        src, dst = trio[k]
        return pltpu.make_async_copy(src.at[i], dst.at[s], row_send.at[k, i])

    def row_remote(k, i):
        src, dst = trio[k]
        return remote(
            src.at[i], dst.at[s], row_send.at[k, i], row_recv.at[k, s], d, first + i
        )

    def row_start(k):
        for i in range(rows):

            @pl.when(first + i == s)
            def _():
                row_local(k, i).start()

            @pl.when(first + i != s)
            def _():
                row_remote(k, i).start()

    def row_sent(k):
        for i in range(rows):

            @pl.when(first + i != s)
            def _():
                row_remote(k, i).wait_send()

    def row_arrival(k, origin):
        src, dst = trio[k]
        remote(
            src.at[0],
            dst.at[origin],
            row_send.at[k, 0],
            row_recv.at[k, origin],
            d,
            origin,
        ).wait_recv()

    def row_own(k):
        for i in range(rows):

            @pl.when(first + i == s)
            def _():
                row_local(k, i).wait()

    def mod_exchange():
        for off in range(1, n_dp):
            remote(
                part.at[d],
                mod_in.at[xor(d, off)],
                mod_send.at[off],
                mod_recv.at[off],
                d,
                s,
            ).wait_recv()
        total = part[d]
        for off in range(1, n_dp):
            total += mod_in[xor(d, off)]
        mod_sum[...] = total
        for i in range(rows):

            @pl.when(first + i == s)
            def _():
                mod_row[s] = mod_sum[i]

            @pl.when(first + i != s)
            def _():
                remote(
                    mod_sum.at[i],
                    mod_row.at[s],
                    modz_send.at[i],
                    modz_recv.at[s],
                    d,
                    first + i,
                ).start()

    @pl.when(jnp.logical_not(active))
    def _():
        tok[...] = jnp.zeros_like(tok)
        segs[...] = jnp.zeros_like(segs)

    row_start(1)
    for k in range(1, n_seq):
        qkv.event(k, 0, forward=False)
    mod_exchange()
    row_start(0)
    for k in range(n_seq):
        qkv.event(k, 1)
    rest.own_start()
    rest.event(1, 0)
    down.event(1, 0, across=False)
    for t in range(2, qkv.steps + 1):
        for k in range(n_seq):
            qkv.event(k, t)
    stage = pltpu.make_async_copy(fulls[0], w_in, out_sem.at[0])
    qkv.own().wait()
    stage.start()

    @pl.when(active)
    def _():
        for off in range(1, n_seq):
            row_arrival(1, lax.rem(s + off, n_seq))

    row_own(1)
    lane = lax.broadcasted_iota(jnp.int32, (length, 128), 1)
    lane = lax.rem(lane, HEAD_DIM).astype(F32)
    for z in range(n_seq):
        ids = jnp.transpose(
            jnp.broadcast_to(segs[z, 0:1, :].astype(F32), (128, length))
        )
        same = ids == lane
        at = pl.ds(z * length, length)
        docs[0, at, :] = jnp.where(
            same | ((lane >= 8.0) & (lane < 11.0)), 1.0, 0.0
        ).astype(BF16)
        docs[1, at, :] = jnp.where(same | (lane >= 8.0), 0.0, MASK_FILL).astype(BF16)
    doc_copy = pltpu.make_async_copy(docs, doc_o, out_sem.at[1])
    doc_copy.start()

    stage.wait()
    depth = w_in.shape[2]

    join_slabs(w_in, w)

    @pl.when(active)
    def _():
        for off in range(1, n_seq):
            origin = lax.rem(s + off, n_seq)
            remote(
                mod_sum.at[0],
                mod_row.at[origin],
                modz_send.at[0],
                modz_recv.at[origin],
                d,
                origin,
            ).wait_recv()
        total = mod_row[0]
        for z in range(1, n_seq):
            total += mod_row[z]
        mod_o[...] = total

    @pl.when(jnp.logical_not(active))
    def _():
        mod_o[...] = jnp.zeros_like(mod_o)

    rest.event(0, 1)

    gain = mod_o[6:7, :] * (1.0 + mod_o[1:2, :])
    shift = mod_o[0:1, :]
    row_own(0)
    for off in range(n_seq):
        z = lax.rem(s + off, n_seq)
        if off:

            @pl.when(active)
            def _():
                row_arrival(0, z)

        normal, _ = normalise(tok[z].astype(F32))
        at = pl.ds(pl.multiple_of(z * length, length), length)
        normed[at, :] = (normal * gain + shift).astype(BF16)
    outs = [
        pltpu.make_async_copy(tok, tok_o, out_sem.at[2]),
        pltpu.make_async_copy(normed, norm_o, out_sem.at[3]),
    ]
    for c in outs:
        c.start()

    for kind in range(3):

        @pl.loop(0, width // 256)
        def _(c):
            col = kind * width + c * 256
            wc = w[:, pl.ds(pl.multiple_of(col, 256), 256)]
            for r in range(seq_len // 256):
                at = pl.ds(r * 256, 256)
                y = dot(normed[at, :], wc, ((1,), (0,)))
                for j in range(2):
                    p = y[:, j * 128 : (j + 1) * 128]
                    if kind < 2:
                        p = p * cos[at, :] + swap_halves(p) * sin[at, :]
                    if kind == 0:
                        p = p * (LOG2E / math.sqrt(HEAD_DIM))
                    packed[kind * (width // 128) + c * 2 + j, at, :] = p.astype(BF16)

    pack_copy = pltpu.make_async_copy(packed, pack_o, out_sem.at[4])
    pack_copy.start()
    early = [(0, 2), (1, 1), (0, 3), (2, 0)]
    for e in early:
        rest.event(*e)
    down.event(2, 0, across=False)
    pairs = width // 128
    slots = {
        1: [(1, 2)],
        2: [(3, 0), (2, 1), (1, 3)],
        4: [(2, 2)],
        5: [(3, 1)],
    }
    done = {e for v in slots.values() for e in v}
    done |= set(early) | {(1, 0), (0, 1)}

    values[:, 128:] = jnp.ones((seq_len, 128), BF16)
    block = 128
    lse_o[...] = jnp.zeros_like(lse_o)

    @pl.loop(0, pairs)
    def _(p):
        k = packed[pairs + p]
        values[:, :128] = packed[2 * pairs + p]
        for j in range(2):
            keys[j] = jnp.where(lanes_of(j, k.shape), k, docs[0])
        for i in range(seq_len // block):
            at = pl.ds(i * block, block)
            q = packed[p, at, :]
            both = []
            stats = lse_o[at, :]
            lane = lax.broadcasted_iota(jnp.int32, (block, 128), 1)
            for j in range(2):
                own = lanes_of(j, q.shape)
                scores = dot(jnp.where(own, q, docs[1, at, :]), keys[j], ((1,), (1,)))
                top = jnp.max(scores, -1, keepdims=True)
                e = jnp.exp2(scores - top).astype(BF16)
                o = dot(e, values[...], ((1,), (0,)))
                total = o[:, 128:]
                both.append(o[:, :128] / total)
                stats = jnp.where(lane == 2 * p + j, top + jnp.log2(total), stats)
            lse_o[at, :] = stats
            mixed_o[at, pl.ds(pl.multiple_of(p * 128, 128), 128)] = jnp.where(
                lane < HEAD_DIM, both[0], both[1]
            ).astype(BF16)
        for slot, events in slots.items():

            @pl.when(p == slot)
            def _():
                for k, t in events:
                    rest.event(k, t)
                    if (k, t) == (3, 0):
                        down.event(3, 0, across=False)

    for t in range(1, rest.steps + 1):
        for k in range(n_seq):
            if (k, t) not in done:
                rest.event(k, t)

    for i in range(rows):

        @pl.when(first + i != s)
        def _():
            remote(
                mod_sum.at[i], mod_row.at[s], modz_send.at[i], modz_recv.at[s], d, first + i
            ).wait_send()

    for off in range(1, n_dp):
        mod_copy(off).wait_send()
    rest.own().wait()
    down.own().wait()
    for c in outs + [doc_copy, pack_copy]:
        c.wait()

    for k in range(2):
        row_sent(k)
    for off in range(1, n_dp):
        emb_copy(off).wait_send()
    qkv.finish(direct=True)
    rest.finish()
    down.finish(across=False)


def front(n_dp, n_seq, tokens, seg, emb, shards, w_mod, base, cos, sin):
    rows, length, width = tokens.shape
    seq_len = length * n_seq
    dma = pltpu.SemaphoreType.DMA
    struct = jax.ShapeDtypeStruct
    pairs = width // 128
    outs = [
        struct((n_seq, length, width), BF16),
        struct((2, seq_len, 128), BF16),
        struct((seq_len, width), BF16),
        struct((3 * pairs, seq_len, 128), BF16),
    ]
    outs += [struct((n_dp, n_seq) + w.shape, BF16) for w in shards[:2]]
    outs += [
        struct((n_seq,) + shards[2].shape, BF16),
        struct((8, width), F32),
        struct(emb.shape, F32),
        struct((seq_len, width), BF16),
        struct((seq_len, 128), F32),
    ]
    return pl.pallas_call(
        functools.partial(front_kernel, n_dp, n_seq, rows),
        out_shape=outs,
        in_specs=[ANY] * 6 + [VMEM] * 4,
        out_specs=[ANY] * 7 + [VMEM] * 4,
        scratch_shapes=[
            pltpu.VMEM((n_seq, length, width), BF16),
            pltpu.VMEM((n_seq,) + seg.shape[1:], jnp.int32),
            pltpu.VMEM((2, seq_len, 128), BF16),
            pltpu.VMEM((seq_len, width), BF16),
            pltpu.VMEM((3 * pairs, seq_len, 128), BF16),
            pltpu.VMEM((n_dp, n_seq) + shards[0].shape, BF16),
            pltpu.VMEM((width, 3 * width), BF16),
            pltpu.VMEM((seq_len, 256), BF16),
            pltpu.VMEM((2, seq_len, 128), BF16),
            pltpu.VMEM((n_dp, rows, 8, width), F32),
            pltpu.VMEM((rows, 8, width), F32),
            pltpu.VMEM((n_seq, 8, width), F32),
            dma((5,)),
            dma((2, rows)),
            dma((2, n_seq)),
            dma((n_dp,)),
            dma((n_dp,)),
            dma((rows,)),
            dma((n_seq,)),
            dma((3,)),
            dma((3, 2, n_seq)),
            dma((3, 2, n_seq)),
            dma((2, n_seq, 2, n_dp)),
            dma((2, n_seq, 2, n_dp)),
            pltpu.VMEM((n_dp, rows, 8, width), F32),
            dma((n_dp,)),
            dma((n_dp,)),
        ],
        compiler_params=pltpu.CompilerParams(
            collective_id=0, has_side_effects=True, vmem_limit_bytes=VMEM_LIMIT
        ),
    )(tokens, seg, emb, *shards, w_mod, base, cos, sin)


class GradReduce:
    def __init__(self, grad, own, local, core_in, step_in, z_in, sems, n_dp, n_seq):
        self.grad, self.own, self.local = grad, own, local
        self.core_in, self.step_in, self.z_in = core_in, step_in, z_in
        self.sems, self.n_seq = sems, n_seq
        self.bits = list(range(n_dp.bit_length() - 2, 0, -1))
        self.m = len(self.bits)
        self.orders = (list(range(self.m)), list(range(self.m))[::-1])
        self.cols = core_in.shape[-1] // 2

    def my(self, dim):
        d, _ = place()
        return lax.rem(lax.div(d, 1 << self.bits[dim]), 2)

    def mine(self):
        return tuple(self.my(dim) for dim in range(self.m))

    def index(self, done, flip=None):
        return tuple(
            self.my(dim)
            if dim in done
            else 1 - self.my(dim)
            if dim == flip
            else slice(None)
            for dim in range(self.m)
        )

    def core_copies(self, z):
        d, s = place()
        core = lax.rem(d, 2)
        lead = (slice(None),) * self.m
        send, recv, local = self.sems["core"]
        copies = [
            remote(
                self.grad.at[lead + (1 - core, z)],
                self.core_in.at[lead + (z,)],
                send.at[z],
                recv.at[z],
                xor(d, 1),
                s,
            )
        ]
        if self.local:
            copies.append(
                pltpu.make_async_copy(
                    self.grad.at[lead + (core, z)],
                    self.own(lead, z, slice(None)),
                    local.at[z],
                )
            )
        return copies

    def core_start(self, z):
        for c in self.core_copies(z):
            c.start()

    def core_add(self, z):
        for c in self.core_copies(z):
            c.wait()

        @pl.loop(0, 1 << self.m)
        def _(n):
            lead = tuple(
                lax.rem(lax.div(n, 1 << (self.m - 1 - dim)), 2) for dim in range(self.m)
            )
            target = self.own(lead, z, slice(None))
            target[...] = target[...] + self.core_in[lead + (z,)]

    def step_copy(self, z, h, step):
        d, s = place()
        order = self.orders[h]
        send, recv = self.sems["step"]
        cols = pl.ds(h * self.cols, self.cols)
        return remote(
            self.own(self.index(order[:step], order[step]), z, cols),
            self.step_in[h][step].at[z],
            send.at[z, h, step],
            recv.at[z, h, step],
            xor(d, 1 << self.bits[order[step]]),
            s,
        )

    def mine_at(self, z):
        return self.own(self.mine(), z, slice(None))

    def z_copy(self, z):
        d, s = place()
        send, recv = self.sems["z"]
        return remote(self.mine_at(z), self.z_in.at[s], send.at[z], recv.at[s], d, z)

    def event(self, z, t):
        for h in range(2):
            if t:
                self.step_copy(z, h, t - 1).wait()
                order = self.orders[h]
                cols = pl.ds(h * self.cols, self.cols)
                free = [dim for dim in range(self.m) if dim not in order[:t]]
                for n in range(1 << len(free)):
                    bits = [(n >> (len(free) - 1 - i)) & 1 for i in range(len(free))]
                    lead = tuple(
                        bits[free.index(dim)] if dim in free else self.my(dim)
                        for dim in range(self.m)
                    )
                    target = self.own(lead, z, cols)
                    target[...] = target[...] + self.step_in[h][t - 1][(z, *bits)]
            if t < self.m:
                self.step_copy(z, h, t).start()
        if t == self.m and self.z_in is not None:
            _, s = place()

            @pl.when(z != s)
            def _():
                self.z_copy(z).start()

    def total(self):
        d, s = place()
        send, recv = self.sems["z"]
        for off in range(1, self.n_seq):
            origin = lax.rem(s + off, self.n_seq)
            remote(
                self.mine_at(s),
                self.z_in.at[origin],
                send.at[origin],
                recv.at[origin],
                d,
                origin,
            ).wait_recv()
        total = self.mine_at(s)[...].astype(F32)
        for off in range(1, self.n_seq):
            total += self.z_in[lax.rem(s + off, self.n_seq)].astype(F32)
        return total

    def sent(self):
        _, s = place()
        for z in range(self.n_seq):

            @pl.when(z != s)
            def _():
                self.z_copy(z).wait_send()


def spread(k, dims):
    idx = []
    for n in dims[::-1]:
        idx.append(k % n if isinstance(k, int) else lax.rem(k, n))
        k = k // n if isinstance(k, int) else lax.div(k, n)
    return tuple(idx[::-1])


GELU_A = math.sqrt(2.0 / math.pi)
GELU_B = 0.044715 * GELU_A


def gelu_both(u):
    square = u * u
    half = 0.5 * jnp.tanh(u * (GELU_B * square + GELU_A)) + 0.5
    value = u * half
    slope = half + value * (1.0 - half) * (6.0 * GELU_B * square + 2.0 * GELU_A)
    return value, slope


class RowReturn:
    def __init__(self, src, dst, send, recv, rows, n_seq):
        self.src, self.dst, self.send, self.recv = src, dst, send, recv
        self.rows, self.n_seq = rows, n_seq
        d, s = place()
        self.first = lax.rem(d, 2)
        self.mine = s - self.first
        self.active = (self.mine >= 0) & (self.mine < rows)

    def local(self):
        _, s = place()
        return pltpu.make_async_copy(
            self.src.at[s], self.dst.at[self.mine], self.send.at[0]
        )

    def remote(self, off):
        d, s = place()
        to = lax.rem(s + off, self.n_seq)
        return remote(
            self.src.at[to],
            self.dst.at[self.mine],
            self.send.at[off],
            self.recv.at[self.mine],
            d,
            to,
        )

    def start(self):
        @pl.when(self.active)
        def _():
            self.local().start()
            for off in range(1, self.n_seq):
                self.remote(off).start()

    def finish(self):
        d, s = place()

        @pl.when(self.active)
        def _():
            self.local().wait()
            for off in range(1, self.n_seq):
                self.remote(off).wait_send()

        for i in range(self.rows):

            @pl.when(self.first + i != s)
            def _():
                remote(
                    self.src.at[0],
                    self.dst.at[i],
                    self.send.at[0],
                    self.recv.at[i],
                    d,
                    self.first + i,
                ).wait_recv()


def middle_kernel(n_dp, n_seq, *refs):
    mixed_h, tok_h, cot_h, rest_h, group_h, mod = refs[:6]
    out_o, mid_h, gmixed_h, grad_h, down_h, gm = refs[6:12]
    m = n_dp.bit_length() - 2
    (
        wo,
        wu,
        wd,
        slabs,
        mixed,
        tok,
        cot,
        act,
        slope,
        normed,
        g_mlp,
        g_attn,
        turned,
        out,
        attn,
        mlp,
        sems,
        cot_send,
        cot_recv,
        row_send,
        row_recv,
        c_send,
        c_recv,
        s_send,
        s_recv,
        tiles,
        tile_sem,
        x_send,
        x_recv,
        own_sem,
        core_in,
        *steps,
    ) = refs[12:]
    d, s = place()
    rows = cot_h.shape[0]
    length = cot_h.shape[1]
    seq_len, width = mixed.shape
    hidden = wu.shape[1]
    depth = slabs.shape[-2]
    lead = slabs.shape[:-2]
    count = math.prod(lead)
    everything = (slice(None),) * len(lead)
    ways = hidden // width
    down = width + hidden
    first = lax.rem(d, 2)
    mine = s - first
    active = (mine >= 0) & (mine < rows)
    ins = [
        pltpu.make_async_copy(*args, sems.at[i])
        for i, args in enumerate(
            (
                (rest_h.at[:, pl.ds(0, width)], wo),
                (mixed_h, mixed),
                (tok_h, tok),
                (rest_h.at[:, pl.ds(width, hidden)], wu),
            )
        )
    ]
    for c in ins:
        c.start()
    greet(n_dp, n_seq)
    core = lax.rem(d, 2)
    sums = GradReduce(
        slabs,
        lambda idx, z, cols: slabs.at[tuple(idx) + (core, z, slice(None), cols)],
        False,
        core_in,
        (steps[:m], steps[m:]),
        None,
        {"core": (c_send, c_recv, None), "step": (s_send, s_recv)},
        n_dp,
        n_seq,
    )

    def slab_at(e, z):
        bits = [lax.rem(lax.div(e, 1 << b), 2) for b in range(len(lead) - 1)]
        return slabs.at[tuple(bits[::-1]) + (z,)]

    gather = WeightGather(
        None, slab_at, None, None, (x_send, x_recv), hidden, n_dp, n_seq
    )
    group_own = [
        pltpu.make_async_copy(group_h.at[z], slab_at(d, z), own_sem.at[z])
        for z in range(n_seq)
    ]
    for z in range(n_seq):
        gather.x_start(z, group_h.at[z])
        group_own[z].start()

    def cot_remote(i):
        return remote(
            cot_h.at[i], cot.at[s], cot_send.at[i], cot_recv.at[s], d, first + i
        )

    def cot_local(i):
        return pltpu.make_async_copy(cot_h.at[i], cot.at[s], cot_send.at[i])

    def cot_each(near, far):
        for i in range(rows):
            pl.when(first + i == s)(functools.partial(near, i))
            pl.when(first + i != s)(functools.partial(far, i))

    cot_each(lambda i: cot_local(i).start(), lambda i: cot_remote(i).start())

    @pl.when(jnp.logical_not(active))
    def _():
        cot[...] = jnp.zeros_like(cot)

    for c in ins:
        c.wait()

    shift = mod[3:4, :]
    gain = mod[7:8, :]
    scale = 1.0 + mod[4:5, :]
    gate_a = mod[2:3, :]
    gate_m = mod[5:6, :]
    gm[...] = jnp.zeros_like(gm)
    chunk = 512
    block = 2 * length
    blocks = [(pl.ds(r * block, block), pl.ds(r * 2, 2)) for r in range(n_seq // 2)]
    three = (2, length, width)

    def middle_of(at):
        return tok[at, :].astype(F32) + gate_a * attn[at, :]

    half = n_seq // 2
    gather_events = [[(z, 1) for z in range(half)], [(z, 1) for z in range(half, n_seq)]]
    gather_events += [
        [(z, t) for z in range(n_seq)] for t in range(2, gather.steps + 1)
    ]
    for at, _ in blocks:
        attn[at, :] = dot(mixed[at, :], wo[...], ((1,), (0,)))
        normal, _ = normalise(middle_of(at))
        normed[at, :] = (normal * (gain * scale) + shift).astype(BF16)

        @pl.loop(0, hidden // chunk)
        def _(c):
            cols = pl.ds(pl.multiple_of(c * chunk, chunk), chunk)
            value, steep = gelu_both(dot(normed[at, :], wu[:, cols], ((1,), (0,))))
            act[at, cols] = value.astype(BF16)
            slope[at, cols] = steep.astype(BF16)

        if gather_events:
            for z, t in gather_events.pop(0):
                gather.passing(z, t)

    for events in gather_events:
        for z, t in events:
            gather.passing(z, t)
    for z in range(n_seq):
        gather.x_sent(z)
        group_own[z].wait()
    group = 16 // math.gcd(16, depth * ways)

    @pl.loop(0, count // group)
    def _(i):
        parts = [
            slabs[spread(i * group + j, lead) + (slice(None), pl.ds(k * width, width))]
            for j in range(group)
            for k in range(ways)
        ]
        n = group * depth * ways
        wd[pl.ds(pl.multiple_of(i * n, n), n), :] = jnp.concatenate(parts, 0)

    for at, two in blocks:
        mlp_out = dot(act[at, :], wd[...], ((1,), (0,)))
        mlp[at, :] = mlp_out.astype(BF16)
        out[two] = (middle_of(at) + gate_m * mlp_out).astype(BF16).reshape(three)
    returned = RowReturn(out, out_o, row_send, row_recv, rows, n_seq)

    cot_each(lambda i: cot_local(i).wait(), lambda i: None)

    @pl.when(active)
    def _():
        for off in range(1, n_seq):
            origin = lax.rem(s + off, n_seq)
            remote(
                cot_h.at[0],
                cot.at[origin],
                cot_send.at[0],
                cot_recv.at[origin],
                d,
                origin,
            ).wait_recv()

    for at, two in blocks:
        grad = cot[two].reshape(block, width).astype(F32)
        g_mlp[at, :] = (grad * gate_m).astype(BF16)
        gm[5:6, :] += jnp.sum(grad * mlp[at, :].astype(F32), 0, keepdims=True)

    several = math.lcm(128, depth * ways) // (depth * ways)

    @pl.loop(0, count // several)
    def _(i):
        n = several * depth * ways
        at = pl.ds(pl.multiple_of(i * n, n), n)
        g = dot(act[:, at], g_mlp[...], ((0,), (0,)))
        for j in range(several):
            for k in range(ways):
                row = (j * ways + k) * depth
                slabs[
                    spread(i * several + j, lead) + (slice(None), pl.ds(k * width, width))
                ] = g[row : row + depth].astype(BF16)

    returned.start()
    for z in range(n_seq):
        sums.core_start(z)
    todo = [[("add", z) for z in range(n_seq)] + [(z, 0) for z in range(n_seq)]]
    todo += [[(z, t) for z in range(n_seq)] for t in range(1, m + 1)]

    def proceed():
        for z, t in todo.pop(0) if todo else []:
            if z == "add":
                sums.core_add(t)
            else:
                sums.event(z, t)

    for at, two in blocks:
        grad = cot[two].reshape(block, width).astype(F32)

        @pl.loop(0, hidden // chunk)
        def _(c):
            cols = pl.ds(pl.multiple_of(c * chunk, chunk), chunk)
            g_act = dot(g_mlp[at, :], wd[cols, :], ((1,), (1,)))
            slope[at, cols] = (g_act * slope[at, cols].astype(F32)).astype(BF16)

        e = dot(slope[at, :], wu[...], ((1,), (1,)))
        gm[3:4, :] += jnp.sum(e, 0, keepdims=True)
        normal, rstd = normalise(middle_of(at))
        weighted = jnp.sum(e * normal, 0, keepdims=True)
        gm[4:5, :] += weighted * gain
        gm[7:8, :] += weighted * scale
        h = e * (gain * scale)
        mean_h = jnp.mean(h, -1, keepdims=True)
        mean_hz = jnp.mean(h * normal, -1, keepdims=True)
        g_mid = grad + (h - mean_h - normal * mean_hz) * rstd
        mlp[at, :] = g_mid.astype(BF16)
        gm[2:3, :] += jnp.sum(g_mid * attn[at, :], 0, keepdims=True)
        g_attn[at, :] = (g_mid * gate_a).astype(BF16)
        g_mixed = dot(g_attn[at, :], wo[...], ((1,), (1,)))
        cot[two] = g_mixed.astype(BF16).reshape(three)
        proceed()

    outs = [
        pltpu.make_async_copy(*args, sems.at[i])
        for i, args in enumerate(((mlp, mid_h), (cot, gmixed_h)))
    ]
    for c in outs:
        c.start()

    tile = 256

    def tile_copy(slot, col):
        return pltpu.make_async_copy(
            tiles.at[slot],
            grad_h.at[everything + (slice(None), pl.ds(col, tile))],
            tile_sem.at[slot],
        )

    def weight_grad(left, right, start, n, busy):
        for r in range(seq_len // 256):
            at = pl.ds(r * 256, 256)
            turned[:, at] = jnp.transpose(left[at, :])

        @pl.loop(0, n // tile)
        def _(c):
            col = pl.multiple_of(c * tile, tile)
            slot = lax.rem(c, 2)
            g = dot(turned[...], right[:, pl.ds(col, tile)], ((1,), (0,)))

            @pl.when((c >= 2) | busy)
            def _():
                tile_copy(slot, 0).wait()

            for i in range(count):
                tiles[(slot,) + spread(i, lead)] = g[
                    i * depth : (i + 1) * depth
                ].astype(BF16)
            tile_copy(slot, pl.multiple_of(start + col, tile)).start()

    weight_grad(normed, slope, width, hidden, False)
    proceed()
    weight_grad(mixed, g_attn, 0, width, True)
    while todo:
        proceed()
    reduced = []
    for z in range(n_seq):
        reduced.append(
            pltpu.make_async_copy(sums.mine_at(z), down_h.at[z], c_send.at[z])
        )
        reduced[-1].start()
    for slot in range(2):
        tile_copy(slot, 0).wait()
    for c in outs + reduced:
        c.wait()
    cot_each(lambda i: None, lambda i: cot_remote(i).wait_send())
    returned.finish()


def middle_call(n_dp, n_seq, mixed, tok, cot, rest, group, mod, width, hidden):
    seq_len = mixed.shape[0]
    rows, length = cot.shape[:2]
    depth, wide = rest.shape[-2:]
    m = n_dp.bit_length() - 2
    lead = (2,) * m
    split = lead + (2, n_seq)
    struct = jax.ShapeDtypeStruct
    dma = pltpu.SemaphoreType.DMA
    row = pltpu.VMEM((seq_len, width), BF16)
    cut = pltpu.VMEM((n_seq, length, width), BF16)
    full = pltpu.VMEM((seq_len, hidden), BF16)
    steps = [
        pltpu.VMEM((n_seq,) + (2,) * (m - 1 - step) + (depth, hidden // 2), BF16)
        for _ in range(2)
        for step in range(m)
    ]
    out, mid, g_mixed, grads, down, gm = pl.pallas_call(
        functools.partial(middle_kernel, n_dp, n_seq),
        out_shape=[
            struct(cot.shape, BF16),
            struct((seq_len, width), BF16),
            struct((n_seq, length, width), BF16),
            struct(split + (depth, width + hidden), BF16),
            struct((n_seq, depth, hidden), BF16),
            struct(mod.shape, F32),
        ],
        in_specs=[ANY] * 5 + [VMEM],
        out_specs=[ANY] * 5 + [VMEM],
        scratch_shapes=[
            pltpu.VMEM((width, width), BF16),
            pltpu.VMEM((width, hidden), BF16),
            pltpu.VMEM((hidden, width), BF16),
            pltpu.VMEM(split + (depth, hidden), BF16),
            row,
            row,
            cut,
            full,
            full,
            row,
            row,
            row,
            pltpu.VMEM((width, seq_len), BF16),
            cut,
            pltpu.VMEM((seq_len, width), F32),
            row,
            dma((6,)),
            dma((rows,)),
            dma((n_seq,)),
            dma((n_seq,)),
            dma((rows,)),
            dma((n_seq,)),
            dma((n_seq,)),
            dma((n_seq, 2, m)),
            dma((n_seq, 2, m)),
            pltpu.VMEM((2,) + split + (depth, 256), BF16),
            dma((2,)),
            dma((n_seq, 2, n_dp)),
            dma((n_seq, 2, n_dp)),
            dma((n_seq,)),
            pltpu.VMEM(lead + (n_seq, depth, hidden), BF16),
            *steps,
        ],
        compiler_params=pltpu.CompilerParams(
            collective_id=2, has_side_effects=True, vmem_limit_bytes=VMEM_LIMIT
        ),
    )(
        mixed,
        tok,
        cot,
        rest.reshape(width, wide),
        group,
        mod,
    )
    return out, mid, g_mixed.reshape(seq_len, width), grads, down, gm


def split3(x):
    high = x.astype(BF16)
    x = x - high.astype(F32)
    middle = x.astype(BF16)
    low = (x - middle.astype(F32)).astype(BF16)
    return high, middle, low


def back_kernel(n_dp, n_seq, rows, hidden, *refs):
    grad_rest, down_h, wq_h, packed_h, mixed_h, grad_mixed_h, normed_h = refs[:7]
    lse, docs, cos, sin, tok, grad_mid, mod, gm_in = refs[7:15]
    gq_o, go_o, gu_o, gd_o = refs[15:19]
    dtok_o, gmod_o = refs[19:21]
    refs = refs[21:]
    m = n_dp.bit_length() - 2
    chunks = 3
    sets = []
    for _ in range(1 + chunks):
        acc, core_in, z_in = refs[:3]
        steps = (refs[3 : 3 + m], refs[3 + m : 3 + 2 * m])
        sets.append((acc, core_in, steps, z_in))
        refs = refs[3 + 2 * m :]
    (
        down_in,
        w,
        qkv,
        normed_t,
        grad_qkv,
        dtok,
        q2,
        k2,
        v2,
        g2,
        dq2,
        gmod,
        qkv_sem,
        w_sem,
        row_send,
        row_recv,
        g_send,
        g_recv,
        gd_send,
        gd_recv,
        c_send,
        c_recv,
        c_local,
        s_send,
        s_recv,
        z_send,
        z_recv,
        down_send,
        down_recv,
    ) = refs
    d, s = place()
    length, width = dtok.shape[1:]
    depth = gq_o.shape[0]
    seq_len = length * n_seq
    pairs = width // 128
    first = lax.rem(d, 2)
    mine = s - first
    active = (mine >= 0) & (mine < rows)
    core = lax.rem(d, 2)

    def pair_copies(p, slot):
        return [
            pltpu.make_async_copy(
                packed_h.at[kind * pairs + p], qkv.at[slot, kind], qkv_sem.at[slot, kind]
            )
            for kind in range(3)
        ] + [
            pltpu.make_async_copy(
                src.at[:, pl.ds(pl.multiple_of(p * 128, 128), 128)],
                qkv.at[slot, kind],
                qkv_sem.at[slot, kind],
            )
            for kind, src in ((3, mixed_h), (4, grad_mixed_h))
        ]

    for c in pair_copies(0, 0):
        c.start()
    normed_copy = pltpu.make_async_copy(normed_h, dtok, w_sem.at[1])
    normed_copy.start()
    greet(n_dp, n_seq)

    def reducer(i, grad, own, local):
        acc, core_in, steps, z_in = sets[i]
        sems = {
            "core": (c_send.at[i], c_recv.at[i], c_local.at[i]),
            "step": (s_send.at[i], s_recv.at[i]),
            "z": (z_send.at[i], z_recv.at[i]),
        }
        return GradReduce(grad, own, local, core_in, steps, z_in, sems, n_dp, n_seq)

    acc_r = sets[0][0]
    rest = reducer(
        0,
        grad_rest,
        lambda lead, z, cols: acc_r.at[tuple(lead) + (z, slice(None), cols)],
        True,
    )

    def chunk_reducer(c):
        stage = sets[1 + c][0]
        return reducer(
            1 + c,
            stage,
            lambda lead, z, cols: stage.at[tuple(lead) + (core, z, slice(None), cols)],
            False,
        )

    parts = [chunk_reducer(c) for c in range(chunks)]
    order = [0, n_seq - 1] + list(range(1, n_seq - 1))
    for z in order:
        rest.core_start(z)

    def down_copy(z):
        return remote(
            down_h.at[z], down_in.at[s], down_send.at[z], down_recv.at[s], d, z
        )

    down_own = pltpu.make_async_copy(down_h.at[s], down_in.at[s], down_send.at[s])
    down_own.start()
    for z in range(n_seq):

        @pl.when(z != s)
        def _():
            down_copy(z).start()

    w_copy = pltpu.make_async_copy(wq_h, w, w_sem.at[0])
    w_copy.start()
    returned = RowReturn(dtok, dtok_o, row_send, row_recv, rows, n_seq)

    normed_copy.wait()
    for r in range(n_seq):
        normed_t[:, pl.ds(r * length, length)] = jnp.transpose(dtok[r])

    def weight_chunk(c):
        stage = sets[1 + c][0]
        n = width // chunks
        lead = stage.shape[:-2]
        for kind in range(3):
            g = dot(
                normed_t[...],
                grad_qkv[:, kind * width + c * n : kind * width + (c + 1) * n],
                ((1,), (0,)),
            )
            for i in range(n_dp * n_seq):
                k, idx = i, []
                for size in lead[::-1]:
                    idx.append(k % size)
                    k //= size
                stage[tuple(idx[::-1]) + (slice(None), pl.ds(kind * n, n))] = g[
                    i * depth : (i + 1) * depth
                ].astype(BF16)
        for z in range(n_seq):
            parts[c].core_start(z)

    def chunk_event(c, t):
        for z in range(n_seq):
            if t == 0:
                parts[c].core_add(z)
            parts[c].event(z, t)

    def run(what, *args):
        if what == "add":
            rest.core_add(order[args[0]])
        elif what == "rest":
            rest.event(order[args[0]], args[1])
        elif what == "grad":
            weight_chunk(*args)
        else:
            chunk_event(*args)

    run("add", 0)
    run("rest", 0, 0)
    run("add", 1)
    run("rest", 1, 0)
    slots = {
        0: [("add", 2), ("add", 3)],
        1: [("rest", 0, 1), ("rest", 2, 0)],
        2: [("rest", 1, 1), ("rest", 3, 0)],
        3: [("rest", 0, 2), ("grad", 0)],
        4: [("rest", 2, 1), ("rest", 1, 2), ("chunk", 0, 0)],
        5: [("rest", 3, 1)],
        6: [("rest", 2, 2), ("chunk", 0, 1)],
        7: [("rest", 3, 2), ("grad", 1)],
        8: [("chunk", 0, 2), ("chunk", 1, 0)],
        10: [("chunk", 1, 1)],
        11: [("chunk", 1, 2), ("grad", 2)],
    }
    tail = [[("chunk", 2, 0)], [], [("chunk", 2, 1)], []]
    block = seq_len // 2
    lane = lax.broadcasted_iota(jnp.int32, (seq_len, 128), 1)
    if m != 2:
        slots, tail = {3: [("grad", 0)], 7: [("grad", 1)], 11: [("grad", 2)]}, []

    @pl.loop(0, pairs)
    def _(p):
        now = lax.rem(p, 2)

        @pl.when(p + 1 < pairs)
        def _():
            for c in pair_copies(p + 1, 1 - now):
                c.start()

        for c in pair_copies(p, now):
            c.wait()
        queries, keys, values = qkv[now, 0], qkv[now, 1], qkv[now, 2]
        at_p = pl.ds(pl.multiple_of(p * 128, 128), 128)
        grads = qkv[now, 4]
        product = grads.astype(F32) * qkv[now, 3].astype(F32)
        nothing = jnp.zeros_like(grads)
        for j in range(2):
            own = lanes_of(j, grads.shape)
            base = HEAD_DIM * (1 - j) + 8

            def with_terms(x, other, column):
                for n, term in enumerate(split3(column)):
                    other = jnp.where(lane == base + n, term, other)
                return jnp.where(own, x, other)

            inner = jnp.sum(jnp.where(own, product, 0.0), -1, keepdims=True)
            stat = jnp.sum(jnp.where(lane == 2 * p + j, lse[...], 0.0), -1, keepdims=True)
            g2[j] = with_terms(grads, nothing, -inner)
            q2[j] = with_terms(queries, docs[1], -stat)
            k2[j] = jnp.where(own, keys, docs[0])
            v2[j] = jnp.where(own, values, docs[0])
        for i in range(seq_len // block):
            at = pl.ds(i * block, block)
            dvs, dks = [], []
            for j in range(2):
                probs = jnp.exp2(dot(k2[j, at, :], q2[j], ((1,), (1,))))
                ds = probs * dot(v2[j, at, :], g2[j], ((1,), (1,)))
                ds = ds.astype(BF16)
                dvs.append(dot(probs.astype(BF16), grads, ((1,), (0,))))
                dks.append(dot(ds, queries, ((1,), (0,))))
                dq = dot(ds, qkv[now, 1, at, :], ((0,), (0,)))
                if i == 0:
                    dq2[j] = dq
                else:
                    dq2[j] += dq
            here = lanes_of(0, dvs[0].shape)
            dk = jnp.where(here, dks[0], dks[1]) * (1.0 / LOG2E)
            grad_qkv[at, pl.ds(pl.multiple_of(width + p * 128, 128), 128)] = (
                dk * cos[at, :] + swap_halves(dk * sin[at, :])
            ).astype(BF16)
            grad_qkv[at, pl.ds(pl.multiple_of(2 * width + p * 128, 128), 128)] = jnp.where(
                here, dvs[0], dvs[1]
            ).astype(BF16)
            if i == seq_len // block - 1:
                dq = jnp.where(lanes_of(0, dq2.shape[1:]), dq2[0], dq2[1])
                dq = dq * (1.0 / math.sqrt(HEAD_DIM))
                grad_qkv[:, at_p] = (dq * cos[...] + swap_halves(dq * sin[...])).astype(
                    BF16
                )
            for slot, events in slots.items():
                if slot % 2 != i:
                    continue

                @pl.when(p == slot // 2)
                def _():
                    for e in events:
                        run(*e)

    w_copy.wait()
    gain = mod[6:7, :]
    scale = 1.0 + mod[1:2, :]
    gmod[...] = gm_in[...]
    for r in range(n_seq):
        at = pl.ds(r * length, length)
        e = dot(grad_qkv[at, :], w[...], ((1,), (1,)))
        normal, rstd = normalise(tok[at, :].astype(F32))
        gmod[0:1, :] += jnp.sum(e, 0, keepdims=True)
        weighted = jnp.sum(e * normal, 0, keepdims=True)
        gmod[1:2, :] += weighted * gain
        gmod[6:7, :] += weighted * scale
        h = e * (gain * scale)
        mean_h = jnp.mean(h, -1, keepdims=True)
        mean_hz = jnp.mean(h * normal, -1, keepdims=True)
        dtok[r] = (grad_mid[at, :] + (h - mean_h - normal * mean_hz) * rstd).astype(BF16)
        if r < len(tail):
            for e in tail[r]:
                run(*e)

    own_row = pltpu.make_async_copy(gmod, gmod_o.at[d, mine], g_send.at[0])

    def group_copy(off):
        return remote(
            gmod,
            gmod_o.at[d, mine],
            g_send.at[off],
            g_recv.at[s],
            d,
            lax.rem(s + off, n_seq),
        )

    @pl.when(active)
    def _():
        own_row.start()
        for off in range(1, n_seq):
            group_copy(off).start()

    if m != 2:
        for n in range(n_seq):
            if n > 1:
                run("add", n)
                run("rest", n, 0)
        for t in range(1, m + 1):
            for n in range(n_seq):
                run("rest", n, t)
        for c in range(chunks):
            for t in range(m + 1):
                run("chunk", c, t)
    returned.start()
    if m == 2:
        run("chunk", 2, 2)

    @pl.when(active)
    def _():
        own_row.wait()

    for i in range(rows):
        owner = first + i

        @pl.when(owner != s)
        def _():
            remote(
                gmod, gmod_o.at[d, i], g_send.at[0], g_recv.at[owner], d, owner
            ).wait_recv()

    def dp_copy(off):
        return remote(
            gmod_o.at[d], gmod_o.at[d], gd_send.at[off], gd_recv.at[off], xor(d, off), s
        )

    for off in range(1, n_dp):
        dp_copy(off).start()

    total = rest.total()
    go_o[...] = total[:, :width]
    gu_o[...] = total[:, width : width + hidden]
    down_own.wait()
    for off in range(1, n_seq):
        origin = lax.rem(s + off, n_seq)
        remote(
            down_h.at[s],
            down_in.at[origin],
            down_send.at[origin],
            down_recv.at[origin],
            d,
            origin,
        ).wait_recv()
    total = down_in[0].astype(F32)
    for z in range(1, n_seq):
        total += down_in[z].astype(F32)
    for i in range(hidden // width):
        gd_o[i * depth : (i + 1) * depth, :] = total[:, i * width : (i + 1) * width]
    n = width // chunks
    for c in range(chunks):
        total = parts[c].total()
        for kind in range(3):
            gq_o[:, kind * width + c * n : kind * width + (c + 1) * n] = total[
                :, kind * n : (kind + 1) * n
            ]

    for off in range(1, n_dp):
        e = xor(d, off)
        dp_copy(off).wait_send()
        remote(
            gmod_o.at[e], gmod_o.at[e], gd_send.at[off], gd_recv.at[off], e, s
        ).wait_recv()

    @pl.when(active)
    def _():
        for off in range(1, n_seq):
            group_copy(off).wait_send()

    returned.finish()
    for z in range(n_seq):

        @pl.when(z != s)
        def _():
            down_copy(z).wait_send()

    rest.sent()
    for p in parts:
        p.sent()


def back(n_dp, n_seq, rows, hidden, grad_rest, grad_down, hbm_args, vmem_args):
    dma = pltpu.SemaphoreType.DMA
    struct = jax.ShapeDtypeStruct
    m = n_dp.bit_length() - 2
    lead = (2,) * m
    length, width = hbm_args[-1].shape[1:]
    seq_len = length * n_seq
    depth, wide = grad_rest.shape[-2:]
    gmod = vmem_args[-1]
    chunks = 3
    outs = [
        struct((depth, 3 * width), F32),
        struct((depth, width), F32),
        struct((depth, hidden), F32),
        struct((depth * hidden // width, width), F32),
        struct((rows, length, width), BF16),
        struct((n_dp, rows) + gmod.shape, F32),
    ]

    def reduce_scratch(n, acc):
        slabs = [
            pltpu.VMEM(acc + (n_seq, depth, n), BF16),
            pltpu.VMEM(lead + (n_seq, depth, n), BF16),
            pltpu.VMEM((n_seq, depth, n), BF16),
        ]
        for _ in range(2):
            for step in range(m):
                slabs.append(
                    pltpu.VMEM(
                        (n_seq,) + (2,) * (m - 1 - step) + (depth, n // 2), BF16
                    )
                )
        return slabs

    scratch = reduce_scratch(wide, lead)
    for _ in range(chunks):
        scratch += reduce_scratch(3 * width // chunks, lead + (2,))
    count = 1 + chunks
    scratch += (
        [
            pltpu.VMEM(grad_down.shape, BF16),
            pltpu.VMEM((width, 3 * width), BF16),
            pltpu.VMEM((2, 5, seq_len, 128), BF16),
            pltpu.VMEM((width, seq_len), BF16),
            pltpu.VMEM((seq_len, 3 * width), BF16),
            pltpu.VMEM((n_seq, length, width), BF16),
        ]
        + [pltpu.VMEM((2, seq_len, 128), BF16)] * 4
        + [
            pltpu.VMEM((2, seq_len, 128), F32),
            pltpu.VMEM(gmod.shape, F32),
            dma((2, 5)),
            dma((2,)),
            dma((n_seq,)),
            dma((rows,)),
            dma((n_seq,)),
            dma((n_seq,)),
            dma((n_dp,)),
            dma((n_dp,)),
            dma((count, n_seq)),
            dma((count, n_seq)),
            dma((count, n_seq)),
            dma((count, n_seq, 2, m)),
            dma((count, n_seq, 2, m)),
            dma((count, n_seq)),
            dma((count, n_seq)),
            dma((n_seq,)),
            dma((n_seq,)),
        ]
    )
    return pl.pallas_call(
        functools.partial(back_kernel, n_dp, n_seq, rows, hidden),
        out_shape=outs,
        in_specs=[ANY] * (2 + len(hbm_args)) + [VMEM] * len(vmem_args),
        out_specs=[VMEM] * 4 + [ANY] * 2,
        scratch_shapes=scratch,
        compiler_params=pltpu.CompilerParams(
            collective_id=1, has_side_effects=True, vmem_limit_bytes=VMEM_LIMIT
        ),
    )(grad_rest, grad_down, *hbm_args, *vmem_args)


def rotary_tables(seq_len):
    half = HEAD_DIM // 2
    freq = np.exp(np.float32(-math.log(10000.0)) * np.arange(half, dtype=np.float32) / np.float32(half))
    angles = np.arange(seq_len, dtype=np.float32)[:, None] * freq.astype(np.float32)[None, :]
    cos = np.tile(np.cos(angles), (1, 4)).astype(np.float32)
    sin = np.sin(angles)
    sin = np.concatenate([-sin, sin, -sin, sin], 1).astype(np.float32)
    return jnp.asarray(cos), jnp.asarray(sin)


def time_embed(step_ids, model_dim):
    half_dim = model_dim // 2
    frequency = jnp.exp(-math.log(10000.0) * jnp.arange(half_dim, dtype=jnp.float32) / half_dim)
    angles = step_ids.astype(jnp.float32)[:, None] * frequency[None, :]
    return jnp.concatenate([jnp.cos(angles), jnp.sin(angles)], axis=-1)


def shards(
    n_dp,
    n_seq,
    tokens,
    segments,
    timesteps,
    w_mod,
    b_mod,
    gain_attn,
    w_qkv,
    w_out,
    gain_mlp,
    w_up,
    w_down,
    cotangent,
):
    rows, length, width = tokens.shape
    seq_len = length * n_seq
    hidden = w_up.shape[1]
    d, s = place()
    me = d * n_seq + s
    depth = w_mod.shape[0]
    cos, sin = rotary_tables(seq_len)

    emb = time_embed(timesteps, width).astype(BF16).astype(F32)
    emb = emb.reshape(rows, n_dp, n_seq, depth)
    emb = lax.dynamic_index_in_dim(emb, s, 2, keepdims=False).transpose(1, 0, 2)
    emb = jnp.pad(emb, ((0, 0), (0, 8 - rows), (0, 128 - depth)))
    n = n_dp * n_seq

    def in_place(vector):
        size = vector.shape[0]
        here = lax.broadcasted_iota(jnp.int32, (n, size), 0) == me
        return jnp.where(here, vector.astype(F32)[None, :], 0.0).reshape(-1, width)

    base = jnp.concatenate([in_place(v) for v in (b_mod, gain_attn, gain_mlp)], 0)
    seg = jnp.broadcast_to(segments[:, None, :], (rows, 8, length))

    down = [w_down[i * depth : (i + 1) * depth] for i in range(hidden // width)]
    tok, docs, normed_a, packed, wq, rest, group, mod, emb, mixed, lse = front(
        n_dp,
        n_seq,
        tokens,
        seg,
        emb,
        (w_qkv, jnp.concatenate([w_out, w_up], 1), jnp.concatenate(down, 1)),
        w_mod,
        base,
        cos,
        sin,
    )
    tok = tok.reshape(seq_len, width)
    out, grad_mid, grad_mixed, grad_rest, grad_down, gm_in = middle_call(
        n_dp, n_seq, mixed, tok, cotangent, rest, group, mod, width, hidden
    )
    g_wqkv, g_wout, g_wup, g_wdown, d_tok, gmods = back(
        n_dp,
        n_seq,
        rows,
        hidden,
        grad_rest,
        grad_down,
        (
            wq.reshape(width, 3 * width),
            packed,
            mixed,
            grad_mixed,
            normed_a.reshape(n_seq, length, width),
        ),
        (lse, docs, cos, sin, tok, grad_mid, mod, gm_in),
    )
    gmods = gmods.reshape(n_dp * rows, 8 * width)
    g_w_mod = jnp.dot(
        emb[:, :rows, :depth].reshape(n_dp * rows, depth).T,
        gmods[:, : 6 * width],
        precision=lax.Precision.HIGHEST,
        preferred_element_type=F32,
    )
    summed = jnp.sum(gmods, 0)

    def own_part(vector, n):
        return lax.dynamic_slice_in_dim(vector, me * n, n, 0)

    return (
        out,
        d_tok,
        g_w_mod,
        own_part(summed[: 6 * width], b_mod.shape[0]),
        own_part(summed[6 * width : 7 * width], gain_attn.shape[0]),
        g_wqkv,
        g_wout,
        own_part(summed[7 * width :], gain_mlp.shape[0]),
        g_wup,
        g_wdown,
    )


def solution(mesh):
    both = P(("dp", "seq"))
    wide = P(("dp", "seq"), None)
    tokens = P("dp", "seq", None)
    return jax.shard_map(
        functools.partial(shards, mesh.shape["dp"], mesh.shape["seq"]),
        mesh=mesh,
        in_specs=(
            tokens,
            P("dp", "seq"),
            P("dp"),
            wide,
            both,
            both,
            wide,
            wide,
            both,
            wide,
            wide,
            tokens,
        ),
        out_specs=(tokens, tokens, wide, both, both, wide, wide, both, wide, wide),
        check_vma=False,
    )
```

```python
import functools
import math

import jax
import jax.numpy as jnp
import numpy as np
from jax import lax
from jax.experimental import pallas as pl
from jax.experimental.pallas import tpu as pltpu
from jax.sharding import PartitionSpec as P

HEAD_DIM = 64
EPSILON = 1e-06
MASK_FILL = -1e30
MESH = pl.DeviceIdType.MESH
BF16 = jnp.bfloat16
F32 = jnp.float32
ANY = pl.BlockSpec(memory_space=pl.ANY)
VMEM = pl.BlockSpec(memory_space=pltpu.VMEM)
VMEM_LIMIT = 60 * 2**20
LOG2E = math.log2(math.e)


def place():
    return lax.axis_index("dp"), lax.axis_index("seq")


def xor(index, bits):
    return jnp.bitwise_xor(index, bits)


def remote(src, dst, send, recv, dp, seq):
    return pltpu.make_async_remote_copy(
        src_ref=src,
        dst_ref=dst,
        send_sem=send,
        recv_sem=recv,
        device_id=(dp, seq),
        device_id_type=MESH,
    )


def greet(n_dp, n_seq):
    d, s = place()
    barrier = pltpu.get_barrier_semaphore()
    for off in range(1, n_dp):
        pl.semaphore_signal(
            barrier, inc=1, device_id=(xor(d, off), s), device_id_type=MESH
        )
    for off in range(1, n_seq):
        pl.semaphore_signal(
            barrier, inc=1, device_id=(d, lax.rem(s + off, n_seq)), device_id_type=MESH
        )
    pl.semaphore_wait(barrier, n_dp - 1 + n_seq - 1)


def bit_orders(n_dp):
    high = [1 << b for b in range(1, n_dp.bit_length() - 1)]
    return (high + [1], high[::-1] + [1])


def signed(value, sign):
    return value if sign > 0 else -value


class WeightGather:
    def __init__(self, shard, at, own_sem, z_sems, x_sems, cols, n_dp, n_seq):
        self.shard, self.at, self.own_sem = shard, at, own_sem
        self.z_sems, self.x_sems = z_sems, x_sems
        self.n_seq = n_seq
        self.cols = cols // 2
        self.orders = bit_orders(n_dp)
        self.steps = len(self.orders[0])
        self.groups = []
        for h in range(2):
            known = [(0, 0)]
            for step, bit in enumerate(self.orders[h]):
                known += [(off ^ bit, step + 1) for off, _ in known]
            self.groups.append(known)

    def own(self):
        d, s = place()
        return pltpu.make_async_copy(self.shard, self.at(d, s), self.own_sem)

    def z_copy(self, way, k):
        d, s = place()
        origin = s - signed(k - 1, way)
        side = 0 if way > 0 else 1
        send, recv = self.z_sems
        return remote(
            self.shard if k == 1 else self.at(d, origin),
            self.at(d, origin),
            send.at[side, k],
            recv.at[side, k],
            d,
            s + way,
        )

    def direct_copy(self, way, k):
        d, s = place()
        side = 0 if way > 0 else 1
        send, recv = self.z_sems
        return remote(
            self.shard,
            self.at(d, s),
            send.at[side, k],
            recv.at[side, k],
            d,
            s + signed(k, way),
        )

    def direct_each(self, body):
        d, s = place()
        for k in range(1, self.n_seq):
            for way in (1, -1):
                to = s + signed(k, way)

                @pl.when((to >= 0) & (to < self.n_seq))
                def _():
                    body(self.direct_copy(way, k))

    def z_valid(self, way, k):
        d, s = place()
        origin = s - signed(k - 1, way)
        to = s + way
        return (origin >= 0) & (origin < self.n_seq) & (to >= 0) & (to < self.n_seq)

    def half(self, ref, h):
        return ref.at[:, pl.ds(h * self.cols, self.cols)]

    def x_copy(self, origin, h, off, bit, src=None):
        d, s = place()
        dst = self.half(self.at(xor(d, off), origin), h)
        send, recv = self.x_sems
        return remote(
            dst if src is None else self.half(src, h),
            dst,
            send.at[origin, h, off ^ bit],
            recv.at[origin, h, off ^ bit],
            xor(d, bit),
            s,
        )

    def each(self, k, body):
        d, s = place()
        if k == 0:
            body(s, 0)
            return
        for way in (1, -1):
            origin = s - signed(k, way)

            @pl.when((origin >= 0) & (origin < self.n_seq))
            def _():
                body(origin, way)

    def z_start(self, k):
        for way in (1, -1):

            @pl.when(self.z_valid(way, k))
            def _():
                self.z_copy(way, k).start()

    def x_start(self, origin, src=None):
        for h in range(2):
            for bit in self.orders[h]:
                self.x_copy(origin, h, 0, bit, src).start()

    def own_start(self):
        d, s = place()
        self.own().start()
        self.x_start(s, self.shard)

    def passing(self, origin, t):
        for h in range(2):
            for off, step in self.groups[h]:
                if step != t:
                    continue
                self.x_copy(origin, h, off, 0).wait_recv()
                for bit in self.orders[h][t:]:
                    self.x_copy(origin, h, off, bit).start()

    def x_sent(self, origin):
        for h in range(2):
            for off, step in self.groups[h]:
                for bit in self.orders[h][step:]:
                    self.x_copy(origin, h, off, bit).wait_send()

    def event(self, k, t, forward=True, across=True):
        if t:
            self.each(k, lambda origin, way: self.passing(origin, t))
            return
        d, s = place()
        send, recv = self.z_sems

        def arrival(origin, way):
            side = 0 if way > 0 else 1
            remote(
                self.shard,
                self.at(d, origin),
                send.at[side, k],
                recv.at[side, k],
                d,
                s,
            ).wait_recv()
            if across:
                self.x_start(origin)

        self.each(k, arrival)
        if forward and k + 1 < self.n_seq:
            self.z_start(k + 1)

    def finish(self, direct=False, across=True):
        if direct:
            self.direct_each(lambda copy: copy.wait_send())
        else:
            for k in range(1, self.n_seq):
                for way in (1, -1):

                    @pl.when(self.z_valid(way, k))
                    def _():
                        self.z_copy(way, k).wait_send()

        if across:
            for k in range(self.n_seq):
                self.each(k, lambda origin, way: self.x_sent(origin))


def dot(a, b, dims):
    return lax.dot_general(a, b, (dims, ((), ())), preferred_element_type=F32)


def swap_halves(x):
    quarter = HEAD_DIM // 2
    lane = lax.broadcasted_iota(jnp.int32, x.shape, 1)
    return jnp.where(
        lax.rem(lane, HEAD_DIM) < quarter,
        pltpu.roll(x, 128 - quarter, axis=1),
        pltpu.roll(x, quarter, axis=1),
    )


def normalise(x):
    mean = jnp.mean(x, -1, keepdims=True)
    centred = x - mean
    var = jnp.mean(centred * centred, -1, keepdims=True)
    rstd = lax.rsqrt(var + EPSILON)
    return centred * rstd, rstd


def join_slabs(slabs, whole):
    depth = slabs.shape[-2]
    count = math.prod(slabs.shape[:-2])
    group = 16 // math.gcd(16, depth)

    @pl.loop(0, count // group)
    def _(i):
        parts = []
        for j in range(group):
            k, idx = i * group + j, []
            for n in slabs.shape[:-2][::-1]:
                idx.append(lax.rem(k, n))
                k = lax.div(k, n)
            parts.append(slabs[tuple(idx[::-1])])
        rows = group * depth
        whole[pl.ds(pl.multiple_of(i * rows, rows), rows), :] = jnp.concatenate(parts, 0)


def lanes_of(j, shape):
    lane = lax.broadcasted_iota(jnp.int32, shape, 1)
    return lax.div(lane, HEAD_DIM) == j


def front_kernel(n_dp, n_seq, rows, *refs):
    tokens, seg, emb_h, *shards = refs[:6]
    w_mod, base, cos, sin = refs[6:10]
    tok_o, doc_o, norm_o, pack_o, *fulls = refs[10:17]
    mod_o, emb, mixed_o, lse_o = refs[17:21]
    (
        tok,
        segs,
        docs,
        normed,
        packed,
        w_in,
        w,
        values,
        keys,
        mod_in,
        mod_sum,
        mod_row,
        out_sem,
        row_send,
        row_recv,
        mod_send,
        mod_recv,
        modz_send,
        modz_recv,
        own_sem,
        z_send,
        z_recv,
        x_send,
        x_recv,
        part,
        emb_send,
        emb_recv,
    ) = refs[21:]
    d, s = place()
    length, width = tokens.shape[1:]
    seq_len = length * n_seq
    first = lax.rem(d, 2)
    mine = s - first
    active = (mine >= 0) & (mine < rows)
    greet(n_dp, n_seq)

    def mod_copy(off):
        return remote(
            part.at[xor(d, off)],
            mod_in.at[d],
            mod_send.at[off],
            mod_recv.at[off],
            xor(d, off),
            s,
        )

    def emb_copy(off):
        return remote(
            emb_h.at[xor(d, off)],
            emb.at[d],
            emb_send.at[off],
            emb_recv.at[off],
            xor(d, off),
            s,
        )

    emb_own = pltpu.make_async_copy(emb_h.at[d], emb.at[d], emb_send.at[0])
    emb_own.start()
    for off in range(1, n_dp):
        emb_copy(off).start()

    ats = [
        lambda e, z: fulls[0].at[e, z],
        lambda e, z: fulls[1].at[e, z],
        lambda e, z: fulls[2].at[z],
    ]
    qkv, rest, down = [
        WeightGather(
            shards[i],
            ats[i],
            own_sem.at[i],
            (z_send.at[i], z_recv.at[i]),
            (x_send.at[i], x_recv.at[i]) if i < 2 else None,
            shards[i].shape[1],
            n_dp,
            n_seq,
        )
        for i in range(3)
    ]
    qkv.direct_each(lambda copy: copy.start())
    rest.z_start(1)
    down.z_start(1)
    down.own().start()
    qkv.own_start()

    emb_own.wait()
    for off in range(1, n_dp):
        e = xor(d, off)
        remote(
            emb_h.at[d], emb.at[e], emb_send.at[off], emb_recv.at[off], d, s
        ).wait_recv()
    features = emb[...].reshape(n_dp * 8, 128)[:, : w_mod.shape[0]].astype(BF16)
    for k in range(8):
        if k < 6:
            terms = dot(features, w_mod[:, k * width : (k + 1) * width], ((1,), (0,)))
            terms = terms + base[k : k + 1, :]
        for e in range(n_dp):
            for i in range(rows):
                part[e, i, k : k + 1, :] = (
                    terms[e * 8 + i : e * 8 + i + 1] if k < 6 else base[k : k + 1, :]
                )
    for off in range(1, n_dp):
        mod_copy(off).start()

    trio = ((tokens, tok), (seg, segs))

    def row_local(k, i):
        src, dst = trio[k]
        return pltpu.make_async_copy(src.at[i], dst.at[s], row_send.at[k, i])

    def row_remote(k, i):
        src, dst = trio[k]
        return remote(
            src.at[i], dst.at[s], row_send.at[k, i], row_recv.at[k, s], d, first + i
        )

    def row_start(k):
        for i in range(rows):

            @pl.when(first + i == s)
            def _():
                row_local(k, i).start()

            @pl.when(first + i != s)
            def _():
                row_remote(k, i).start()

    def row_sent(k):
        for i in range(rows):

            @pl.when(first + i != s)
            def _():
                row_remote(k, i).wait_send()

    def row_arrival(k, origin):
        src, dst = trio[k]
        remote(
            src.at[0],
            dst.at[origin],
            row_send.at[k, 0],
            row_recv.at[k, origin],
            d,
            origin,
        ).wait_recv()

    def row_own(k):
        for i in range(rows):

            @pl.when(first + i == s)
            def _():
                row_local(k, i).wait()

    def mod_exchange():
        for off in range(1, n_dp):
            remote(
                part.at[d],
                mod_in.at[xor(d, off)],
                mod_send.at[off],
                mod_recv.at[off],
                d,
                s,
            ).wait_recv()
        total = part[d]
        for off in range(1, n_dp):
            total += mod_in[xor(d, off)]
        mod_sum[...] = total
        for i in range(rows):

            @pl.when(first + i == s)
            def _():
                mod_row[s] = mod_sum[i]

            @pl.when(first + i != s)
            def _():
                remote(
                    mod_sum.at[i],
                    mod_row.at[s],
                    modz_send.at[i],
                    modz_recv.at[s],
                    d,
                    first + i,
                ).start()

    @pl.when(jnp.logical_not(active))
    def _():
        tok[...] = jnp.zeros_like(tok)
        segs[...] = jnp.zeros_like(segs)

    row_start(1)
    for k in range(1, n_seq):
        qkv.event(k, 0, forward=False)
    mod_exchange()
    row_start(0)
    for k in range(n_seq):
        qkv.event(k, 1)
    rest.own_start()
    rest.event(1, 0)
    down.event(1, 0, across=False)
    for t in range(2, qkv.steps + 1):
        for k in range(n_seq):
            qkv.event(k, t)
    stage = pltpu.make_async_copy(fulls[0], w_in, out_sem.at[0])
    qkv.own().wait()
    stage.start()

    @pl.when(active)
    def _():
        for off in range(1, n_seq):
            row_arrival(1, lax.rem(s + off, n_seq))

    row_own(1)
    lane = lax.broadcasted_iota(jnp.int32, (length, 128), 1)
    lane = lax.rem(lane, HEAD_DIM).astype(F32)
    for z in range(n_seq):
        ids = jnp.transpose(
            jnp.broadcast_to(segs[z, 0:1, :].astype(F32), (128, length))
        )
        same = ids == lane
        at = pl.ds(z * length, length)
        docs[0, at, :] = jnp.where(
            same | ((lane >= 8.0) & (lane < 11.0)), 1.0, 0.0
        ).astype(BF16)
        docs[1, at, :] = jnp.where(same | (lane >= 8.0), 0.0, MASK_FILL).astype(BF16)
    doc_copy = pltpu.make_async_copy(docs, doc_o, out_sem.at[1])
    doc_copy.start()

    stage.wait()
    depth = w_in.shape[2]

    join_slabs(w_in, w)

    @pl.when(active)
    def _():
        for off in range(1, n_seq):
            origin = lax.rem(s + off, n_seq)
            remote(
                mod_sum.at[0],
                mod_row.at[origin],
                modz_send.at[0],
                modz_recv.at[origin],
                d,
                origin,
            ).wait_recv()
        total = mod_row[0]
        for z in range(1, n_seq):
            total += mod_row[z]
        mod_o[...] = total

    @pl.when(jnp.logical_not(active))
    def _():
        mod_o[...] = jnp.zeros_like(mod_o)

    rest.event(0, 1)

    gain = mod_o[6:7, :] * (1.0 + mod_o[1:2, :])
    shift = mod_o[0:1, :]
    row_own(0)
    for off in range(n_seq):
        z = lax.rem(s + off, n_seq)
        if off:

            @pl.when(active)
            def _():
                row_arrival(0, z)

        normal, _ = normalise(tok[z].astype(F32))
        at = pl.ds(pl.multiple_of(z * length, length), length)
        normed[at, :] = (normal * gain + shift).astype(BF16)
    outs = [
        pltpu.make_async_copy(tok, tok_o, out_sem.at[2]),
        pltpu.make_async_copy(normed, norm_o, out_sem.at[3]),
    ]
    for c in outs:
        c.start()

    early = [[(0, 2), (1, 1)], [(2, 0)], [(0, 3)]]
    for kind in range(3):

        @pl.loop(0, width // 256)
        def _(c):
            col = kind * width + c * 256
            wc = w[:, pl.ds(pl.multiple_of(col, 256), 256)]
            for r in range(seq_len // 256):
                at = pl.ds(r * 256, 256)
                y = dot(normed[at, :], wc, ((1,), (0,)))
                for j in range(2):
                    p = y[:, j * 128 : (j + 1) * 128]
                    if kind < 2:
                        p = p * cos[at, :] + swap_halves(p) * sin[at, :]
                    if kind == 0:
                        p = p * (LOG2E / math.sqrt(HEAD_DIM))
                    packed[kind * (width // 128) + c * 2 + j, at, :] = p.astype(BF16)

        for e in early[kind]:
            rest.event(*e)
            if e == (2, 0):
                down.event(2, 0, across=False)

    pack_copy = pltpu.make_async_copy(packed, pack_o, out_sem.at[4])
    pack_copy.start()
    pairs = width // 128
    slots = {
        0: [(1, 2)],
        1: [(2, 1), (3, 0)],
        2: [(1, 3)],
        3: [(2, 2), (3, 1)],
        4: [(3, 2)],
    }
    done = {e for v in slots.values() for e in v}
    done |= {e for v in early for e in v} | {(1, 0), (0, 1)}

    values[:, 128:] = jnp.ones((seq_len, 128), BF16)
    block = 128
    lse_o[...] = jnp.zeros_like(lse_o)

    @pl.loop(0, pairs)
    def _(p):
        k = packed[pairs + p]
        values[:, :128] = packed[2 * pairs + p]
        for j in range(2):
            keys[j] = jnp.where(lanes_of(j, k.shape), k, docs[0])
        for i in range(seq_len // block):
            at = pl.ds(i * block, block)
            q = packed[p, at, :]
            both = []
            stats = lse_o[at, :]
            lane = lax.broadcasted_iota(jnp.int32, (block, 128), 1)
            for j in range(2):
                own = lanes_of(j, q.shape)
                scores = dot(jnp.where(own, q, docs[1, at, :]), keys[j], ((1,), (1,)))
                top = jnp.max(scores, -1, keepdims=True)
                e = jnp.exp2(scores - top).astype(BF16)
                o = dot(e, values[...], ((1,), (0,)))
                total = o[:, 128:]
                both.append(o[:, :128] / total)
                stats = jnp.where(lane == 2 * p + j, top + jnp.log2(total), stats)
            lse_o[at, :] = stats
            mixed_o[at, pl.ds(pl.multiple_of(p * 128, 128), 128)] = jnp.where(
                lane < HEAD_DIM, both[0], both[1]
            ).astype(BF16)
        for slot, events in slots.items():

            @pl.when(p == slot)
            def _():
                for k, t in events:
                    rest.event(k, t)
                    if (k, t) == (3, 0):
                        down.event(3, 0, across=False)

    for t in range(1, rest.steps + 1):
        for k in range(n_seq):
            if (k, t) not in done:
                rest.event(k, t)

    for i in range(rows):

        @pl.when(first + i != s)
        def _():
            remote(
                mod_sum.at[i], mod_row.at[s], modz_send.at[i], modz_recv.at[s], d, first + i
            ).wait_send()

    for off in range(1, n_dp):
        mod_copy(off).wait_send()
    rest.own().wait()
    down.own().wait()
    for c in outs + [doc_copy, pack_copy]:
        c.wait()

    for k in range(2):
        row_sent(k)
    for off in range(1, n_dp):
        emb_copy(off).wait_send()
    qkv.finish(direct=True)
    rest.finish()
    down.finish(across=False)


def front(n_dp, n_seq, tokens, seg, emb, shards, w_mod, base, cos, sin):
    rows, length, width = tokens.shape
    seq_len = length * n_seq
    dma = pltpu.SemaphoreType.DMA
    struct = jax.ShapeDtypeStruct
    pairs = width // 128
    outs = [
        struct((n_seq, length, width), BF16),
        struct((2, seq_len, 128), BF16),
        struct((seq_len, width), BF16),
        struct((3 * pairs, seq_len, 128), BF16),
    ]
    outs += [struct((n_dp, n_seq) + w.shape, BF16) for w in shards[:2]]
    outs += [
        struct((n_seq,) + shards[2].shape, BF16),
        struct((8, width), F32),
        struct(emb.shape, F32),
        struct((seq_len, width), BF16),
        struct((seq_len, 128), F32),
    ]
    return pl.pallas_call(
        functools.partial(front_kernel, n_dp, n_seq, rows),
        out_shape=outs,
        in_specs=[ANY] * 6 + [VMEM] * 4,
        out_specs=[ANY] * 7 + [VMEM] * 4,
        scratch_shapes=[
            pltpu.VMEM((n_seq, length, width), BF16),
            pltpu.VMEM((n_seq,) + seg.shape[1:], jnp.int32),
            pltpu.VMEM((2, seq_len, 128), BF16),
            pltpu.VMEM((seq_len, width), BF16),
            pltpu.VMEM((3 * pairs, seq_len, 128), BF16),
            pltpu.VMEM((n_dp, n_seq) + shards[0].shape, BF16),
            pltpu.VMEM((width, 3 * width), BF16),
            pltpu.VMEM((seq_len, 256), BF16),
            pltpu.VMEM((2, seq_len, 128), BF16),
            pltpu.VMEM((n_dp, rows, 8, width), F32),
            pltpu.VMEM((rows, 8, width), F32),
            pltpu.VMEM((n_seq, 8, width), F32),
            dma((5,)),
            dma((2, rows)),
            dma((2, n_seq)),
            dma((n_dp,)),
            dma((n_dp,)),
            dma((rows,)),
            dma((n_seq,)),
            dma((3,)),
            dma((3, 2, n_seq)),
            dma((3, 2, n_seq)),
            dma((2, n_seq, 2, n_dp)),
            dma((2, n_seq, 2, n_dp)),
            pltpu.VMEM((n_dp, rows, 8, width), F32),
            dma((n_dp,)),
            dma((n_dp,)),
        ],
        compiler_params=pltpu.CompilerParams(
            collective_id=0, has_side_effects=True, vmem_limit_bytes=VMEM_LIMIT
        ),
    )(tokens, seg, emb, *shards, w_mod, base, cos, sin)


class GradReduce:
    def __init__(self, grad, own, local, core_in, step_in, z_in, sems, n_dp, n_seq):
        self.grad, self.own, self.local = grad, own, local
        self.core_in, self.step_in, self.z_in = core_in, step_in, z_in
        self.sems, self.n_seq = sems, n_seq
        self.bits = list(range(n_dp.bit_length() - 2, 0, -1))
        self.m = len(self.bits)
        self.orders = (list(range(self.m)), list(range(self.m))[::-1])
        self.cols = core_in.shape[-1] // 2

    def my(self, dim):
        d, _ = place()
        return lax.rem(lax.div(d, 1 << self.bits[dim]), 2)

    def mine(self):
        return tuple(self.my(dim) for dim in range(self.m))

    def index(self, done, flip=None):
        return tuple(
            self.my(dim)
            if dim in done
            else 1 - self.my(dim)
            if dim == flip
            else slice(None)
            for dim in range(self.m)
        )

    def core_copies(self, z):
        d, s = place()
        core = lax.rem(d, 2)
        lead = (slice(None),) * self.m
        send, recv, local = self.sems["core"]
        copies = [
            remote(
                self.grad.at[lead + (1 - core, z)],
                self.core_in.at[lead + (z,)],
                send.at[z],
                recv.at[z],
                xor(d, 1),
                s,
            )
        ]
        if self.local:
            copies.append(
                pltpu.make_async_copy(
                    self.grad.at[lead + (core, z)],
                    self.own(lead, z, slice(None)),
                    local.at[z],
                )
            )
        return copies

    def core_start(self, z):
        for c in self.core_copies(z):
            c.start()

    def core_add(self, z):
        for c in self.core_copies(z):
            c.wait()

        @pl.loop(0, 1 << self.m)
        def _(n):
            lead = tuple(
                lax.rem(lax.div(n, 1 << (self.m - 1 - dim)), 2) for dim in range(self.m)
            )
            target = self.own(lead, z, slice(None))
            target[...] = target[...] + self.core_in[lead + (z,)]

    def step_copy(self, z, h, step):
        d, s = place()
        order = self.orders[h]
        send, recv = self.sems["step"]
        cols = pl.ds(h * self.cols, self.cols)
        return remote(
            self.own(self.index(order[:step], order[step]), z, cols),
            self.step_in[h][step].at[z],
            send.at[z, h, step],
            recv.at[z, h, step],
            xor(d, 1 << self.bits[order[step]]),
            s,
        )

    def mine_at(self, z):
        return self.own(self.mine(), z, slice(None))

    def z_copy(self, z):
        d, s = place()
        send, recv = self.sems["z"]
        return remote(self.mine_at(z), self.z_in.at[s], send.at[z], recv.at[s], d, z)

    def event(self, z, t):
        for h in range(2):
            if t:
                self.step_copy(z, h, t - 1).wait()
                order = self.orders[h]
                cols = pl.ds(h * self.cols, self.cols)
                free = [dim for dim in range(self.m) if dim not in order[:t]]
                for n in range(1 << len(free)):
                    bits = [(n >> (len(free) - 1 - i)) & 1 for i in range(len(free))]
                    lead = tuple(
                        bits[free.index(dim)] if dim in free else self.my(dim)
                        for dim in range(self.m)
                    )
                    target = self.own(lead, z, cols)
                    target[...] = target[...] + self.step_in[h][t - 1][(z, *bits)]
            if t < self.m:
                self.step_copy(z, h, t).start()
        if t == self.m and self.z_in is not None:
            _, s = place()

            @pl.when(z != s)
            def _():
                self.z_copy(z).start()

    def total(self):
        d, s = place()
        send, recv = self.sems["z"]
        for off in range(1, self.n_seq):
            origin = lax.rem(s + off, self.n_seq)
            remote(
                self.mine_at(s),
                self.z_in.at[origin],
                send.at[origin],
                recv.at[origin],
                d,
                origin,
            ).wait_recv()
        total = self.mine_at(s)[...].astype(F32)
        for off in range(1, self.n_seq):
            total += self.z_in[lax.rem(s + off, self.n_seq)].astype(F32)
        return total

    def sent(self):
        _, s = place()
        for z in range(self.n_seq):

            @pl.when(z != s)
            def _():
                self.z_copy(z).wait_send()


def spread(k, dims):
    idx = []
    for n in dims[::-1]:
        idx.append(k % n if isinstance(k, int) else lax.rem(k, n))
        k = k // n if isinstance(k, int) else lax.div(k, n)
    return tuple(idx[::-1])


GELU_A = math.sqrt(2.0 / math.pi)
GELU_B = 0.044715 * GELU_A


def gelu_both(u):
    square = u * u
    half = 0.5 * jnp.tanh(u * (GELU_B * square + GELU_A)) + 0.5
    value = u * half
    slope = half + value * (1.0 - half) * (6.0 * GELU_B * square + 2.0 * GELU_A)
    return value, slope


class RowReturn:
    def __init__(self, src, dst, send, recv, rows, n_seq):
        self.src, self.dst, self.send, self.recv = src, dst, send, recv
        self.rows, self.n_seq = rows, n_seq
        d, s = place()
        self.first = lax.rem(d, 2)
        self.mine = s - self.first
        self.active = (self.mine >= 0) & (self.mine < rows)

    def local(self):
        _, s = place()
        return pltpu.make_async_copy(
            self.src.at[s], self.dst.at[self.mine], self.send.at[0]
        )

    def remote(self, off):
        d, s = place()
        to = lax.rem(s + off, self.n_seq)
        return remote(
            self.src.at[to],
            self.dst.at[self.mine],
            self.send.at[off],
            self.recv.at[self.mine],
            d,
            to,
        )

    def start(self, offs=None):
        @pl.when(self.active)
        def _():
            for off in range(self.n_seq) if offs is None else offs:
                if off:
                    self.remote(off).start()
                else:
                    self.local().start()

    def finish(self):
        d, s = place()

        @pl.when(self.active)
        def _():
            self.local().wait()
            for off in range(1, self.n_seq):
                self.remote(off).wait_send()

        for i in range(self.rows):

            @pl.when(self.first + i != s)
            def _():
                remote(
                    self.src.at[0],
                    self.dst.at[i],
                    self.send.at[0],
                    self.recv.at[i],
                    d,
                    self.first + i,
                ).wait_recv()


def middle_kernel(n_dp, n_seq, *refs):
    mixed_h, tok_h, cot_h, rest_h, group_h, mod = refs[:6]
    out_o, mid_h, gmixed_h, grad_h, down_h, gm = refs[6:12]
    m = n_dp.bit_length() - 2
    (
        wo,
        wu,
        wd,
        slabs,
        mixed,
        tok,
        cot,
        act,
        slope,
        normed,
        g_mlp,
        g_attn,
        turned,
        out,
        attn,
        mlp,
        sems,
        cot_send,
        cot_recv,
        row_send,
        row_recv,
        c_send,
        c_recv,
        s_send,
        s_recv,
        tiles,
        tile_sem,
        x_send,
        x_recv,
        own_sem,
        core_in,
        *steps,
    ) = refs[12:]
    d, s = place()
    rows = cot_h.shape[0]
    length = cot_h.shape[1]
    seq_len, width = mixed.shape
    hidden = wu.shape[1]
    depth = slabs.shape[-2]
    lead = slabs.shape[:-2]
    count = math.prod(lead)
    everything = (slice(None),) * len(lead)
    ways = hidden // width
    down = width + hidden
    first = lax.rem(d, 2)
    mine = s - first
    active = (mine >= 0) & (mine < rows)
    ins = [
        pltpu.make_async_copy(*args, sems.at[i])
        for i, args in enumerate(
            (
                (rest_h.at[:, pl.ds(0, width)], wo),
                (mixed_h, mixed),
                (tok_h, tok),
                (rest_h.at[:, pl.ds(width, hidden)], wu),
            )
        )
    ]
    for c in ins:
        c.start()
    greet(n_dp, n_seq)
    core = lax.rem(d, 2)
    sums = GradReduce(
        slabs,
        lambda idx, z, cols: slabs.at[tuple(idx) + (core, z, slice(None), cols)],
        False,
        core_in,
        (steps[:m], steps[m:]),
        None,
        {"core": (c_send, c_recv, None), "step": (s_send, s_recv)},
        n_dp,
        n_seq,
    )

    def slab_at(e, z):
        bits = [lax.rem(lax.div(e, 1 << b), 2) for b in range(len(lead) - 1)]
        return slabs.at[tuple(bits[::-1]) + (z,)]

    gather = WeightGather(
        None, slab_at, None, None, (x_send, x_recv), hidden, n_dp, n_seq
    )
    group_own = [
        pltpu.make_async_copy(group_h.at[z], slab_at(d, z), own_sem.at[z])
        for z in range(n_seq)
    ]
    for z in range(n_seq):
        gather.x_start(z, group_h.at[z])
        group_own[z].start()

    def cot_remote(i):
        return remote(
            cot_h.at[i], cot.at[s], cot_send.at[i], cot_recv.at[s], d, first + i
        )

    def cot_local(i):
        return pltpu.make_async_copy(cot_h.at[i], cot.at[s], cot_send.at[i])

    def cot_each(near, far):
        for i in range(rows):
            pl.when(first + i == s)(functools.partial(near, i))
            pl.when(first + i != s)(functools.partial(far, i))

    cot_each(lambda i: cot_local(i).start(), lambda i: cot_remote(i).start())

    @pl.when(jnp.logical_not(active))
    def _():
        cot[...] = jnp.zeros_like(cot)

    for c in ins:
        c.wait()

    shift = mod[3:4, :]
    gain = mod[7:8, :]
    scale = 1.0 + mod[4:5, :]
    gate_a = mod[2:3, :]
    gate_m = mod[5:6, :]
    gm[...] = jnp.zeros_like(gm)
    chunk = 512
    block = 2 * length
    blocks = [(pl.ds(r * block, block), pl.ds(r * 2, 2)) for r in range(n_seq // 2)]
    three = (2, length, width)

    def middle_of(at):
        return tok[at, :].astype(F32) + gate_a * attn[at, :]

    half = n_seq // 2
    gather_events = [[(z, 1) for z in range(half)], [(z, 1) for z in range(half, n_seq)]]
    gather_events += [
        [(z, t) for z in range(n_seq)] for t in range(2, gather.steps + 1)
    ]
    for at, _ in blocks:
        attn[at, :] = dot(mixed[at, :], wo[...], ((1,), (0,)))
        normal, _ = normalise(middle_of(at))
        normed[at, :] = (normal * (gain * scale) + shift).astype(BF16)

        @pl.loop(0, hidden // chunk)
        def _(c):
            cols = pl.ds(pl.multiple_of(c * chunk, chunk), chunk)
            value, steep = gelu_both(dot(normed[at, :], wu[:, cols], ((1,), (0,))))
            act[at, cols] = value.astype(BF16)
            slope[at, cols] = steep.astype(BF16)

        if gather_events:
            for z, t in gather_events.pop(0):
                gather.passing(z, t)

    def turn(left):
        for r in range(seq_len // 256):
            at = pl.ds(r * 256, 256)
            turned[:, at] = jnp.transpose(left[at, :])

    turn(normed)
    for events in gather_events:
        for z, t in events:
            gather.passing(z, t)
    for z in range(n_seq):
        gather.x_sent(z)
        group_own[z].wait()
    group = 16 // math.gcd(16, depth * ways)

    @pl.loop(0, count // group)
    def _(i):
        parts = [
            slabs[spread(i * group + j, lead) + (slice(None), pl.ds(k * width, width))]
            for j in range(group)
            for k in range(ways)
        ]
        n = group * depth * ways
        wd[pl.ds(pl.multiple_of(i * n, n), n), :] = jnp.concatenate(parts, 0)

    for at, two in blocks:
        mlp_out = dot(act[at, :], wd[...], ((1,), (0,)))
        mlp[at, :] = mlp_out.astype(BF16)
        out[two] = (middle_of(at) + gate_m * mlp_out).astype(BF16).reshape(three)
    returned = RowReturn(out, out_o, row_send, row_recv, rows, n_seq)

    cot_each(lambda i: cot_local(i).wait(), lambda i: None)

    @pl.when(active)
    def _():
        for off in range(1, n_seq):
            origin = lax.rem(s + off, n_seq)
            remote(
                cot_h.at[0],
                cot.at[origin],
                cot_send.at[0],
                cot_recv.at[origin],
                d,
                origin,
            ).wait_recv()

    for at, two in blocks:
        grad = cot[two].reshape(block, width).astype(F32)
        g_mlp[at, :] = (grad * gate_m).astype(BF16)
        gm[5:6, :] += jnp.sum(grad * mlp[at, :].astype(F32), 0, keepdims=True)

    several = math.lcm(128, depth * ways) // (depth * ways)

    @pl.loop(0, count // several)
    def _(i):
        n = several * depth * ways
        at = pl.ds(pl.multiple_of(i * n, n), n)
        g = dot(act[:, at], g_mlp[...], ((0,), (0,)))
        for j in range(several):
            for k in range(ways):
                row = (j * ways + k) * depth
                slabs[
                    spread(i * several + j, lead) + (slice(None), pl.ds(k * width, width))
                ] = g[row : row + depth].astype(BF16)

    returned.start()
    for z in range(n_seq):
        sums.core_start(z)
    todo = [[("add", z) for z in range(n_seq)] + [(z, 0) for z in range(n_seq)]]
    todo += [[(z, t) for z in range(n_seq)] for t in range(1, m + 1)]

    def proceed():
        for z, t in todo.pop(0) if todo else []:
            if z == "add":
                sums.core_add(t)
            else:
                sums.event(z, t)

    for at, two in blocks:
        grad = cot[two].reshape(block, width).astype(F32)

        @pl.loop(0, hidden // chunk)
        def _(c):
            cols = pl.ds(pl.multiple_of(c * chunk, chunk), chunk)
            g_act = dot(g_mlp[at, :], wd[cols, :], ((1,), (1,)))
            slope[at, cols] = (g_act * slope[at, cols].astype(F32)).astype(BF16)

        e = dot(slope[at, :], wu[...], ((1,), (1,)))
        gm[3:4, :] += jnp.sum(e, 0, keepdims=True)
        normal, rstd = normalise(middle_of(at))
        weighted = jnp.sum(e * normal, 0, keepdims=True)
        gm[4:5, :] += weighted * gain
        gm[7:8, :] += weighted * scale
        h = e * (gain * scale)
        mean_h = jnp.mean(h, -1, keepdims=True)
        mean_hz = jnp.mean(h * normal, -1, keepdims=True)
        g_mid = grad + (h - mean_h - normal * mean_hz) * rstd
        mlp[at, :] = g_mid.astype(BF16)
        gm[2:3, :] += jnp.sum(g_mid * attn[at, :], 0, keepdims=True)
        g_attn[at, :] = (g_mid * gate_a).astype(BF16)
        g_mixed = dot(g_attn[at, :], wo[...], ((1,), (1,)))
        cot[two] = g_mixed.astype(BF16).reshape(three)
        proceed()

    outs = [
        pltpu.make_async_copy(*args, sems.at[i])
        for i, args in enumerate(((mlp, mid_h), (cot, gmixed_h)))
    ]
    for c in outs:
        c.start()

    tile = 256

    def tile_copy(slot, col):
        return pltpu.make_async_copy(
            tiles.at[slot],
            grad_h.at[everything + (slice(None), pl.ds(col, tile))],
            tile_sem.at[slot],
        )

    def weight_grad(right, start, n, busy):
        @pl.loop(0, n // tile)
        def _(c):
            col = pl.multiple_of(c * tile, tile)
            slot = lax.rem(c, 2)
            g = dot(turned[...], right[:, pl.ds(col, tile)], ((1,), (0,)))

            @pl.when((c >= 2) | busy)
            def _():
                tile_copy(slot, 0).wait()

            for i in range(count):
                tiles[(slot,) + spread(i, lead)] = g[
                    i * depth : (i + 1) * depth
                ].astype(BF16)
            tile_copy(slot, pl.multiple_of(start + col, tile)).start()

    weight_grad(slope, width, hidden, False)
    proceed()
    turn(mixed)
    weight_grad(g_attn, 0, width, True)
    while todo:
        proceed()
    reduced = []
    for z in range(n_seq):
        reduced.append(
            pltpu.make_async_copy(sums.mine_at(z), down_h.at[z], c_send.at[z])
        )
        reduced[-1].start()
    for slot in range(2):
        tile_copy(slot, 0).wait()
    for c in outs + reduced:
        c.wait()
    cot_each(lambda i: None, lambda i: cot_remote(i).wait_send())
    returned.finish()


def middle_call(n_dp, n_seq, mixed, tok, cot, rest, group, mod, width, hidden):
    seq_len = mixed.shape[0]
    rows, length = cot.shape[:2]
    depth, wide = rest.shape[-2:]
    m = n_dp.bit_length() - 2
    lead = (2,) * m
    split = lead + (2, n_seq)
    struct = jax.ShapeDtypeStruct
    dma = pltpu.SemaphoreType.DMA
    row = pltpu.VMEM((seq_len, width), BF16)
    cut = pltpu.VMEM((n_seq, length, width), BF16)
    full = pltpu.VMEM((seq_len, hidden), BF16)
    steps = [
        pltpu.VMEM((n_seq,) + (2,) * (m - 1 - step) + (depth, hidden // 2), BF16)
        for _ in range(2)
        for step in range(m)
    ]
    out, mid, g_mixed, grads, down, gm = pl.pallas_call(
        functools.partial(middle_kernel, n_dp, n_seq),
        out_shape=[
            struct(cot.shape, BF16),
            struct((seq_len, width), BF16),
            struct((n_seq, length, width), BF16),
            struct(split + (depth, width + hidden), BF16),
            struct((n_seq, depth, hidden), BF16),
            struct(mod.shape, F32),
        ],
        in_specs=[ANY] * 5 + [VMEM],
        out_specs=[ANY] * 5 + [VMEM],
        scratch_shapes=[
            pltpu.VMEM((width, width), BF16),
            pltpu.VMEM((width, hidden), BF16),
            pltpu.VMEM((hidden, width), BF16),
            pltpu.VMEM(split + (depth, hidden), BF16),
            row,
            row,
            cut,
            full,
            full,
            row,
            row,
            row,
            pltpu.VMEM((width, seq_len), BF16),
            cut,
            pltpu.VMEM((seq_len, width), F32),
            row,
            dma((6,)),
            dma((rows,)),
            dma((n_seq,)),
            dma((n_seq,)),
            dma((rows,)),
            dma((n_seq,)),
            dma((n_seq,)),
            dma((n_seq, 2, m)),
            dma((n_seq, 2, m)),
            pltpu.VMEM((2,) + split + (depth, 256), BF16),
            dma((2,)),
            dma((n_seq, 2, n_dp)),
            dma((n_seq, 2, n_dp)),
            dma((n_seq,)),
            pltpu.VMEM(lead + (n_seq, depth, hidden), BF16),
            *steps,
        ],
        compiler_params=pltpu.CompilerParams(
            collective_id=2, has_side_effects=True, vmem_limit_bytes=VMEM_LIMIT
        ),
    )(
        mixed,
        tok,
        cot,
        rest.reshape(width, wide),
        group,
        mod,
    )
    return out, mid, g_mixed.reshape(seq_len, width), grads, down, gm


def split3(x):
    high = x.astype(BF16)
    x = x - high.astype(F32)
    middle = x.astype(BF16)
    low = (x - middle.astype(F32)).astype(BF16)
    return high, middle, low


def back_kernel(n_dp, n_seq, rows, hidden, *refs):
    grad_rest, down_h, wq_h, packed_h, mixed_h, grad_mixed_h, normed_h = refs[:7]
    lse, docs, cos, sin, tok, grad_mid, mod, gm_in = refs[7:15]
    gq_o, go_o, gu_o, gd_o = refs[15:19]
    dtok_o, gmod_o = refs[19:21]
    refs = refs[21:]
    m = n_dp.bit_length() - 2
    chunks = 3
    sets = []
    for _ in range(1 + chunks):
        acc, core_in, z_in = refs[:3]
        steps = (refs[3 : 3 + m], refs[3 + m : 3 + 2 * m])
        sets.append((acc, core_in, steps, z_in))
        refs = refs[3 + 2 * m :]
    (
        down_in,
        w,
        qkv,
        normed_t,
        grad_qkv,
        dtok,
        q2,
        k2,
        v2,
        g2,
        dq2,
        keys_t,
        gmod,
        qkv_sem,
        w_sem,
        row_send,
        row_recv,
        g_send,
        g_recv,
        gd_send,
        gd_recv,
        c_send,
        c_recv,
        c_local,
        s_send,
        s_recv,
        z_send,
        z_recv,
        down_send,
        down_recv,
    ) = refs
    d, s = place()
    length, width = dtok.shape[1:]
    depth = gq_o.shape[0]
    seq_len = length * n_seq
    pairs = width // 128
    first = lax.rem(d, 2)
    mine = s - first
    active = (mine >= 0) & (mine < rows)
    core = lax.rem(d, 2)

    def pair_copies(p, slot):
        return [
            pltpu.make_async_copy(
                packed_h.at[kind * pairs + p], qkv.at[slot, kind], qkv_sem.at[slot, kind]
            )
            for kind in range(3)
        ] + [
            pltpu.make_async_copy(
                src.at[:, pl.ds(pl.multiple_of(p * 128, 128), 128)],
                qkv.at[slot, kind],
                qkv_sem.at[slot, kind],
            )
            for kind, src in ((3, mixed_h), (4, grad_mixed_h))
        ]

    for c in pair_copies(0, 0):
        c.start()
    normed_copy = pltpu.make_async_copy(normed_h, dtok, w_sem.at[1])
    normed_copy.start()
    greet(n_dp, n_seq)

    def reducer(i, grad, own, local):
        acc, core_in, steps, z_in = sets[i]
        sems = {
            "core": (c_send.at[i], c_recv.at[i], c_local.at[i]),
            "step": (s_send.at[i], s_recv.at[i]),
            "z": (z_send.at[i], z_recv.at[i]),
        }
        return GradReduce(grad, own, local, core_in, steps, z_in, sems, n_dp, n_seq)

    acc_r = sets[0][0]
    rest = reducer(
        0,
        grad_rest,
        lambda lead, z, cols: acc_r.at[tuple(lead) + (z, slice(None), cols)],
        True,
    )

    def chunk_reducer(c):
        stage = sets[1 + c][0]
        return reducer(
            1 + c,
            stage,
            lambda lead, z, cols: stage.at[tuple(lead) + (core, z, slice(None), cols)],
            False,
        )

    parts = [chunk_reducer(c) for c in range(chunks)]
    order = [0, n_seq - 1] + list(range(1, n_seq - 1))
    for z in order:
        rest.core_start(z)

    def down_copy(z):
        return remote(
            down_h.at[z], down_in.at[s], down_send.at[z], down_recv.at[s], d, z
        )

    down_own = pltpu.make_async_copy(down_h.at[s], down_in.at[s], down_send.at[s])
    down_own.start()
    for z in range(n_seq):

        @pl.when(z != s)
        def _():
            down_copy(z).start()

    w_copy = pltpu.make_async_copy(wq_h, w, w_sem.at[0])
    w_copy.start()
    returned = RowReturn(dtok, dtok_o, row_send, row_recv, rows, n_seq)

    normed_copy.wait()
    for r in range(n_seq):
        normed_t[:, pl.ds(r * length, length)] = jnp.transpose(dtok[r])

    def weight_chunk(c):
        stage = sets[1 + c][0]
        n = width // chunks
        lead = stage.shape[:-2]
        for kind in range(3):
            g = dot(
                normed_t[...],
                grad_qkv[:, kind * width + c * n : kind * width + (c + 1) * n],
                ((1,), (0,)),
            )
            for i in range(n_dp * n_seq):
                k, idx = i, []
                for size in lead[::-1]:
                    idx.append(k % size)
                    k //= size
                stage[tuple(idx[::-1]) + (slice(None), pl.ds(kind * n, n))] = g[
                    i * depth : (i + 1) * depth
                ].astype(BF16)
        for z in range(n_seq):
            parts[c].core_start(z)

    def chunk_event(c, t):
        for z in range(n_seq):
            if t == 0:
                parts[c].core_add(z)
            parts[c].event(z, t)

    def run(what, *args):
        if what == "add":
            rest.core_add(order[args[0]])
        elif what == "rest":
            rest.event(order[args[0]], args[1])
        elif what == "grad":
            weight_chunk(*args)
        else:
            chunk_event(*args)

    run("add", 0)
    run("rest", 0, 0)
    run("add", 1)
    run("rest", 1, 0)
    slots = {
        0: [("add", 2), ("add", 3)],
        1: [("rest", 0, 1), ("rest", 2, 0)],
        2: [("rest", 1, 1), ("rest", 3, 0)],
        3: [("rest", 0, 2), ("grad", 0)],
        4: [("rest", 2, 1), ("rest", 1, 2), ("chunk", 0, 0)],
        5: [("rest", 3, 1)],
        6: [("rest", 2, 2), ("chunk", 0, 1)],
        7: [("rest", 3, 2), ("grad", 1)],
        8: [("chunk", 0, 2), ("chunk", 1, 0)],
        10: [("chunk", 1, 1)],
        11: [("chunk", 1, 2), ("grad", 2)],
    }
    tail = [[("chunk", 2, 0)], [], [("chunk", 2, 1)], []]
    block = seq_len // 2
    lane = lax.broadcasted_iota(jnp.int32, (seq_len, 128), 1)
    if m != 2:
        slots, tail = {3: [("grad", 0)], 7: [("grad", 1)], 11: [("grad", 2)]}, []

    @pl.loop(0, pairs)
    def _(p):
        now = lax.rem(p, 2)

        @pl.when(p + 1 < pairs)
        def _():
            for c in pair_copies(p + 1, 1 - now):
                c.start()

        for c in pair_copies(p, now):
            c.wait()
        queries, keys, values = qkv[now, 0], qkv[now, 1], qkv[now, 2]
        at_p = pl.ds(pl.multiple_of(p * 128, 128), 128)
        grads = qkv[now, 4]
        product = grads.astype(F32) * qkv[now, 3].astype(F32)
        nothing = jnp.zeros_like(grads)
        keys_t[...] = jnp.transpose(keys)
        for j in range(2):
            own = lanes_of(j, grads.shape)
            base = HEAD_DIM * (1 - j) + 8

            def with_terms(x, other, column):
                for n, term in enumerate(split3(column)):
                    other = jnp.where(lane == base + n, term, other)
                return jnp.where(own, x, other)

            inner = jnp.sum(jnp.where(own, product, 0.0), -1, keepdims=True)
            stat = jnp.sum(jnp.where(lane == 2 * p + j, lse[...], 0.0), -1, keepdims=True)
            g2[j] = with_terms(grads, nothing, -inner)
            q2[j] = with_terms(queries, docs[1], -stat)
            k2[j] = jnp.where(own, keys, docs[0])
            v2[j] = jnp.where(own, values, docs[0])
        for i in range(seq_len // block):
            at = pl.ds(i * block, block)
            dvs, dks = [], []
            for j in range(2):
                probs = jnp.exp2(dot(k2[j, at, :], q2[j], ((1,), (1,))))
                ds = probs * dot(v2[j, at, :], g2[j], ((1,), (1,)))
                ds = ds.astype(BF16)
                dvs.append(dot(probs.astype(BF16), grads, ((1,), (0,))))
                dks.append(dot(ds, queries, ((1,), (0,))))
                dq = dot(keys_t[:, at], ds, ((1,), (0,)))
                if i == 0:
                    dq2[j] = dq
                else:
                    dq2[j] += dq
            here = lanes_of(0, dvs[0].shape)
            dk = jnp.where(here, dks[0], dks[1]) * (1.0 / LOG2E)
            grad_qkv[at, pl.ds(pl.multiple_of(width + p * 128, 128), 128)] = (
                dk * cos[at, :] + swap_halves(dk * sin[at, :])
            ).astype(BF16)
            grad_qkv[at, pl.ds(pl.multiple_of(2 * width + p * 128, 128), 128)] = jnp.where(
                here, dvs[0], dvs[1]
            ).astype(BF16)
            if i == seq_len // block - 1:
                row = lax.broadcasted_iota(jnp.int32, dq2.shape[1:], 0)
                dq = jnp.where(row < HEAD_DIM, dq2[0], dq2[1])
                dq = jnp.transpose(dq) * (1.0 / math.sqrt(HEAD_DIM))
                grad_qkv[:, at_p] = (dq * cos[...] + swap_halves(dq * sin[...])).astype(
                    BF16
                )
            for slot, events in slots.items():
                if slot % 2 != i:
                    continue

                @pl.when(p == slot // 2)
                def _():
                    for e in events:
                        run(*e)

    w_copy.wait()
    gain = mod[6:7, :]
    scale = 1.0 + mod[1:2, :]
    gmod[...] = gm_in[...]
    offs = [n_seq // 2] + [off for off in range(1, n_seq) if off != n_seq // 2] + [0]
    for r, off in enumerate(offs):
        to = lax.rem(s + off, n_seq)
        at = pl.ds(pl.multiple_of(to * length, length), length)
        e = dot(grad_qkv[at, :], w[...], ((1,), (1,)))
        normal, rstd = normalise(tok[at, :].astype(F32))
        gmod[0:1, :] += jnp.sum(e, 0, keepdims=True)
        weighted = jnp.sum(e * normal, 0, keepdims=True)
        gmod[1:2, :] += weighted * gain
        gmod[6:7, :] += weighted * scale
        h = e * (gain * scale)
        mean_h = jnp.mean(h, -1, keepdims=True)
        mean_hz = jnp.mean(h * normal, -1, keepdims=True)
        dtok[to] = (grad_mid[at, :] + (h - mean_h - normal * mean_hz) * rstd).astype(BF16)
        if r < n_seq // 2:
            returned.start([off])
        if r < len(tail):
            for e in tail[r]:
                run(*e)

    own_row = pltpu.make_async_copy(gmod, gmod_o.at[d, mine], g_send.at[0])

    def group_copy(off):
        return remote(
            gmod,
            gmod_o.at[d, mine],
            g_send.at[off],
            g_recv.at[s],
            d,
            lax.rem(s + off, n_seq),
        )

    @pl.when(active)
    def _():
        own_row.start()
        for off in range(1, n_seq):
            group_copy(off).start()

    if m != 2:
        for n in range(n_seq):
            if n > 1:
                run("add", n)
                run("rest", n, 0)
        for t in range(1, m + 1):
            for n in range(n_seq):
                run("rest", n, t)
        for c in range(chunks):
            for t in range(m + 1):
                run("chunk", c, t)
    returned.start(offs[n_seq // 2 :])
    if m == 2:
        run("chunk", 2, 2)

    @pl.when(active)
    def _():
        own_row.wait()

    for i in range(rows):
        owner = first + i

        @pl.when(owner != s)
        def _():
            remote(
                gmod, gmod_o.at[d, i], g_send.at[0], g_recv.at[owner], d, owner
            ).wait_recv()

    def dp_copy(off):
        return remote(
            gmod_o.at[d], gmod_o.at[d], gd_send.at[off], gd_recv.at[off], xor(d, off), s
        )

    for off in range(1, n_dp):
        dp_copy(off).start()

    total = rest.total()
    go_o[...] = total[:, :width]
    gu_o[...] = total[:, width : width + hidden]
    down_own.wait()
    for off in range(1, n_seq):
        origin = lax.rem(s + off, n_seq)
        remote(
            down_h.at[s],
            down_in.at[origin],
            down_send.at[origin],
            down_recv.at[origin],
            d,
            origin,
        ).wait_recv()
    total = down_in[0].astype(F32)
    for z in range(1, n_seq):
        total += down_in[z].astype(F32)
    for i in range(hidden // width):
        gd_o[i * depth : (i + 1) * depth, :] = total[:, i * width : (i + 1) * width]
    n = width // chunks
    for c in range(chunks):
        total = parts[c].total()
        for kind in range(3):
            gq_o[:, kind * width + c * n : kind * width + (c + 1) * n] = total[
                :, kind * n : (kind + 1) * n
            ]

    for off in range(1, n_dp):
        e = xor(d, off)
        dp_copy(off).wait_send()
        remote(
            gmod_o.at[e], gmod_o.at[e], gd_send.at[off], gd_recv.at[off], e, s
        ).wait_recv()

    @pl.when(active)
    def _():
        for off in range(1, n_seq):
            group_copy(off).wait_send()

    returned.finish()
    for z in range(n_seq):

        @pl.when(z != s)
        def _():
            down_copy(z).wait_send()

    rest.sent()
    for p in parts:
        p.sent()


def back(n_dp, n_seq, rows, hidden, grad_rest, grad_down, hbm_args, vmem_args):
    dma = pltpu.SemaphoreType.DMA
    struct = jax.ShapeDtypeStruct
    m = n_dp.bit_length() - 2
    lead = (2,) * m
    length, width = hbm_args[-1].shape[1:]
    seq_len = length * n_seq
    depth, wide = grad_rest.shape[-2:]
    gmod = vmem_args[-1]
    chunks = 3
    outs = [
        struct((depth, 3 * width), F32),
        struct((depth, width), F32),
        struct((depth, hidden), F32),
        struct((depth * hidden // width, width), F32),
        struct((rows, length, width), BF16),
        struct((n_dp, rows) + gmod.shape, F32),
    ]

    def reduce_scratch(n, acc):
        slabs = [
            pltpu.VMEM(acc + (n_seq, depth, n), BF16),
            pltpu.VMEM(lead + (n_seq, depth, n), BF16),
            pltpu.VMEM((n_seq, depth, n), BF16),
        ]
        for _ in range(2):
            for step in range(m):
                slabs.append(
                    pltpu.VMEM(
                        (n_seq,) + (2,) * (m - 1 - step) + (depth, n // 2), BF16
                    )
                )
        return slabs

    scratch = reduce_scratch(wide, lead)
    for _ in range(chunks):
        scratch += reduce_scratch(3 * width // chunks, lead + (2,))
    count = 1 + chunks
    scratch += (
        [
            pltpu.VMEM(grad_down.shape, BF16),
            pltpu.VMEM((width, 3 * width), BF16),
            pltpu.VMEM((2, 5, seq_len, 128), BF16),
            pltpu.VMEM((width, seq_len), BF16),
            pltpu.VMEM((seq_len, 3 * width), BF16),
            pltpu.VMEM((n_seq, length, width), BF16),
        ]
        + [pltpu.VMEM((2, seq_len, 128), BF16)] * 4
        + [
            pltpu.VMEM((2, 128, seq_len), F32),
            pltpu.VMEM((128, seq_len), BF16),
            pltpu.VMEM(gmod.shape, F32),
            dma((2, 5)),
            dma((2,)),
            dma((n_seq,)),
            dma((rows,)),
            dma((n_seq,)),
            dma((n_seq,)),
            dma((n_dp,)),
            dma((n_dp,)),
            dma((count, n_seq)),
            dma((count, n_seq)),
            dma((count, n_seq)),
            dma((count, n_seq, 2, m)),
            dma((count, n_seq, 2, m)),
            dma((count, n_seq)),
            dma((count, n_seq)),
            dma((n_seq,)),
            dma((n_seq,)),
        ]
    )
    return pl.pallas_call(
        functools.partial(back_kernel, n_dp, n_seq, rows, hidden),
        out_shape=outs,
        in_specs=[ANY] * (2 + len(hbm_args)) + [VMEM] * len(vmem_args),
        out_specs=[VMEM] * 4 + [ANY] * 2,
        scratch_shapes=scratch,
        compiler_params=pltpu.CompilerParams(
            collective_id=1, has_side_effects=True, vmem_limit_bytes=VMEM_LIMIT
        ),
    )(grad_rest, grad_down, *hbm_args, *vmem_args)


def last_kernel(emb, gmods, *refs):
    count = len(refs) // 2 - 1
    grads = refs[:count]
    gwm_o, sum_o, *grads_o = refs[count:]
    n_dp, rows, _, width = gmods.shape
    depth = gwm_o.shape[0]
    features = jnp.transpose(emb[...].reshape(n_dp * 8, 128))[:depth]
    total = gmods[0, 0]
    for k in range(n_dp * rows):
        if k:
            total += gmods[k // rows, k % rows]
    sum_o[...] = total
    for p in range(6):
        acc = jnp.zeros((depth, width), F32)
        for k in range(n_dp * rows):
            e, i = k // rows, k % rows
            acc += features[:, e * 8 + i : e * 8 + i + 1] * gmods[e, i, p : p + 1, :]
        gwm_o[:, p * width : (p + 1) * width] = acc
    for g, o in zip(grads, grads_o):
        o[...] = g[...]


def last_call(emb, gmods, results, depth):
    width = gmods.shape[-1]
    struct = jax.ShapeDtypeStruct
    n = len(results)
    return pl.pallas_call(
        last_kernel,
        out_shape=[struct((depth, 6 * width), F32), struct((8, width), F32)]
        + [struct(g.shape, g.dtype) for g in results],
        in_specs=[VMEM] * (2 + n),
        out_specs=[VMEM] * (2 + n),
        compiler_params=pltpu.CompilerParams(vmem_limit_bytes=VMEM_LIMIT),
    )(emb, gmods, *results)


def rotary_tables(seq_len):
    half = HEAD_DIM // 2
    freq = np.exp(np.float32(-math.log(10000.0)) * np.arange(half, dtype=np.float32) / np.float32(half))
    angles = np.arange(seq_len, dtype=np.float32)[:, None] * freq.astype(np.float32)[None, :]
    cos = np.tile(np.cos(angles), (1, 4)).astype(np.float32)
    sin = np.sin(angles)
    sin = np.concatenate([-sin, sin, -sin, sin], 1).astype(np.float32)
    return jnp.asarray(cos), jnp.asarray(sin)


def time_embed(step_ids, model_dim):
    half_dim = model_dim // 2
    frequency = jnp.exp(-math.log(10000.0) * jnp.arange(half_dim, dtype=jnp.float32) / half_dim)
    angles = step_ids.astype(jnp.float32)[:, None] * frequency[None, :]
    return jnp.concatenate([jnp.cos(angles), jnp.sin(angles)], axis=-1)


def shards(
    n_dp,
    n_seq,
    tokens,
    segments,
    timesteps,
    w_mod,
    b_mod,
    gain_attn,
    w_qkv,
    w_out,
    gain_mlp,
    w_up,
    w_down,
    cotangent,
):
    rows, length, width = tokens.shape
    seq_len = length * n_seq
    hidden = w_up.shape[1]
    d, s = place()
    me = d * n_seq + s
    depth = w_mod.shape[0]
    cos, sin = rotary_tables(seq_len)

    emb = time_embed(timesteps, width).astype(BF16).astype(F32)
    emb = emb.reshape(rows, n_dp, n_seq, depth)
    emb = lax.dynamic_index_in_dim(emb, s, 2, keepdims=False).transpose(1, 0, 2)
    emb = jnp.pad(emb, ((0, 0), (0, 8 - rows), (0, 128 - depth)))
    n = n_dp * n_seq

    def in_place(vector):
        size = vector.shape[0]
        here = lax.broadcasted_iota(jnp.int32, (n, size), 0) == me
        return jnp.where(here, vector.astype(F32)[None, :], 0.0).reshape(-1, width)

    base = jnp.concatenate([in_place(v) for v in (b_mod, gain_attn, gain_mlp)], 0)
    seg = jnp.broadcast_to(segments[:, None, :], (rows, 8, length))

    down = [w_down[i * depth : (i + 1) * depth] for i in range(hidden // width)]
    tok, docs, normed_a, packed, wq, rest, group, mod, emb, mixed, lse = front(
        n_dp,
        n_seq,
        tokens,
        seg,
        emb,
        (w_qkv, jnp.concatenate([w_out, w_up], 1), jnp.concatenate(down, 1)),
        w_mod,
        base,
        cos,
        sin,
    )
    tok = tok.reshape(seq_len, width)
    out, grad_mid, grad_mixed, grad_rest, grad_down, gm_in = middle_call(
        n_dp, n_seq, mixed, tok, cotangent, rest, group, mod, width, hidden
    )
    g_wqkv, g_wout, g_wup, g_wdown, d_tok, gmods = back(
        n_dp,
        n_seq,
        rows,
        hidden,
        grad_rest,
        grad_down,
        (
            wq.reshape(width, 3 * width),
            packed,
            mixed,
            grad_mixed,
            normed_a.reshape(n_seq, length, width),
        ),
        (lse, docs, cos, sin, tok, grad_mid, mod, gm_in),
    )
    g_w_mod, summed, out, d_tok, g_wqkv, g_wout, g_wup, g_wdown = last_call(
        emb, gmods, (out, d_tok, g_wqkv, g_wout, g_wup, g_wdown), depth
    )
    summed = summed.reshape(8 * width)

    def own_part(vector, n):
        return lax.dynamic_slice_in_dim(vector, me * n, n, 0)

    return (
        out,
        d_tok,
        g_w_mod,
        own_part(summed[: 6 * width], b_mod.shape[0]),
        own_part(summed[6 * width : 7 * width], gain_attn.shape[0]),
        g_wqkv,
        g_wout,
        own_part(summed[7 * width :], gain_mlp.shape[0]),
        g_wup,
        g_wdown,
    )


def solution(mesh):
    both = P(("dp", "seq"))
    wide = P(("dp", "seq"), None)
    tokens = P("dp", "seq", None)
    return jax.shard_map(
        functools.partial(shards, mesh.shape["dp"], mesh.shape["seq"]),
        mesh=mesh,
        in_specs=(
            tokens,
            P("dp", "seq"),
            P("dp"),
            wide,
            both,
            both,
            wide,
            wide,
            both,
            wide,
            wide,
            tokens,
        ),
        out_specs=(tokens, tokens, wide, both, both, wide, wide, both, wide, wide),
        check_vma=False,
    )
```

```python
import functools
import math

import jax
import jax.numpy as jnp
import numpy as np
from jax import lax
from jax.experimental import pallas as pl
from jax.experimental.pallas import tpu as pltpu
from jax.sharding import PartitionSpec as P

HEAD_DIM = 64
EPSILON = 1e-06
MASK_FILL = -1e30
MESH = pl.DeviceIdType.MESH
BF16 = jnp.bfloat16
F32 = jnp.float32
ANY = pl.BlockSpec(memory_space=pl.ANY)
VMEM = pl.BlockSpec(memory_space=pltpu.VMEM)
VMEM_LIMIT = 60 * 2**20
LOG2E = math.log2(math.e)


def place():
    return lax.axis_index("dp"), lax.axis_index("seq")


def xor(index, bits):
    return jnp.bitwise_xor(index, bits)


def remote(src, dst, send, recv, dp, seq):
    return pltpu.make_async_remote_copy(
        src_ref=src,
        dst_ref=dst,
        send_sem=send,
        recv_sem=recv,
        device_id=(dp, seq),
        device_id_type=MESH,
    )


def greet(n_dp, n_seq):
    d, s = place()
    barrier = pltpu.get_barrier_semaphore()
    for off in range(1, n_dp):
        pl.semaphore_signal(
            barrier, inc=1, device_id=(xor(d, off), s), device_id_type=MESH
        )
    for off in range(1, n_seq):
        pl.semaphore_signal(
            barrier, inc=1, device_id=(d, lax.rem(s + off, n_seq)), device_id_type=MESH
        )
    pl.semaphore_wait(barrier, n_dp - 1 + n_seq - 1)


def bit_orders(n_dp):
    high = [1 << b for b in range(1, n_dp.bit_length() - 1)]
    return (high + [1], high[::-1] + [1])


def signed(value, sign):
    return value if sign > 0 else -value


class WeightGather:
    def __init__(self, shard, at, own_sem, z_sems, x_sems, cols, n_dp, n_seq):
        self.shard, self.at, self.own_sem = shard, at, own_sem
        self.z_sems, self.x_sems = z_sems, x_sems
        self.n_seq = n_seq
        self.cols = cols // 2
        self.orders = bit_orders(n_dp)
        self.steps = len(self.orders[0])
        self.groups = []
        for h in range(2):
            known = [(0, 0)]
            for step, bit in enumerate(self.orders[h]):
                known += [(off ^ bit, step + 1) for off, _ in known]
            self.groups.append(known)

    def own(self):
        d, s = place()
        return pltpu.make_async_copy(self.shard, self.at(d, s), self.own_sem)

    def z_copy(self, way, k):
        d, s = place()
        origin = s - signed(k - 1, way)
        side = 0 if way > 0 else 1
        send, recv = self.z_sems
        return remote(
            self.shard if k == 1 else self.at(d, origin),
            self.at(d, origin),
            send.at[side, k],
            recv.at[side, k],
            d,
            s + way,
        )

    def direct_copy(self, way, k):
        d, s = place()
        side = 0 if way > 0 else 1
        send, recv = self.z_sems
        return remote(
            self.shard,
            self.at(d, s),
            send.at[side, k],
            recv.at[side, k],
            d,
            s + signed(k, way),
        )

    def direct_each(self, body):
        d, s = place()
        for k in range(1, self.n_seq):
            for way in (1, -1):
                to = s + signed(k, way)

                @pl.when((to >= 0) & (to < self.n_seq))
                def _():
                    body(self.direct_copy(way, k))

    def z_valid(self, way, k):
        d, s = place()
        origin = s - signed(k - 1, way)
        to = s + way
        return (origin >= 0) & (origin < self.n_seq) & (to >= 0) & (to < self.n_seq)

    def half(self, ref, h):
        return ref.at[:, pl.ds(h * self.cols, self.cols)]

    def x_copy(self, origin, h, off, bit, src=None):
        d, s = place()
        dst = self.half(self.at(xor(d, off), origin), h)
        send, recv = self.x_sems
        return remote(
            dst if src is None else self.half(src, h),
            dst,
            send.at[origin, h, off ^ bit],
            recv.at[origin, h, off ^ bit],
            xor(d, bit),
            s,
        )

    def each(self, k, body):
        d, s = place()
        if k == 0:
            body(s, 0)
            return
        for way in (1, -1):
            origin = s - signed(k, way)

            @pl.when((origin >= 0) & (origin < self.n_seq))
            def _():
                body(origin, way)

    def z_start(self, k):
        for way in (1, -1):

            @pl.when(self.z_valid(way, k))
            def _():
                self.z_copy(way, k).start()

    def x_start(self, origin, src=None):
        for h in range(2):
            for bit in self.orders[h]:
                self.x_copy(origin, h, 0, bit, src).start()

    def own_start(self):
        d, s = place()
        self.own().start()
        self.x_start(s, self.shard)

    def passing(self, origin, t):
        for h in range(2):
            for off, step in self.groups[h]:
                if step != t:
                    continue
                self.x_copy(origin, h, off, 0).wait_recv()
                for bit in self.orders[h][t:]:
                    self.x_copy(origin, h, off, bit).start()

    def x_sent(self, origin):
        for h in range(2):
            for off, step in self.groups[h]:
                for bit in self.orders[h][step:]:
                    self.x_copy(origin, h, off, bit).wait_send()

    def event(self, k, t, forward=True, across=True):
        if t:
            self.each(k, lambda origin, way: self.passing(origin, t))
            return
        d, s = place()
        send, recv = self.z_sems

        def arrival(origin, way):
            side = 0 if way > 0 else 1
            remote(
                self.shard,
                self.at(d, origin),
                send.at[side, k],
                recv.at[side, k],
                d,
                s,
            ).wait_recv()
            if across:
                self.x_start(origin)

        self.each(k, arrival)
        if forward and k + 1 < self.n_seq:
            self.z_start(k + 1)

    def finish(self, direct=False, across=True):
        if direct:
            self.direct_each(lambda copy: copy.wait_send())
        else:
            for k in range(1, self.n_seq):
                for way in (1, -1):

                    @pl.when(self.z_valid(way, k))
                    def _():
                        self.z_copy(way, k).wait_send()

        if across:
            for k in range(self.n_seq):
                self.each(k, lambda origin, way: self.x_sent(origin))


def dot(a, b, dims):
    return lax.dot_general(a, b, (dims, ((), ())), preferred_element_type=F32)


def swap_halves(x):
    quarter = HEAD_DIM // 2
    lane = lax.broadcasted_iota(jnp.int32, x.shape, 1)
    return jnp.where(
        lax.rem(lane, HEAD_DIM) < quarter,
        pltpu.roll(x, 128 - quarter, axis=1),
        pltpu.roll(x, quarter, axis=1),
    )


def normalise(x):
    mean = jnp.mean(x, -1, keepdims=True)
    centred = x - mean
    var = jnp.mean(centred * centred, -1, keepdims=True)
    rstd = lax.rsqrt(var + EPSILON)
    return centred * rstd, rstd


def join_slabs(slabs, whole):
    depth = slabs.shape[-2]
    count = math.prod(slabs.shape[:-2])
    group = 16 // math.gcd(16, depth)

    @pl.loop(0, count // group)
    def _(i):
        parts = []
        for j in range(group):
            k, idx = i * group + j, []
            for n in slabs.shape[:-2][::-1]:
                idx.append(lax.rem(k, n))
                k = lax.div(k, n)
            parts.append(slabs[tuple(idx[::-1])])
        rows = group * depth
        whole[pl.ds(pl.multiple_of(i * rows, rows), rows), :] = jnp.concatenate(parts, 0)


def lanes_of(j, shape):
    lane = lax.broadcasted_iota(jnp.int32, shape, 1)
    return lax.div(lane, HEAD_DIM) == j


def front_kernel(n_dp, n_seq, rows, *refs):
    tokens, seg, emb_h, *shards = refs[:6]
    w_mod, base, cos, sin = refs[6:10]
    tok_o, doc_o, norm_o, pack_o, *fulls = refs[10:17]
    mod_o, emb, mixed_o, lse_o = refs[17:21]
    (
        tok,
        segs,
        docs,
        normed,
        packed,
        w_in,
        w,
        values,
        keys,
        mod_in,
        mod_sum,
        mod_row,
        out_sem,
        row_send,
        row_recv,
        mod_send,
        mod_recv,
        modz_send,
        modz_recv,
        own_sem,
        z_send,
        z_recv,
        x_send,
        x_recv,
        part,
        emb_send,
        emb_recv,
    ) = refs[21:]
    d, s = place()
    length, width = tokens.shape[1:]
    seq_len = length * n_seq
    first = lax.rem(d, 2)
    mine = s - first
    active = (mine >= 0) & (mine < rows)
    greet(n_dp, n_seq)

    def mod_copy(off):
        return remote(
            part.at[xor(d, off)],
            mod_in.at[d],
            mod_send.at[off],
            mod_recv.at[off],
            xor(d, off),
            s,
        )

    def emb_copy(off):
        return remote(
            emb_h.at[xor(d, off)],
            emb.at[d],
            emb_send.at[off],
            emb_recv.at[off],
            xor(d, off),
            s,
        )

    emb_own = pltpu.make_async_copy(emb_h.at[d], emb.at[d], emb_send.at[0])
    emb_own.start()
    for off in range(1, n_dp):
        emb_copy(off).start()

    ats = [
        lambda e, z: fulls[0].at[e, z],
        lambda e, z: fulls[1].at[e, z],
        lambda e, z: fulls[2].at[z],
    ]
    qkv, rest, down = [
        WeightGather(
            shards[i],
            ats[i],
            own_sem.at[i],
            (z_send.at[i], z_recv.at[i]),
            (x_send.at[i], x_recv.at[i]) if i < 2 else None,
            shards[i].shape[1],
            n_dp,
            n_seq,
        )
        for i in range(3)
    ]
    qkv.direct_each(lambda copy: copy.start())
    rest.z_start(1)
    down.z_start(1)
    down.own().start()
    qkv.own_start()

    emb_own.wait()
    for off in range(1, n_dp):
        e = xor(d, off)
        remote(
            emb_h.at[d], emb.at[e], emb_send.at[off], emb_recv.at[off], d, s
        ).wait_recv()
    features = emb[...].reshape(n_dp * 8, 128)[:, : w_mod.shape[0]].astype(BF16)
    for k in range(8):
        if k < 6:
            terms = dot(features, w_mod[:, k * width : (k + 1) * width], ((1,), (0,)))
            terms = terms + base[k : k + 1, :]
        for e in range(n_dp):
            for i in range(rows):
                part[e, i, k : k + 1, :] = (
                    terms[e * 8 + i : e * 8 + i + 1] if k < 6 else base[k : k + 1, :]
                )
    for off in range(1, n_dp):
        mod_copy(off).start()

    trio = ((tokens, tok), (seg, segs))

    def row_local(k, i):
        src, dst = trio[k]
        return pltpu.make_async_copy(src.at[i], dst.at[s], row_send.at[k, i])

    def row_remote(k, i):
        src, dst = trio[k]
        return remote(
            src.at[i], dst.at[s], row_send.at[k, i], row_recv.at[k, s], d, first + i
        )

    def row_start(k):
        for i in range(rows):

            @pl.when(first + i == s)
            def _():
                row_local(k, i).start()

            @pl.when(first + i != s)
            def _():
                row_remote(k, i).start()

    def row_sent(k):
        for i in range(rows):

            @pl.when(first + i != s)
            def _():
                row_remote(k, i).wait_send()

    def row_arrival(k, origin):
        src, dst = trio[k]
        remote(
            src.at[0],
            dst.at[origin],
            row_send.at[k, 0],
            row_recv.at[k, origin],
            d,
            origin,
        ).wait_recv()

    def row_own(k):
        for i in range(rows):

            @pl.when(first + i == s)
            def _():
                row_local(k, i).wait()

    def mod_exchange():
        for off in range(1, n_dp):
            remote(
                part.at[d],
                mod_in.at[xor(d, off)],
                mod_send.at[off],
                mod_recv.at[off],
                d,
                s,
            ).wait_recv()
        total = part[d]
        for off in range(1, n_dp):
            total += mod_in[xor(d, off)]
        mod_sum[...] = total
        for i in range(rows):

            @pl.when(first + i == s)
            def _():
                mod_row[s] = mod_sum[i]

            @pl.when(first + i != s)
            def _():
                remote(
                    mod_sum.at[i],
                    mod_row.at[s],
                    modz_send.at[i],
                    modz_recv.at[s],
                    d,
                    first + i,
                ).start()

    @pl.when(jnp.logical_not(active))
    def _():
        tok[...] = jnp.zeros_like(tok)
        segs[...] = jnp.zeros_like(segs)

    row_start(1)
    for k in range(1, n_seq):
        qkv.event(k, 0, forward=False)
    mod_exchange()
    row_start(0)
    for k in range(n_seq):
        qkv.event(k, 1)
    rest.own_start()
    rest.event(1, 0)
    down.event(1, 0, across=False)
    for t in range(2, qkv.steps + 1):
        for k in range(n_seq):
            qkv.event(k, t)
    stage = pltpu.make_async_copy(fulls[0], w_in, out_sem.at[0])
    qkv.own().wait()
    stage.start()

    @pl.when(active)
    def _():
        for off in range(1, n_seq):
            row_arrival(1, lax.rem(s + off, n_seq))

    row_own(1)
    lane = lax.broadcasted_iota(jnp.int32, (length, 128), 1)
    lane = lax.rem(lane, HEAD_DIM).astype(F32)
    for z in range(n_seq):
        ids = jnp.transpose(
            jnp.broadcast_to(segs[z, 0:1, :].astype(F32), (128, length))
        )
        same = ids == lane
        at = pl.ds(z * length, length)
        docs[0, at, :] = jnp.where(
            same | ((lane >= 8.0) & (lane < 11.0)), 1.0, 0.0
        ).astype(BF16)
        docs[1, at, :] = jnp.where(same | (lane >= 8.0), 0.0, MASK_FILL).astype(BF16)
    doc_copy = pltpu.make_async_copy(docs, doc_o, out_sem.at[1])
    doc_copy.start()

    stage.wait()
    depth = w_in.shape[2]

    join_slabs(w_in, w)

    @pl.when(active)
    def _():
        for off in range(1, n_seq):
            origin = lax.rem(s + off, n_seq)
            remote(
                mod_sum.at[0],
                mod_row.at[origin],
                modz_send.at[0],
                modz_recv.at[origin],
                d,
                origin,
            ).wait_recv()
        total = mod_row[0]
        for z in range(1, n_seq):
            total += mod_row[z]
        mod_o[...] = total

    @pl.when(jnp.logical_not(active))
    def _():
        mod_o[...] = jnp.zeros_like(mod_o)

    rest.event(0, 1)

    gain = mod_o[6:7, :] * (1.0 + mod_o[1:2, :])
    shift = mod_o[0:1, :]
    row_own(0)
    for off in range(n_seq):
        z = lax.rem(s + off, n_seq)
        if off:

            @pl.when(active)
            def _():
                row_arrival(0, z)

        normal, _ = normalise(tok[z].astype(F32))
        at = pl.ds(pl.multiple_of(z * length, length), length)
        normed[at, :] = (normal * gain + shift).astype(BF16)
    outs = [
        pltpu.make_async_copy(tok, tok_o, out_sem.at[2]),
        pltpu.make_async_copy(normed, norm_o, out_sem.at[3]),
    ]
    for c in outs:
        c.start()

    early = [[(0, 2), (1, 1)], [(2, 0)], [(0, 3)]]
    for kind in range(3):

        @pl.loop(0, width // 256)
        def _(c):
            col = kind * width + c * 256
            wc = w[:, pl.ds(pl.multiple_of(col, 256), 256)]
            for r in range(seq_len // 256):
                at = pl.ds(r * 256, 256)
                y = dot(normed[at, :], wc, ((1,), (0,)))
                for j in range(2):
                    p = y[:, j * 128 : (j + 1) * 128]
                    if kind < 2:
                        p = p * cos[at, :] + swap_halves(p) * sin[at, :]
                    if kind == 0:
                        p = p * (LOG2E / math.sqrt(HEAD_DIM))
                    packed[kind * (width // 128) + c * 2 + j, at, :] = p.astype(BF16)

        for e in early[kind]:
            rest.event(*e)
            if e == (2, 0):
                down.event(2, 0, across=False)

    pack_copy = pltpu.make_async_copy(packed, pack_o, out_sem.at[4])
    pack_copy.start()
    pairs = width // 128
    slots = {
        0: [(1, 2)],
        1: [(2, 1), (3, 0)],
        2: [(1, 3)],
        3: [(2, 2), (3, 1)],
        4: [(3, 2)],
    }
    done = {e for v in slots.values() for e in v}
    done |= {e for v in early for e in v} | {(1, 0), (0, 1)}

    values[:, 128:] = jnp.ones((seq_len, 128), BF16)
    block = 128
    lse_o[...] = jnp.zeros_like(lse_o)

    @pl.loop(0, pairs)
    def _(p):
        k = packed[pairs + p]
        values[:, :128] = packed[2 * pairs + p]
        for j in range(2):
            keys[j] = jnp.where(lanes_of(j, k.shape), k, docs[0])
        for i in range(seq_len // block):
            at = pl.ds(i * block, block)
            q = packed[p, at, :]
            both = []
            stats = lse_o[at, :]
            lane = lax.broadcasted_iota(jnp.int32, (block, 128), 1)
            for j in range(2):
                own = lanes_of(j, q.shape)
                scores = dot(jnp.where(own, q, docs[1, at, :]), keys[j], ((1,), (1,)))
                top = jnp.max(scores, -1, keepdims=True)
                e = jnp.exp2(scores - top).astype(BF16)
                o = dot(e, values[...], ((1,), (0,)))
                total = o[:, 128:]
                both.append(o[:, :128] / total)
                stats = jnp.where(lane == 2 * p + j, top + jnp.log2(total), stats)
            lse_o[at, :] = stats
            mixed_o[at, pl.ds(pl.multiple_of(p * 128, 128), 128)] = jnp.where(
                lane < HEAD_DIM, both[0], both[1]
            ).astype(BF16)
        for slot, events in slots.items():

            @pl.when(p == slot)
            def _():
                for k, t in events:
                    rest.event(k, t)
                    if (k, t) == (3, 0):
                        down.event(3, 0, across=False)

    for t in range(1, rest.steps + 1):
        for k in range(n_seq):
            if (k, t) not in done:
                rest.event(k, t)

    for i in range(rows):

        @pl.when(first + i != s)
        def _():
            remote(
                mod_sum.at[i], mod_row.at[s], modz_send.at[i], modz_recv.at[s], d, first + i
            ).wait_send()

    for off in range(1, n_dp):
        mod_copy(off).wait_send()
    rest.own().wait()
    down.own().wait()
    for c in outs + [doc_copy, pack_copy]:
        c.wait()

    for k in range(2):
        row_sent(k)
    for off in range(1, n_dp):
        emb_copy(off).wait_send()
    qkv.finish(direct=True)
    rest.finish()
    down.finish(across=False)


def front(n_dp, n_seq, tokens, seg, emb, shards, w_mod, base, cos, sin):
    rows, length, width = tokens.shape
    seq_len = length * n_seq
    dma = pltpu.SemaphoreType.DMA
    struct = jax.ShapeDtypeStruct
    pairs = width // 128
    outs = [
        struct((n_seq, length, width), BF16),
        struct((2, seq_len, 128), BF16),
        struct((seq_len, width), BF16),
        struct((3 * pairs, seq_len, 128), BF16),
    ]
    outs += [struct((n_dp, n_seq) + w.shape, BF16) for w in shards[:2]]
    outs += [
        struct((n_seq,) + shards[2].shape, BF16),
        struct((8, width), F32),
        struct(emb.shape, F32),
        struct((seq_len, width), BF16),
        struct((seq_len, 128), F32),
    ]
    return pl.pallas_call(
        functools.partial(front_kernel, n_dp, n_seq, rows),
        out_shape=outs,
        in_specs=[ANY] * 6 + [VMEM] * 4,
        out_specs=[ANY] * 7 + [VMEM] * 4,
        scratch_shapes=[
            pltpu.VMEM((n_seq, length, width), BF16),
            pltpu.VMEM((n_seq,) + seg.shape[1:], jnp.int32),
            pltpu.VMEM((2, seq_len, 128), BF16),
            pltpu.VMEM((seq_len, width), BF16),
            pltpu.VMEM((3 * pairs, seq_len, 128), BF16),
            pltpu.VMEM((n_dp, n_seq) + shards[0].shape, BF16),
            pltpu.VMEM((width, 3 * width), BF16),
            pltpu.VMEM((seq_len, 256), BF16),
            pltpu.VMEM((2, seq_len, 128), BF16),
            pltpu.VMEM((n_dp, rows, 8, width), F32),
            pltpu.VMEM((rows, 8, width), F32),
            pltpu.VMEM((n_seq, 8, width), F32),
            dma((5,)),
            dma((2, rows)),
            dma((2, n_seq)),
            dma((n_dp,)),
            dma((n_dp,)),
            dma((rows,)),
            dma((n_seq,)),
            dma((3,)),
            dma((3, 2, n_seq)),
            dma((3, 2, n_seq)),
            dma((2, n_seq, 2, n_dp)),
            dma((2, n_seq, 2, n_dp)),
            pltpu.VMEM((n_dp, rows, 8, width), F32),
            dma((n_dp,)),
            dma((n_dp,)),
        ],
        compiler_params=pltpu.CompilerParams(
            collective_id=0, has_side_effects=True, vmem_limit_bytes=VMEM_LIMIT
        ),
    )(tokens, seg, emb, *shards, w_mod, base, cos, sin)


class GradReduce:
    def __init__(self, grad, own, local, core_in, step_in, z_in, sems, n_dp, n_seq):
        self.grad, self.own, self.local = grad, own, local
        self.core_in, self.step_in, self.z_in = core_in, step_in, z_in
        self.sems, self.n_seq = sems, n_seq
        self.bits = list(range(n_dp.bit_length() - 2, 0, -1))
        self.m = len(self.bits)
        self.orders = (list(range(self.m)), list(range(self.m))[::-1])
        self.cols = core_in.shape[-1] // 2

    def my(self, dim):
        d, _ = place()
        return lax.rem(lax.div(d, 1 << self.bits[dim]), 2)

    def mine(self):
        return tuple(self.my(dim) for dim in range(self.m))

    def index(self, done, flip=None):
        return tuple(
            self.my(dim)
            if dim in done
            else 1 - self.my(dim)
            if dim == flip
            else slice(None)
            for dim in range(self.m)
        )

    def core_copies(self, z):
        d, s = place()
        core = lax.rem(d, 2)
        lead = (slice(None),) * self.m
        send, recv, local = self.sems["core"]
        copies = [
            remote(
                self.grad.at[lead + (1 - core, z)],
                self.core_in.at[lead + (z,)],
                send.at[z],
                recv.at[z],
                xor(d, 1),
                s,
            )
        ]
        if self.local:
            copies.append(
                pltpu.make_async_copy(
                    self.grad.at[lead + (core, z)],
                    self.own(lead, z, slice(None)),
                    local.at[z],
                )
            )
        return copies

    def core_start(self, z):
        for c in self.core_copies(z):
            c.start()

    def core_add(self, z):
        for c in self.core_copies(z):
            c.wait()

        @pl.loop(0, 1 << self.m)
        def _(n):
            lead = tuple(
                lax.rem(lax.div(n, 1 << (self.m - 1 - dim)), 2) for dim in range(self.m)
            )
            target = self.own(lead, z, slice(None))
            target[...] = target[...] + self.core_in[lead + (z,)]

    def step_copy(self, z, h, step):
        d, s = place()
        order = self.orders[h]
        send, recv = self.sems["step"]
        cols = pl.ds(h * self.cols, self.cols)
        return remote(
            self.own(self.index(order[:step], order[step]), z, cols),
            self.step_in[h][step].at[z],
            send.at[z, h, step],
            recv.at[z, h, step],
            xor(d, 1 << self.bits[order[step]]),
            s,
        )

    def mine_at(self, z):
        return self.own(self.mine(), z, slice(None))

    def z_copy(self, z):
        d, s = place()
        send, recv = self.sems["z"]
        return remote(self.mine_at(z), self.z_in.at[s], send.at[z], recv.at[s], d, z)

    def event(self, z, t):
        for h in range(2):
            if t:
                self.step_copy(z, h, t - 1).wait()
                order = self.orders[h]
                cols = pl.ds(h * self.cols, self.cols)
                free = [dim for dim in range(self.m) if dim not in order[:t]]
                for n in range(1 << len(free)):
                    bits = [(n >> (len(free) - 1 - i)) & 1 for i in range(len(free))]
                    lead = tuple(
                        bits[free.index(dim)] if dim in free else self.my(dim)
                        for dim in range(self.m)
                    )
                    target = self.own(lead, z, cols)
                    target[...] = target[...] + self.step_in[h][t - 1][(z, *bits)]
            if t < self.m:
                self.step_copy(z, h, t).start()
        if t == self.m and self.z_in is not None:
            _, s = place()

            @pl.when(z != s)
            def _():
                self.z_copy(z).start()

    def total(self):
        d, s = place()
        send, recv = self.sems["z"]
        for off in range(1, self.n_seq):
            origin = lax.rem(s + off, self.n_seq)
            remote(
                self.mine_at(s),
                self.z_in.at[origin],
                send.at[origin],
                recv.at[origin],
                d,
                origin,
            ).wait_recv()
        total = self.mine_at(s)[...].astype(F32)
        for off in range(1, self.n_seq):
            total += self.z_in[lax.rem(s + off, self.n_seq)].astype(F32)
        return total

    def sent(self):
        _, s = place()
        for z in range(self.n_seq):

            @pl.when(z != s)
            def _():
                self.z_copy(z).wait_send()


def spread(k, dims):
    idx = []
    for n in dims[::-1]:
        idx.append(k % n if isinstance(k, int) else lax.rem(k, n))
        k = k // n if isinstance(k, int) else lax.div(k, n)
    return tuple(idx[::-1])


GELU_A = math.sqrt(2.0 / math.pi)
GELU_B = 0.044715 * GELU_A


def gelu_both(u):
    square = u * u
    half = 0.5 * jnp.tanh(u * (GELU_B * square + GELU_A)) + 0.5
    value = u * half
    slope = half + value * (1.0 - half) * (6.0 * GELU_B * square + 2.0 * GELU_A)
    return value, slope


class RowReturn:
    def __init__(self, src, dst, send, recv, rows, n_seq):
        self.src, self.dst, self.send, self.recv = src, dst, send, recv
        self.rows, self.n_seq = rows, n_seq
        d, s = place()
        self.first = lax.rem(d, 2)
        self.mine = s - self.first
        self.active = (self.mine >= 0) & (self.mine < rows)

    def local(self):
        _, s = place()
        return pltpu.make_async_copy(
            self.src.at[s], self.dst.at[self.mine], self.send.at[0]
        )

    def remote(self, off):
        d, s = place()
        to = lax.rem(s + off, self.n_seq)
        return remote(
            self.src.at[to],
            self.dst.at[self.mine],
            self.send.at[off],
            self.recv.at[self.mine],
            d,
            to,
        )

    def start(self, offs=None):
        @pl.when(self.active)
        def _():
            for off in range(self.n_seq) if offs is None else offs:
                if off:
                    self.remote(off).start()
                else:
                    self.local().start()

    def finish(self):
        d, s = place()

        @pl.when(self.active)
        def _():
            self.local().wait()
            for off in range(1, self.n_seq):
                self.remote(off).wait_send()

        for i in range(self.rows):

            @pl.when(self.first + i != s)
            def _():
                remote(
                    self.src.at[0],
                    self.dst.at[i],
                    self.send.at[0],
                    self.recv.at[i],
                    d,
                    self.first + i,
                ).wait_recv()


def middle_kernel(n_dp, n_seq, *refs):
    mixed_h, tok_h, cot_h, rest_h, group_h, mod = refs[:6]
    out_o, mid_h, gmixed_h, grad_h, down_h, gm = refs[6:12]
    m = n_dp.bit_length() - 2
    (
        wo,
        wu,
        wd,
        slabs,
        mixed,
        tok,
        cot,
        act,
        slope,
        normed,
        g_mlp,
        g_attn,
        turned,
        out,
        attn,
        mlp,
        sems,
        cot_send,
        cot_recv,
        row_send,
        row_recv,
        c_send,
        c_recv,
        s_send,
        s_recv,
        tiles,
        tile_sem,
        x_send,
        x_recv,
        own_sem,
        core_in,
        *steps,
    ) = refs[12:]
    d, s = place()
    rows = cot_h.shape[0]
    length = cot_h.shape[1]
    seq_len, width = mixed.shape
    hidden = wu.shape[1]
    depth = slabs.shape[-2]
    lead = slabs.shape[:-2]
    count = math.prod(lead)
    everything = (slice(None),) * len(lead)
    ways = hidden // width
    down = width + hidden
    first = lax.rem(d, 2)
    mine = s - first
    active = (mine >= 0) & (mine < rows)
    ins = [
        pltpu.make_async_copy(*args, sems.at[i])
        for i, args in enumerate(
            (
                (rest_h.at[:, pl.ds(0, width)], wo),
                (mixed_h, mixed),
                (tok_h, tok),
                (rest_h.at[:, pl.ds(width, hidden)], wu),
            )
        )
    ]
    for c in ins:
        c.start()
    greet(n_dp, n_seq)
    core = lax.rem(d, 2)
    sums = GradReduce(
        slabs,
        lambda idx, z, cols: slabs.at[tuple(idx) + (core, z, slice(None), cols)],
        False,
        core_in,
        (steps[:m], steps[m:]),
        None,
        {"core": (c_send, c_recv, None), "step": (s_send, s_recv)},
        n_dp,
        n_seq,
    )

    def slab_at(e, z):
        bits = [lax.rem(lax.div(e, 1 << b), 2) for b in range(len(lead) - 1)]
        return slabs.at[tuple(bits[::-1]) + (z,)]

    gather = WeightGather(
        None, slab_at, None, None, (x_send, x_recv), hidden, n_dp, n_seq
    )
    group_own = [
        pltpu.make_async_copy(group_h.at[z], slab_at(d, z), own_sem.at[z])
        for z in range(n_seq)
    ]
    for z in range(n_seq):
        gather.x_start(z, group_h.at[z])
        group_own[z].start()

    def cot_remote(i):
        return remote(
            cot_h.at[i], cot.at[s], cot_send.at[i], cot_recv.at[s], d, first + i
        )

    def cot_local(i):
        return pltpu.make_async_copy(cot_h.at[i], cot.at[s], cot_send.at[i])

    def cot_each(near, far):
        for i in range(rows):
            pl.when(first + i == s)(functools.partial(near, i))
            pl.when(first + i != s)(functools.partial(far, i))

    cot_each(lambda i: cot_local(i).start(), lambda i: cot_remote(i).start())

    @pl.when(jnp.logical_not(active))
    def _():
        cot[...] = jnp.zeros_like(cot)

    for c in ins:
        c.wait()

    shift = mod[3:4, :]
    gain = mod[7:8, :]
    scale = 1.0 + mod[4:5, :]
    gate_a = mod[2:3, :]
    gate_m = mod[5:6, :]
    gm[...] = jnp.zeros_like(gm)
    chunk = 1024
    block = 2 * length
    blocks = [(pl.ds(r * block, block), pl.ds(r * 2, 2)) for r in range(n_seq // 2)]
    three = (2, length, width)

    def middle_of(at):
        return tok[at, :].astype(F32) + gate_a * attn[at, :]

    half = n_seq // 2
    gather_events = [[(z, 1) for z in range(half)], [(z, 1) for z in range(half, n_seq)]]
    gather_events += [
        [(z, t) for z in range(n_seq)] for t in range(2, gather.steps + 1)
    ]
    for at, _ in blocks:
        attn[at, :] = dot(mixed[at, :], wo[...], ((1,), (0,)))
        normal, _ = normalise(middle_of(at))
        normed[at, :] = (normal * (gain * scale) + shift).astype(BF16)

        @pl.loop(0, hidden // chunk)
        def _(c):
            cols = pl.ds(pl.multiple_of(c * chunk, chunk), chunk)
            value, steep = gelu_both(dot(normed[at, :], wu[:, cols], ((1,), (0,))))
            act[at, cols] = value.astype(BF16)
            slope[at, cols] = steep.astype(BF16)

        if gather_events:
            for z, t in gather_events.pop(0):
                gather.passing(z, t)

    def turn(left):
        for r in range(seq_len // 256):
            at = pl.ds(r * 256, 256)
            turned[:, at] = jnp.transpose(left[at, :])

    turn(normed)
    for events in gather_events:
        for z, t in events:
            gather.passing(z, t)
    for z in range(n_seq):
        gather.x_sent(z)
        group_own[z].wait()
    group = 16 // math.gcd(16, depth * ways)

    @pl.loop(0, count // group)
    def _(i):
        parts = [
            slabs[spread(i * group + j, lead) + (slice(None), pl.ds(k * width, width))]
            for j in range(group)
            for k in range(ways)
        ]
        n = group * depth * ways
        wd[pl.ds(pl.multiple_of(i * n, n), n), :] = jnp.concatenate(parts, 0)

    for at, two in blocks:
        mlp_out = dot(act[at, :], wd[...], ((1,), (0,)))
        mlp[at, :] = mlp_out.astype(BF16)
        out[two] = (middle_of(at) + gate_m * mlp_out).astype(BF16).reshape(three)
    returned = RowReturn(out, out_o, row_send, row_recv, rows, n_seq)

    cot_each(lambda i: cot_local(i).wait(), lambda i: None)

    @pl.when(active)
    def _():
        for off in range(1, n_seq):
            origin = lax.rem(s + off, n_seq)
            remote(
                cot_h.at[0],
                cot.at[origin],
                cot_send.at[0],
                cot_recv.at[origin],
                d,
                origin,
            ).wait_recv()

    for at, two in blocks:
        grad = cot[two].reshape(block, width).astype(F32)
        g_mlp[at, :] = (grad * gate_m).astype(BF16)
        gm[5:6, :] += jnp.sum(grad * mlp[at, :].astype(F32), 0, keepdims=True)

    several = math.lcm(128, depth * ways) // (depth * ways)

    @pl.loop(0, count // several)
    def _(i):
        n = several * depth * ways
        at = pl.ds(pl.multiple_of(i * n, n), n)
        g = dot(act[:, at], g_mlp[...], ((0,), (0,)))
        for j in range(several):
            for k in range(ways):
                row = (j * ways + k) * depth
                slabs[
                    spread(i * several + j, lead) + (slice(None), pl.ds(k * width, width))
                ] = g[row : row + depth].astype(BF16)

    returned.start()
    for z in range(n_seq):
        sums.core_start(z)
    todo = [[("add", z) for z in range(n_seq)] + [(z, 0) for z in range(n_seq)]]
    todo += [[(z, t) for z in range(n_seq)] for t in range(1, m + 1)]

    def proceed():
        for z, t in todo.pop(0) if todo else []:
            if z == "add":
                sums.core_add(t)
            else:
                sums.event(z, t)

    for b, (at, two) in enumerate(blocks):
        grad = cot[two].reshape(block, width).astype(F32)

        @pl.loop(0, hidden // chunk)
        def _(c):
            cols = pl.ds(pl.multiple_of(c * chunk, chunk), chunk)
            g_act = dot(g_mlp[at, :], wd[cols, :], ((1,), (1,)))
            slope[at, cols] = (g_act * slope[at, cols].astype(F32)).astype(BF16)

        e = dot(slope[at, :], wu[...], ((1,), (1,)))
        if b == 0:
            proceed()
        gm[3:4, :] += jnp.sum(e, 0, keepdims=True)
        normal, rstd = normalise(middle_of(at))
        weighted = jnp.sum(e * normal, 0, keepdims=True)
        gm[4:5, :] += weighted * gain
        gm[7:8, :] += weighted * scale
        h = e * (gain * scale)
        mean_h = jnp.mean(h, -1, keepdims=True)
        mean_hz = jnp.mean(h * normal, -1, keepdims=True)
        g_mid = grad + (h - mean_h - normal * mean_hz) * rstd
        mlp[at, :] = g_mid.astype(BF16)
        gm[2:3, :] += jnp.sum(g_mid * attn[at, :], 0, keepdims=True)
        g_attn[at, :] = (g_mid * gate_a).astype(BF16)
        g_mixed = dot(g_attn[at, :], wo[...], ((1,), (1,)))
        cot[two] = g_mixed.astype(BF16).reshape(three)
    proceed()

    outs = [
        pltpu.make_async_copy(*args, sems.at[i])
        for i, args in enumerate(((mlp, mid_h), (cot, gmixed_h)))
    ]
    for c in outs:
        c.start()

    tile = 256

    def tile_copy(slot, col):
        return pltpu.make_async_copy(
            tiles.at[slot],
            grad_h.at[everything + (slice(None), pl.ds(col, tile))],
            tile_sem.at[slot],
        )

    def weight_grad(right, start, n, busy):
        @pl.loop(0, n // tile)
        def _(c):
            col = pl.multiple_of(c * tile, tile)
            slot = lax.rem(c, 2)
            g = dot(turned[...], right[:, pl.ds(col, tile)], ((1,), (0,)))

            @pl.when((c >= 2) | busy)
            def _():
                tile_copy(slot, 0).wait()

            for i in range(count):
                tiles[(slot,) + spread(i, lead)] = g[
                    i * depth : (i + 1) * depth
                ].astype(BF16)
            tile_copy(slot, pl.multiple_of(start + col, tile)).start()

    weight_grad(slope, width, hidden, False)
    proceed()
    turn(mixed)
    weight_grad(g_attn, 0, width, True)
    while todo:
        proceed()
    reduced = []
    for z in range(n_seq):
        reduced.append(
            pltpu.make_async_copy(sums.mine_at(z), down_h.at[z], c_send.at[z])
        )
        reduced[-1].start()
    for slot in range(2):
        tile_copy(slot, 0).wait()
    for c in outs + reduced:
        c.wait()
    cot_each(lambda i: None, lambda i: cot_remote(i).wait_send())
    returned.finish()


def middle_call(n_dp, n_seq, mixed, tok, cot, rest, group, mod, width, hidden):
    seq_len = mixed.shape[0]
    rows, length = cot.shape[:2]
    depth, wide = rest.shape[-2:]
    m = n_dp.bit_length() - 2
    lead = (2,) * m
    split = lead + (2, n_seq)
    struct = jax.ShapeDtypeStruct
    dma = pltpu.SemaphoreType.DMA
    row = pltpu.VMEM((seq_len, width), BF16)
    cut = pltpu.VMEM((n_seq, length, width), BF16)
    full = pltpu.VMEM((seq_len, hidden), BF16)
    steps = [
        pltpu.VMEM((n_seq,) + (2,) * (m - 1 - step) + (depth, hidden // 2), BF16)
        for _ in range(2)
        for step in range(m)
    ]
    out, mid, g_mixed, grads, down, gm = pl.pallas_call(
        functools.partial(middle_kernel, n_dp, n_seq),
        out_shape=[
            struct(cot.shape, BF16),
            struct((seq_len, width), BF16),
            struct((n_seq, length, width), BF16),
            struct(split + (depth, width + hidden), BF16),
            struct((n_seq, depth, hidden), BF16),
            struct(mod.shape, F32),
        ],
        in_specs=[ANY] * 5 + [VMEM],
        out_specs=[ANY] * 5 + [VMEM],
        scratch_shapes=[
            pltpu.VMEM((width, width), BF16),
            pltpu.VMEM((width, hidden), BF16),
            pltpu.VMEM((hidden, width), BF16),
            pltpu.VMEM(split + (depth, hidden), BF16),
            row,
            row,
            cut,
            full,
            full,
            row,
            row,
            row,
            pltpu.VMEM((width, seq_len), BF16),
            cut,
            pltpu.VMEM((seq_len, width), F32),
            row,
            dma((6,)),
            dma((rows,)),
            dma((n_seq,)),
            dma((n_seq,)),
            dma((rows,)),
            dma((n_seq,)),
            dma((n_seq,)),
            dma((n_seq, 2, m)),
            dma((n_seq, 2, m)),
            pltpu.VMEM((2,) + split + (depth, 256), BF16),
            dma((2,)),
            dma((n_seq, 2, n_dp)),
            dma((n_seq, 2, n_dp)),
            dma((n_seq,)),
            pltpu.VMEM(lead + (n_seq, depth, hidden), BF16),
            *steps,
        ],
        compiler_params=pltpu.CompilerParams(
            collective_id=2, has_side_effects=True, vmem_limit_bytes=VMEM_LIMIT
        ),
    )(
        mixed,
        tok,
        cot,
        rest.reshape(width, wide),
        group,
        mod,
    )
    return out, mid, g_mixed.reshape(seq_len, width), grads, down, gm


def split3(x):
    high = x.astype(BF16)
    x = x - high.astype(F32)
    middle = x.astype(BF16)
    low = (x - middle.astype(F32)).astype(BF16)
    return high, middle, low


def back_kernel(n_dp, n_seq, rows, hidden, *refs):
    grad_rest, down_h, wq_h, packed_h, mixed_h, grad_mixed_h, normed_h = refs[:7]
    lse, docs, cos, sin, tok, grad_mid, mod, gm_in = refs[7:15]
    gq_o, go_o, gu_o, gd_o = refs[15:19]
    dtok_o, gmod_o = refs[19:21]
    refs = refs[21:]
    m = n_dp.bit_length() - 2
    chunks = 3
    sets = []
    for _ in range(1 + chunks):
        acc, core_in, z_in = refs[:3]
        steps = (refs[3 : 3 + m], refs[3 + m : 3 + 2 * m])
        sets.append((acc, core_in, steps, z_in))
        refs = refs[3 + 2 * m :]
    (
        down_in,
        w,
        qkv,
        normed_t,
        grad_qkv,
        dtok,
        q2,
        k2,
        v2,
        g2,
        dq2,
        keys_t,
        gmod,
        qkv_sem,
        w_sem,
        row_send,
        row_recv,
        g_send,
        g_recv,
        gd_send,
        gd_recv,
        c_send,
        c_recv,
        c_local,
        s_send,
        s_recv,
        z_send,
        z_recv,
        down_send,
        down_recv,
    ) = refs
    d, s = place()
    length, width = dtok.shape[1:]
    depth = gq_o.shape[0]
    seq_len = length * n_seq
    pairs = width // 128
    first = lax.rem(d, 2)
    mine = s - first
    active = (mine >= 0) & (mine < rows)
    core = lax.rem(d, 2)

    def pair_copies(p, slot):
        return [
            pltpu.make_async_copy(
                packed_h.at[kind * pairs + p], qkv.at[slot, kind], qkv_sem.at[slot, kind]
            )
            for kind in range(3)
        ] + [
            pltpu.make_async_copy(
                src.at[:, pl.ds(pl.multiple_of(p * 128, 128), 128)],
                qkv.at[slot, kind],
                qkv_sem.at[slot, kind],
            )
            for kind, src in ((3, mixed_h), (4, grad_mixed_h))
        ]

    for c in pair_copies(0, 0):
        c.start()
    normed_copy = pltpu.make_async_copy(normed_h, dtok, w_sem.at[1])
    normed_copy.start()
    greet(n_dp, n_seq)

    def reducer(i, grad, own, local):
        acc, core_in, steps, z_in = sets[i]
        sems = {
            "core": (c_send.at[i], c_recv.at[i], c_local.at[i]),
            "step": (s_send.at[i], s_recv.at[i]),
            "z": (z_send.at[i], z_recv.at[i]),
        }
        return GradReduce(grad, own, local, core_in, steps, z_in, sems, n_dp, n_seq)

    acc_r = sets[0][0]
    rest = reducer(
        0,
        grad_rest,
        lambda lead, z, cols: acc_r.at[tuple(lead) + (z, slice(None), cols)],
        True,
    )

    def chunk_reducer(c):
        stage = sets[1 + c][0]
        return reducer(
            1 + c,
            stage,
            lambda lead, z, cols: stage.at[tuple(lead) + (core, z, slice(None), cols)],
            False,
        )

    parts = [chunk_reducer(c) for c in range(chunks)]
    order = [0, n_seq - 1] + list(range(1, n_seq - 1))
    for z in order:
        rest.core_start(z)

    def down_copy(z):
        return remote(
            down_h.at[z], down_in.at[s], down_send.at[z], down_recv.at[s], d, z
        )

    down_own = pltpu.make_async_copy(down_h.at[s], down_in.at[s], down_send.at[s])
    down_own.start()
    for z in range(n_seq):

        @pl.when(z != s)
        def _():
            down_copy(z).start()

    w_copy = pltpu.make_async_copy(wq_h, w, w_sem.at[0])
    w_copy.start()
    returned = RowReturn(dtok, dtok_o, row_send, row_recv, rows, n_seq)

    normed_copy.wait()
    for r in range(n_seq):
        normed_t[:, pl.ds(r * length, length)] = jnp.transpose(dtok[r])

    def weight_chunk(c):
        stage = sets[1 + c][0]
        n = width // chunks
        lead = stage.shape[:-2]
        for kind in range(3):
            g = dot(
                normed_t[...],
                grad_qkv[:, kind * width + c * n : kind * width + (c + 1) * n],
                ((1,), (0,)),
            )
            for i in range(n_dp * n_seq):
                k, idx = i, []
                for size in lead[::-1]:
                    idx.append(k % size)
                    k //= size
                stage[tuple(idx[::-1]) + (slice(None), pl.ds(kind * n, n))] = g[
                    i * depth : (i + 1) * depth
                ].astype(BF16)
        for z in range(n_seq):
            parts[c].core_start(z)

    def chunk_event(c, t):
        for z in range(n_seq):
            if t == 0:
                parts[c].core_add(z)
            parts[c].event(z, t)

    def run(what, *args):
        if what == "add":
            rest.core_add(order[args[0]])
        elif what == "rest":
            rest.event(order[args[0]], args[1])
        elif what == "grad":
            weight_chunk(*args)
        else:
            chunk_event(*args)

    run("add", 0)
    run("rest", 0, 0)
    run("add", 1)
    run("rest", 1, 0)
    slots = {
        0: [("add", 2), ("add", 3)],
        1: [("rest", 0, 1), ("rest", 2, 0)],
        2: [("rest", 1, 1), ("rest", 3, 0)],
        3: [("rest", 0, 2), ("grad", 0)],
        4: [("rest", 2, 1), ("rest", 1, 2), ("chunk", 0, 0)],
        5: [("rest", 3, 1)],
        6: [("rest", 2, 2), ("chunk", 0, 1)],
        7: [("rest", 3, 2), ("grad", 1)],
        8: [("chunk", 0, 2), ("chunk", 1, 0)],
        10: [("chunk", 1, 1)],
        11: [("chunk", 1, 2)],
    }
    tail = [[], [("grad", 2)], [], [("chunk", 2, 0)]]
    block = seq_len // 2
    lane = lax.broadcasted_iota(jnp.int32, (seq_len, 128), 1)
    if m != 2:
        slots, tail = {3: [("grad", 0)], 7: [("grad", 1)], 11: [("grad", 2)]}, []

    @pl.loop(0, pairs)
    def _(p):
        now = lax.rem(p, 2)

        @pl.when(p + 1 < pairs)
        def _():
            for c in pair_copies(p + 1, 1 - now):
                c.start()

        for c in pair_copies(p, now):
            c.wait()
        queries, keys, values = qkv[now, 0], qkv[now, 1], qkv[now, 2]
        at_p = pl.ds(pl.multiple_of(p * 128, 128), 128)
        grads = qkv[now, 4]
        product = grads.astype(F32) * qkv[now, 3].astype(F32)
        nothing = jnp.zeros_like(grads)
        keys_t[...] = jnp.transpose(keys)
        for j in range(2):
            own = lanes_of(j, grads.shape)
            base = HEAD_DIM * (1 - j) + 8

            def with_terms(x, other, column):
                for n, term in enumerate(split3(column)):
                    other = jnp.where(lane == base + n, term, other)
                return jnp.where(own, x, other)

            inner = jnp.sum(jnp.where(own, product, 0.0), -1, keepdims=True)
            stat = jnp.sum(jnp.where(lane == 2 * p + j, lse[...], 0.0), -1, keepdims=True)
            g2[j] = with_terms(grads, nothing, -inner)
            q2[j] = with_terms(queries, docs[1], -stat)
            k2[j] = jnp.where(own, keys, docs[0])
            v2[j] = jnp.where(own, values, docs[0])
        for i in range(seq_len // block):
            at = pl.ds(i * block, block)
            dvs, dks = [], []
            for j in range(2):
                probs = jnp.exp2(dot(k2[j, at, :], q2[j], ((1,), (1,))))
                ds = probs * dot(v2[j, at, :], g2[j], ((1,), (1,)))
                ds = ds.astype(BF16)
                dvs.append(dot(probs.astype(BF16), grads, ((1,), (0,))))
                dks.append(dot(ds, queries, ((1,), (0,))))
                dq = dot(keys_t[:, at], ds, ((1,), (0,)))
                if i == 0:
                    dq2[j] = dq
                else:
                    dq2[j] += dq
            here = lanes_of(0, dvs[0].shape)
            dk = jnp.where(here, dks[0], dks[1]) * (1.0 / LOG2E)
            grad_qkv[at, pl.ds(pl.multiple_of(width + p * 128, 128), 128)] = (
                dk * cos[at, :] + swap_halves(dk * sin[at, :])
            ).astype(BF16)
            grad_qkv[at, pl.ds(pl.multiple_of(2 * width + p * 128, 128), 128)] = jnp.where(
                here, dvs[0], dvs[1]
            ).astype(BF16)
            if i == seq_len // block - 1:
                row = lax.broadcasted_iota(jnp.int32, dq2.shape[1:], 0)
                dq = jnp.where(row < HEAD_DIM, dq2[0], dq2[1])
                dq = jnp.transpose(dq) * (1.0 / math.sqrt(HEAD_DIM))
                grad_qkv[:, at_p] = (dq * cos[...] + swap_halves(dq * sin[...])).astype(
                    BF16
                )
            for slot, events in slots.items():
                if slot % 2 != i:
                    continue

                @pl.when(p == slot // 2)
                def _():
                    for e in events:
                        run(*e)

    w_copy.wait()
    gain = mod[6:7, :]
    scale = 1.0 + mod[1:2, :]
    gmod[...] = gm_in[...]
    offs = [n_seq // 2] + [off for off in range(1, n_seq) if off != n_seq // 2] + [0]
    for r, off in enumerate(offs):
        to = lax.rem(s + off, n_seq)
        at = pl.ds(pl.multiple_of(to * length, length), length)
        e = dot(grad_qkv[at, :], w[...], ((1,), (1,)))
        normal, rstd = normalise(tok[at, :].astype(F32))
        gmod[0:1, :] += jnp.sum(e, 0, keepdims=True)
        weighted = jnp.sum(e * normal, 0, keepdims=True)
        gmod[1:2, :] += weighted * gain
        gmod[6:7, :] += weighted * scale
        h = e * (gain * scale)
        mean_h = jnp.mean(h, -1, keepdims=True)
        mean_hz = jnp.mean(h * normal, -1, keepdims=True)
        dtok[to] = (grad_mid[at, :] + (h - mean_h - normal * mean_hz) * rstd).astype(BF16)
        if r == 0:
            returned.start([off])
        if r < len(tail):
            for e in tail[r]:
                run(*e)

    own_row = pltpu.make_async_copy(gmod, gmod_o.at[d, mine], g_send.at[0])

    def group_copy(off):
        return remote(
            gmod,
            gmod_o.at[d, mine],
            g_send.at[off],
            g_recv.at[s],
            d,
            lax.rem(s + off, n_seq),
        )

    @pl.when(active)
    def _():
        own_row.start()
        for off in range(1, n_seq):
            group_copy(off).start()

    if m != 2:
        for n in range(n_seq):
            if n > 1:
                run("add", n)
                run("rest", n, 0)
        for t in range(1, m + 1):
            for n in range(n_seq):
                run("rest", n, t)
        for c in range(chunks):
            for t in range(m + 1):
                run("chunk", c, t)
    returned.start(offs[1:])
    if m == 2:
        run("chunk", 2, 1)
        run("chunk", 2, 2)

    @pl.when(active)
    def _():
        own_row.wait()

    for i in range(rows):
        owner = first + i

        @pl.when(owner != s)
        def _():
            remote(
                gmod, gmod_o.at[d, i], g_send.at[0], g_recv.at[owner], d, owner
            ).wait_recv()

    def dp_copy(off):
        return remote(
            gmod_o.at[d], gmod_o.at[d], gd_send.at[off], gd_recv.at[off], xor(d, off), s
        )

    for off in range(1, n_dp):
        dp_copy(off).start()

    total = rest.total()
    go_o[...] = total[:, :width]
    gu_o[...] = total[:, width : width + hidden]
    down_own.wait()
    for off in range(1, n_seq):
        origin = lax.rem(s + off, n_seq)
        remote(
            down_h.at[s],
            down_in.at[origin],
            down_send.at[origin],
            down_recv.at[origin],
            d,
            origin,
        ).wait_recv()
    total = down_in[0].astype(F32)
    for z in range(1, n_seq):
        total += down_in[z].astype(F32)
    for i in range(hidden // width):
        gd_o[i * depth : (i + 1) * depth, :] = total[:, i * width : (i + 1) * width]
    n = width // chunks
    for c in range(chunks):
        total = parts[c].total()
        for kind in range(3):
            gq_o[:, kind * width + c * n : kind * width + (c + 1) * n] = total[
                :, kind * n : (kind + 1) * n
            ]

    for off in range(1, n_dp):
        e = xor(d, off)
        dp_copy(off).wait_send()
        remote(
            gmod_o.at[e], gmod_o.at[e], gd_send.at[off], gd_recv.at[off], e, s
        ).wait_recv()

    @pl.when(active)
    def _():
        for off in range(1, n_seq):
            group_copy(off).wait_send()

    returned.finish()
    for z in range(n_seq):

        @pl.when(z != s)
        def _():
            down_copy(z).wait_send()

    rest.sent()
    for p in parts:
        p.sent()


def back(n_dp, n_seq, rows, hidden, grad_rest, grad_down, hbm_args, vmem_args):
    dma = pltpu.SemaphoreType.DMA
    struct = jax.ShapeDtypeStruct
    m = n_dp.bit_length() - 2
    lead = (2,) * m
    length, width = hbm_args[-1].shape[1:]
    seq_len = length * n_seq
    depth, wide = grad_rest.shape[-2:]
    gmod = vmem_args[-1]
    chunks = 3
    outs = [
        struct((depth, 3 * width), F32),
        struct((depth, width), F32),
        struct((depth, hidden), F32),
        struct((depth * hidden // width, width), F32),
        struct((rows, length, width), BF16),
        struct((n_dp, rows) + gmod.shape, F32),
    ]

    def reduce_scratch(n, acc):
        slabs = [
            pltpu.VMEM(acc + (n_seq, depth, n), BF16),
            pltpu.VMEM(lead + (n_seq, depth, n), BF16),
            pltpu.VMEM((n_seq, depth, n), BF16),
        ]
        for _ in range(2):
            for step in range(m):
                slabs.append(
                    pltpu.VMEM(
                        (n_seq,) + (2,) * (m - 1 - step) + (depth, n // 2), BF16
                    )
                )
        return slabs

    scratch = reduce_scratch(wide, lead)
    for _ in range(chunks):
        scratch += reduce_scratch(3 * width // chunks, lead + (2,))
    count = 1 + chunks
    scratch += (
        [
            pltpu.VMEM(grad_down.shape, BF16),
            pltpu.VMEM((width, 3 * width), BF16),
            pltpu.VMEM((2, 5, seq_len, 128), BF16),
            pltpu.VMEM((width, seq_len), BF16),
            pltpu.VMEM((seq_len, 3 * width), BF16),
            pltpu.VMEM((n_seq, length, width), BF16),
        ]
        + [pltpu.VMEM((2, seq_len, 128), BF16)] * 4
        + [
            pltpu.VMEM((2, 128, seq_len), F32),
            pltpu.VMEM((128, seq_len), BF16),
            pltpu.VMEM(gmod.shape, F32),
            dma((2, 5)),
            dma((2,)),
            dma((n_seq,)),
            dma((rows,)),
            dma((n_seq,)),
            dma((n_seq,)),
            dma((n_dp,)),
            dma((n_dp,)),
            dma((count, n_seq)),
            dma((count, n_seq)),
            dma((count, n_seq)),
            dma((count, n_seq, 2, m)),
            dma((count, n_seq, 2, m)),
            dma((count, n_seq)),
            dma((count, n_seq)),
            dma((n_seq,)),
            dma((n_seq,)),
        ]
    )
    return pl.pallas_call(
        functools.partial(back_kernel, n_dp, n_seq, rows, hidden),
        out_shape=outs,
        in_specs=[ANY] * (2 + len(hbm_args)) + [VMEM] * len(vmem_args),
        out_specs=[VMEM] * 4 + [ANY] * 2,
        scratch_shapes=scratch,
        compiler_params=pltpu.CompilerParams(
            collective_id=1, has_side_effects=True, vmem_limit_bytes=VMEM_LIMIT
        ),
    )(grad_rest, grad_down, *hbm_args, *vmem_args)


def last_kernel(emb, gmods, *refs):
    count = len(refs) // 2 - 1
    grads = refs[:count]
    gwm_o, sum_o, *grads_o = refs[count:]
    n_dp, rows, _, width = gmods.shape
    depth = gwm_o.shape[0]
    features = jnp.transpose(emb[...].reshape(n_dp * 8, 128))[:depth]
    total = gmods[0, 0]
    for k in range(n_dp * rows):
        if k:
            total += gmods[k // rows, k % rows]
    sum_o[...] = total
    for p in range(6):
        acc = jnp.zeros((depth, width), F32)
        for k in range(n_dp * rows):
            e, i = k // rows, k % rows
            acc += features[:, e * 8 + i : e * 8 + i + 1] * gmods[e, i, p : p + 1, :]
        gwm_o[:, p * width : (p + 1) * width] = acc
    for g, o in zip(grads, grads_o):
        o[...] = g[...]


def last_call(emb, gmods, results, depth):
    width = gmods.shape[-1]
    struct = jax.ShapeDtypeStruct
    n = len(results)
    return pl.pallas_call(
        last_kernel,
        out_shape=[struct((depth, 6 * width), F32), struct((8, width), F32)]
        + [struct(g.shape, g.dtype) for g in results],
        in_specs=[VMEM] * (2 + n),
        out_specs=[VMEM] * (2 + n),
        compiler_params=pltpu.CompilerParams(vmem_limit_bytes=VMEM_LIMIT),
    )(emb, gmods, *results)


def rotary_tables(seq_len):
    half = HEAD_DIM // 2
    freq = np.exp(np.float32(-math.log(10000.0)) * np.arange(half, dtype=np.float32) / np.float32(half))
    angles = np.arange(seq_len, dtype=np.float32)[:, None] * freq.astype(np.float32)[None, :]
    cos = np.tile(np.cos(angles), (1, 4)).astype(np.float32)
    sin = np.sin(angles)
    sin = np.concatenate([-sin, sin, -sin, sin], 1).astype(np.float32)
    return jnp.asarray(cos), jnp.asarray(sin)


def time_embed(step_ids, model_dim):
    half_dim = model_dim // 2
    frequency = jnp.exp(-math.log(10000.0) * jnp.arange(half_dim, dtype=jnp.float32) / half_dim)
    angles = step_ids.astype(jnp.float32)[:, None] * frequency[None, :]
    return jnp.concatenate([jnp.cos(angles), jnp.sin(angles)], axis=-1)


def shards(
    n_dp,
    n_seq,
    tokens,
    segments,
    timesteps,
    w_mod,
    b_mod,
    gain_attn,
    w_qkv,
    w_out,
    gain_mlp,
    w_up,
    w_down,
    cotangent,
):
    rows, length, width = tokens.shape
    seq_len = length * n_seq
    hidden = w_up.shape[1]
    d, s = place()
    me = d * n_seq + s
    depth = w_mod.shape[0]
    cos, sin = rotary_tables(seq_len)

    emb = time_embed(timesteps, width).astype(BF16).astype(F32)
    emb = emb.reshape(rows, n_dp, n_seq, depth)
    emb = lax.dynamic_index_in_dim(emb, s, 2, keepdims=False).transpose(1, 0, 2)
    emb = jnp.pad(emb, ((0, 0), (0, 8 - rows), (0, 128 - depth)))
    n = n_dp * n_seq

    def in_place(vector):
        size = vector.shape[0]
        here = lax.broadcasted_iota(jnp.int32, (n, size), 0) == me
        return jnp.where(here, vector.astype(F32)[None, :], 0.0).reshape(-1, width)

    base = jnp.concatenate([in_place(v) for v in (b_mod, gain_attn, gain_mlp)], 0)
    seg = jnp.broadcast_to(segments[:, None, :], (rows, 8, length))

    down = [w_down[i * depth : (i + 1) * depth] for i in range(hidden // width)]
    tok, docs, normed_a, packed, wq, rest, group, mod, emb, mixed, lse = front(
        n_dp,
        n_seq,
        tokens,
        seg,
        emb,
        (w_qkv, jnp.concatenate([w_out, w_up], 1), jnp.concatenate(down, 1)),
        w_mod,
        base,
        cos,
        sin,
    )
    tok = tok.reshape(seq_len, width)
    out, grad_mid, grad_mixed, grad_rest, grad_down, gm_in = middle_call(
        n_dp, n_seq, mixed, tok, cotangent, rest, group, mod, width, hidden
    )
    g_wqkv, g_wout, g_wup, g_wdown, d_tok, gmods = back(
        n_dp,
        n_seq,
        rows,
        hidden,
        grad_rest,
        grad_down,
        (
            wq.reshape(width, 3 * width),
            packed,
            mixed,
            grad_mixed,
            normed_a.reshape(n_seq, length, width),
        ),
        (lse, docs, cos, sin, tok, grad_mid, mod, gm_in),
    )
    g_w_mod, summed, out, d_tok, g_wqkv, g_wout, g_wup, g_wdown = last_call(
        emb, gmods, (out, d_tok, g_wqkv, g_wout, g_wup, g_wdown), depth
    )
    summed = summed.reshape(8 * width)

    def own_part(vector, n):
        return lax.dynamic_slice_in_dim(vector, me * n, n, 0)

    return (
        out,
        d_tok,
        g_w_mod,
        own_part(summed[: 6 * width], b_mod.shape[0]),
        own_part(summed[6 * width : 7 * width], gain_attn.shape[0]),
        g_wqkv,
        g_wout,
        own_part(summed[7 * width :], gain_mlp.shape[0]),
        g_wup,
        g_wdown,
    )


def solution(mesh):
    both = P(("dp", "seq"))
    wide = P(("dp", "seq"), None)
    tokens = P("dp", "seq", None)
    return jax.shard_map(
        functools.partial(shards, mesh.shape["dp"], mesh.shape["seq"]),
        mesh=mesh,
        in_specs=(
            tokens,
            P("dp", "seq"),
            P("dp"),
            wide,
            both,
            both,
            wide,
            wide,
            both,
            wide,
            wide,
            tokens,
        ),
        out_specs=(tokens, tokens, wide, both, both, wide, wide, both, wide, wide),
        check_vma=False,
    )
```

```python
import functools
import math

import jax
import jax.numpy as jnp
import numpy as np
from jax import lax
from jax.experimental import pallas as pl
from jax.experimental.pallas import tpu as pltpu
from jax.sharding import PartitionSpec as P

HEAD_DIM = 64
EPSILON = 1e-06
MASK_FILL = -1e30
MESH = pl.DeviceIdType.MESH
BF16 = jnp.bfloat16
F32 = jnp.float32
ANY = pl.BlockSpec(memory_space=pl.ANY)
VMEM = pl.BlockSpec(memory_space=pltpu.VMEM)
VMEM_LIMIT = 60 * 2**20
LOG2E = math.log2(math.e)


def place():
    return lax.axis_index("dp"), lax.axis_index("seq")


def xor(index, bits):
    return jnp.bitwise_xor(index, bits)


def remote(src, dst, send, recv, dp, seq):
    return pltpu.make_async_remote_copy(
        src_ref=src,
        dst_ref=dst,
        send_sem=send,
        recv_sem=recv,
        device_id=(dp, seq),
        device_id_type=MESH,
    )


def greet(n_dp, n_seq):
    d, s = place()
    barrier = pltpu.get_barrier_semaphore()
    for off in range(1, n_dp):
        pl.semaphore_signal(
            barrier, inc=1, device_id=(xor(d, off), s), device_id_type=MESH
        )
    for off in range(1, n_seq):
        pl.semaphore_signal(
            barrier, inc=1, device_id=(d, lax.rem(s + off, n_seq)), device_id_type=MESH
        )
    pl.semaphore_wait(barrier, n_dp - 1 + n_seq - 1)


def bit_orders(n_dp):
    high = [1 << b for b in range(1, n_dp.bit_length() - 1)]
    return (high + [1], high[::-1] + [1])


def signed(value, sign):
    return value if sign > 0 else -value


class WeightGather:
    def __init__(self, shard, at, own_sem, z_sems, x_sems, cols, n_dp, n_seq):
        self.shard, self.at, self.own_sem = shard, at, own_sem
        self.z_sems, self.x_sems = z_sems, x_sems
        self.n_seq = n_seq
        self.cols = cols // 2
        self.orders = bit_orders(n_dp)
        self.steps = len(self.orders[0])
        self.groups = []
        for h in range(2):
            known = [(0, 0)]
            for step, bit in enumerate(self.orders[h]):
                known += [(off ^ bit, step + 1) for off, _ in known]
            self.groups.append(known)

    def own(self):
        d, s = place()
        return pltpu.make_async_copy(self.shard, self.at(d, s), self.own_sem)

    def z_copy(self, way, k):
        d, s = place()
        origin = s - signed(k - 1, way)
        side = 0 if way > 0 else 1
        send, recv = self.z_sems
        return remote(
            self.shard if k == 1 else self.at(d, origin),
            self.at(d, origin),
            send.at[side, k],
            recv.at[side, k],
            d,
            s + way,
        )

    def direct_copy(self, way, k):
        d, s = place()
        side = 0 if way > 0 else 1
        send, recv = self.z_sems
        return remote(
            self.shard,
            self.at(d, s),
            send.at[side, k],
            recv.at[side, k],
            d,
            s + signed(k, way),
        )

    def direct_each(self, body):
        d, s = place()
        for k in range(1, self.n_seq):
            for way in (1, -1):
                to = s + signed(k, way)

                @pl.when((to >= 0) & (to < self.n_seq))
                def _():
                    body(self.direct_copy(way, k))

    def z_valid(self, way, k):
        d, s = place()
        origin = s - signed(k - 1, way)
        to = s + way
        return (origin >= 0) & (origin < self.n_seq) & (to >= 0) & (to < self.n_seq)

    def half(self, ref, h):
        return ref.at[:, pl.ds(h * self.cols, self.cols)]

    def x_copy(self, origin, h, off, bit, src=None):
        d, s = place()
        dst = self.half(self.at(xor(d, off), origin), h)
        send, recv = self.x_sems
        return remote(
            dst if src is None else self.half(src, h),
            dst,
            send.at[origin, h, off ^ bit],
            recv.at[origin, h, off ^ bit],
            xor(d, bit),
            s,
        )

    def each(self, k, body):
        d, s = place()
        if k == 0:
            body(s, 0)
            return
        for way in (1, -1):
            origin = s - signed(k, way)

            @pl.when((origin >= 0) & (origin < self.n_seq))
            def _():
                body(origin, way)

    def z_start(self, k):
        for way in (1, -1):

            @pl.when(self.z_valid(way, k))
            def _():
                self.z_copy(way, k).start()

    def x_start(self, origin, src=None):
        for h in range(2):
            for bit in self.orders[h]:
                self.x_copy(origin, h, 0, bit, src).start()

    def own_start(self):
        d, s = place()
        self.own().start()
        self.x_start(s, self.shard)

    def passing(self, origin, t):
        for h in range(2):
            for off, step in self.groups[h]:
                if step != t:
                    continue
                self.x_copy(origin, h, off, 0).wait_recv()
                for bit in self.orders[h][t:]:
                    self.x_copy(origin, h, off, bit).start()

    def x_sent(self, origin):
        for h in range(2):
            for off, step in self.groups[h]:
                for bit in self.orders[h][step:]:
                    self.x_copy(origin, h, off, bit).wait_send()

    def event(self, k, t, forward=True, across=True):
        if t:
            self.each(k, lambda origin, way: self.passing(origin, t))
            return
        d, s = place()
        send, recv = self.z_sems

        def arrival(origin, way):
            side = 0 if way > 0 else 1
            remote(
                self.shard,
                self.at(d, origin),
                send.at[side, k],
                recv.at[side, k],
                d,
                s,
            ).wait_recv()
            if across:
                self.x_start(origin)

        self.each(k, arrival)
        if forward and k + 1 < self.n_seq:
            self.z_start(k + 1)

    def finish(self, direct=False, across=True):
        if direct:
            self.direct_each(lambda copy: copy.wait_send())
        else:
            for k in range(1, self.n_seq):
                for way in (1, -1):

                    @pl.when(self.z_valid(way, k))
                    def _():
                        self.z_copy(way, k).wait_send()

        if across:
            for k in range(self.n_seq):
                self.each(k, lambda origin, way: self.x_sent(origin))


def dot(a, b, dims):
    return lax.dot_general(a, b, (dims, ((), ())), preferred_element_type=F32)


def swap_halves(x):
    quarter = HEAD_DIM // 2
    lane = lax.broadcasted_iota(jnp.int32, x.shape, 1)
    return jnp.where(
        lax.rem(lane, HEAD_DIM) < quarter,
        pltpu.roll(x, 128 - quarter, axis=1),
        pltpu.roll(x, quarter, axis=1),
    )


def normalise(x):
    mean = jnp.mean(x, -1, keepdims=True)
    centred = x - mean
    var = jnp.mean(centred * centred, -1, keepdims=True)
    rstd = lax.rsqrt(var + EPSILON)
    return centred * rstd, rstd


def join_slabs(slabs, whole):
    depth = slabs.shape[-2]
    count = math.prod(slabs.shape[:-2])
    group = 16 // math.gcd(16, depth)

    @pl.loop(0, count // group)
    def _(i):
        parts = []
        for j in range(group):
            k, idx = i * group + j, []
            for n in slabs.shape[:-2][::-1]:
                idx.append(lax.rem(k, n))
                k = lax.div(k, n)
            parts.append(slabs[tuple(idx[::-1])])
        rows = group * depth
        whole[pl.ds(pl.multiple_of(i * rows, rows), rows), :] = jnp.concatenate(parts, 0)


def lanes_of(j, shape):
    lane = lax.broadcasted_iota(jnp.int32, shape, 1)
    return lax.div(lane, HEAD_DIM) == j


def front_kernel(n_dp, n_seq, rows, *refs):
    tokens, seg, emb_h, *shards = refs[:6]
    w_mod, base, cos, sin = refs[6:10]
    tok_o, doc_o, norm_o, pack_o, *fulls = refs[10:17]
    mod_o, emb, mixed_o, lse_o = refs[17:21]
    (
        tok,
        segs,
        docs,
        normed,
        packed,
        w_in,
        w,
        values,
        keys,
        mod_in,
        mod_sum,
        mod_row,
        out_sem,
        row_send,
        row_recv,
        mod_send,
        mod_recv,
        modz_send,
        modz_recv,
        own_sem,
        z_send,
        z_recv,
        x_send,
        x_recv,
        part,
        emb_send,
        emb_recv,
    ) = refs[21:]
    d, s = place()
    length, width = tokens.shape[1:]
    seq_len = length * n_seq
    first = lax.rem(d, 2)
    mine = s - first
    active = (mine >= 0) & (mine < rows)
    greet(n_dp, n_seq)

    def mod_copy(off):
        return remote(
            part.at[xor(d, off)],
            mod_in.at[d],
            mod_send.at[off],
            mod_recv.at[off],
            xor(d, off),
            s,
        )

    def emb_copy(off):
        return remote(
            emb_h.at[xor(d, off)],
            emb.at[d],
            emb_send.at[off],
            emb_recv.at[off],
            xor(d, off),
            s,
        )

    emb_own = pltpu.make_async_copy(emb_h.at[d], emb.at[d], emb_send.at[0])
    emb_own.start()
    for off in range(1, n_dp):
        emb_copy(off).start()

    ats = [
        lambda e, z: fulls[0].at[e, z],
        lambda e, z: fulls[1].at[e, z],
        lambda e, z: fulls[2].at[z],
    ]
    qkv, rest, down = [
        WeightGather(
            shards[i],
            ats[i],
            own_sem.at[i],
            (z_send.at[i], z_recv.at[i]),
            (x_send.at[i], x_recv.at[i]) if i < 2 else None,
            shards[i].shape[1],
            n_dp,
            n_seq,
        )
        for i in range(3)
    ]
    qkv.direct_each(lambda copy: copy.start())
    rest.z_start(1)
    down.z_start(1)
    down.own().start()
    qkv.own_start()

    emb_own.wait()
    for off in range(1, n_dp):
        e = xor(d, off)
        remote(
            emb_h.at[d], emb.at[e], emb_send.at[off], emb_recv.at[off], d, s
        ).wait_recv()
    features = emb[...].reshape(n_dp * 8, 128)[:, : w_mod.shape[0]].astype(BF16)
    for k in range(8):
        if k < 6:
            terms = dot(features, w_mod[:, k * width : (k + 1) * width], ((1,), (0,)))
            terms = terms + base[k : k + 1, :]
        for e in range(n_dp):
            for i in range(rows):
                part[e, i, k : k + 1, :] = (
                    terms[e * 8 + i : e * 8 + i + 1] if k < 6 else base[k : k + 1, :]
                )
    for off in range(1, n_dp):
        mod_copy(off).start()

    trio = ((tokens, tok), (seg, segs))

    def row_local(k, i):
        src, dst = trio[k]
        return pltpu.make_async_copy(src.at[i], dst.at[s], row_send.at[k, i])

    def row_remote(k, i):
        src, dst = trio[k]
        return remote(
            src.at[i], dst.at[s], row_send.at[k, i], row_recv.at[k, s], d, first + i
        )

    def row_start(k):
        for i in range(rows):

            @pl.when(first + i == s)
            def _():
                row_local(k, i).start()

            @pl.when(first + i != s)
            def _():
                row_remote(k, i).start()

    def row_sent(k):
        for i in range(rows):

            @pl.when(first + i != s)
            def _():
                row_remote(k, i).wait_send()

    def row_arrival(k, origin):
        src, dst = trio[k]
        remote(
            src.at[0],
            dst.at[origin],
            row_send.at[k, 0],
            row_recv.at[k, origin],
            d,
            origin,
        ).wait_recv()

    def row_own(k):
        for i in range(rows):

            @pl.when(first + i == s)
            def _():
                row_local(k, i).wait()

    def mod_exchange():
        for off in range(1, n_dp):
            remote(
                part.at[d],
                mod_in.at[xor(d, off)],
                mod_send.at[off],
                mod_recv.at[off],
                d,
                s,
            ).wait_recv()
        total = part[d]
        for off in range(1, n_dp):
            total += mod_in[xor(d, off)]
        mod_sum[...] = total
        for i in range(rows):

            @pl.when(first + i == s)
            def _():
                mod_row[s] = mod_sum[i]

            @pl.when(first + i != s)
            def _():
                remote(
                    mod_sum.at[i],
                    mod_row.at[s],
                    modz_send.at[i],
                    modz_recv.at[s],
                    d,
                    first + i,
                ).start()

    @pl.when(jnp.logical_not(active))
    def _():
        tok[...] = jnp.zeros_like(tok)
        segs[...] = jnp.zeros_like(segs)

    row_start(1)
    for k in range(1, n_seq):
        qkv.event(k, 0, forward=False)
    mod_exchange()
    row_start(0)
    for k in range(n_seq):
        qkv.event(k, 1)
    rest.own_start()
    rest.event(1, 0)
    down.event(1, 0, forward=False, across=False)
    for t in range(2, qkv.steps + 1):
        for k in range(n_seq):
            qkv.event(k, t)
    stage = pltpu.make_async_copy(fulls[0], w_in, out_sem.at[0])
    qkv.own().wait()
    stage.start()

    @pl.when(active)
    def _():
        for off in range(1, n_seq):
            row_arrival(1, lax.rem(s + off, n_seq))

    row_own(1)
    lane = lax.broadcasted_iota(jnp.int32, (length, 128), 1)
    lane = lax.rem(lane, HEAD_DIM).astype(F32)
    for z in range(n_seq):
        ids = jnp.transpose(
            jnp.broadcast_to(segs[z, 0:1, :].astype(F32), (128, length))
        )
        same = ids == lane
        at = pl.ds(z * length, length)
        docs[0, at, :] = jnp.where(
            same | ((lane >= 8.0) & (lane < 11.0)), 1.0, 0.0
        ).astype(BF16)
        docs[1, at, :] = jnp.where(same | (lane >= 8.0), 0.0, MASK_FILL).astype(BF16)
    doc_copy = pltpu.make_async_copy(docs, doc_o, out_sem.at[1])
    doc_copy.start()

    stage.wait()
    depth = w_in.shape[2]

    join_slabs(w_in, w)

    @pl.when(active)
    def _():
        for off in range(1, n_seq):
            origin = lax.rem(s + off, n_seq)
            remote(
                mod_sum.at[0],
                mod_row.at[origin],
                modz_send.at[0],
                modz_recv.at[origin],
                d,
                origin,
            ).wait_recv()
        total = mod_row[0]
        for z in range(1, n_seq):
            total += mod_row[z]
        mod_o[...] = total

    @pl.when(jnp.logical_not(active))
    def _():
        mod_o[...] = jnp.zeros_like(mod_o)

    rest.event(0, 1)

    gain = mod_o[6:7, :] * (1.0 + mod_o[1:2, :])
    shift = mod_o[0:1, :]
    row_own(0)
    for off in range(n_seq):
        z = lax.rem(s + off, n_seq)
        if off:

            @pl.when(active)
            def _():
                row_arrival(0, z)

        normal, _ = normalise(tok[z].astype(F32))
        at = pl.ds(pl.multiple_of(z * length, length), length)
        normed[at, :] = (normal * gain + shift).astype(BF16)
    outs = [
        pltpu.make_async_copy(tok, tok_o, out_sem.at[2]),
        pltpu.make_async_copy(normed, norm_o, out_sem.at[3]),
    ]
    for c in outs:
        c.start()

    early = [[(0, 2), (1, 1)], [(2, 0)], [(0, 3)]]
    for kind in range(3):

        @pl.loop(0, width // 256)
        def _(c):
            col = kind * width + c * 256
            wc = w[:, pl.ds(pl.multiple_of(col, 256), 256)]
            for r in range(seq_len // 256):
                at = pl.ds(r * 256, 256)
                y = dot(normed[at, :], wc, ((1,), (0,)))
                for j in range(2):
                    p = y[:, j * 128 : (j + 1) * 128]
                    if kind < 2:
                        p = p * cos[at, :] + swap_halves(p) * sin[at, :]
                    if kind == 0:
                        p = p * (LOG2E / math.sqrt(HEAD_DIM))
                    packed[kind * (width // 128) + c * 2 + j, at, :] = p.astype(BF16)

        for e in early[kind]:
            rest.event(*e)
            if e == (2, 0):
                down.z_start(2)

    pack_copy = pltpu.make_async_copy(packed, pack_o, out_sem.at[4])
    pack_copy.start()
    pairs = width // 128
    slots = {
        0: [(1, 2)],
        1: [(2, 1), (3, 0)],
        2: [(1, 3)],
        3: [(2, 2), (3, 1)],
        4: [(3, 2)],
    }
    done = {e for v in slots.values() for e in v}
    done |= {e for v in early for e in v} | {(1, 0), (0, 1)}

    values[:, 128:] = jnp.ones((seq_len, 128), BF16)
    block = 128
    lse_o[...] = jnp.zeros_like(lse_o)

    @pl.loop(0, pairs)
    def _(p):
        k = packed[pairs + p]
        values[:, :128] = packed[2 * pairs + p]
        for j in range(2):
            keys[j] = jnp.where(lanes_of(j, k.shape), k, docs[0])
        for i in range(seq_len // block):
            at = pl.ds(i * block, block)
            q = packed[p, at, :]
            both = []
            stats = lse_o[at, :]
            lane = lax.broadcasted_iota(jnp.int32, (block, 128), 1)
            for j in range(2):
                own = lanes_of(j, q.shape)
                scores = dot(jnp.where(own, q, docs[1, at, :]), keys[j], ((1,), (1,)))
                top = jnp.max(scores, -1, keepdims=True)
                e = jnp.exp2(scores - top).astype(BF16)
                o = dot(e, values[...], ((1,), (0,)))
                total = o[:, 128:]
                both.append(o[:, :128] / total)
                stats = jnp.where(lane == 2 * p + j, top + jnp.log2(total), stats)
            lse_o[at, :] = stats
            mixed_o[at, pl.ds(pl.multiple_of(p * 128, 128), 128)] = jnp.where(
                lane < HEAD_DIM, both[0], both[1]
            ).astype(BF16)
        for slot, events in slots.items():

            @pl.when(p == slot)
            def _():
                for k, t in events:
                    rest.event(k, t)
                    if (k, t) == (3, 0):
                        down.event(2, 0, across=False)
                    if (k, t) == (3, 2):
                        down.event(3, 0, across=False)

    for t in range(1, rest.steps + 1):
        for k in range(n_seq):
            if (k, t) not in done:
                rest.event(k, t)

    for i in range(rows):

        @pl.when(first + i != s)
        def _():
            remote(
                mod_sum.at[i], mod_row.at[s], modz_send.at[i], modz_recv.at[s], d, first + i
            ).wait_send()

    for off in range(1, n_dp):
        mod_copy(off).wait_send()
    rest.own().wait()
    down.own().wait()
    for c in outs + [doc_copy, pack_copy]:
        c.wait()

    for k in range(2):
        row_sent(k)
    for off in range(1, n_dp):
        emb_copy(off).wait_send()
    qkv.finish(direct=True)
    rest.finish()
    down.finish(across=False)


def front(n_dp, n_seq, tokens, seg, emb, shards, w_mod, base, cos, sin):
    rows, length, width = tokens.shape
    seq_len = length * n_seq
    dma = pltpu.SemaphoreType.DMA
    struct = jax.ShapeDtypeStruct
    pairs = width // 128
    outs = [
        struct((n_seq, length, width), BF16),
        struct((2, seq_len, 128), BF16),
        struct((seq_len, width), BF16),
        struct((3 * pairs, seq_len, 128), BF16),
    ]
    outs += [struct((n_dp, n_seq) + w.shape, BF16) for w in shards[:2]]
    outs += [
        struct((n_seq,) + shards[2].shape, BF16),
        struct((8, width), F32),
        struct(emb.shape, F32),
        struct((seq_len, width), BF16),
        struct((seq_len, 128), F32),
    ]
    return pl.pallas_call(
        functools.partial(front_kernel, n_dp, n_seq, rows),
        out_shape=outs,
        in_specs=[ANY] * 6 + [VMEM] * 4,
        out_specs=[ANY] * 7 + [VMEM] * 4,
        scratch_shapes=[
            pltpu.VMEM((n_seq, length, width), BF16),
            pltpu.VMEM((n_seq,) + seg.shape[1:], jnp.int32),
            pltpu.VMEM((2, seq_len, 128), BF16),
            pltpu.VMEM((seq_len, width), BF16),
            pltpu.VMEM((3 * pairs, seq_len, 128), BF16),
            pltpu.VMEM((n_dp, n_seq) + shards[0].shape, BF16),
            pltpu.VMEM((width, 3 * width), BF16),
            pltpu.VMEM((seq_len, 256), BF16),
            pltpu.VMEM((2, seq_len, 128), BF16),
            pltpu.VMEM((n_dp, rows, 8, width), F32),
            pltpu.VMEM((rows, 8, width), F32),
            pltpu.VMEM((n_seq, 8, width), F32),
            dma((5,)),
            dma((2, rows)),
            dma((2, n_seq)),
            dma((n_dp,)),
            dma((n_dp,)),
            dma((rows,)),
            dma((n_seq,)),
            dma((3,)),
            dma((3, 2, n_seq)),
            dma((3, 2, n_seq)),
            dma((2, n_seq, 2, n_dp)),
            dma((2, n_seq, 2, n_dp)),
            pltpu.VMEM((n_dp, rows, 8, width), F32),
            dma((n_dp,)),
            dma((n_dp,)),
        ],
        compiler_params=pltpu.CompilerParams(
            collective_id=0, has_side_effects=True, vmem_limit_bytes=VMEM_LIMIT
        ),
    )(tokens, seg, emb, *shards, w_mod, base, cos, sin)


class GradReduce:
    def __init__(self, grad, own, local, core_in, step_in, z_in, sems, n_dp, n_seq):
        self.grad, self.own, self.local = grad, own, local
        self.core_in, self.step_in, self.z_in = core_in, step_in, z_in
        self.sems, self.n_seq = sems, n_seq
        self.bits = list(range(n_dp.bit_length() - 2, 0, -1))
        self.m = len(self.bits)
        self.orders = (list(range(self.m)), list(range(self.m))[::-1])
        self.cols = core_in.shape[-1] // 2

    def my(self, dim):
        d, _ = place()
        return lax.rem(lax.div(d, 1 << self.bits[dim]), 2)

    def mine(self):
        return tuple(self.my(dim) for dim in range(self.m))

    def index(self, done, flip=None):
        return tuple(
            self.my(dim)
            if dim in done
            else 1 - self.my(dim)
            if dim == flip
            else slice(None)
            for dim in range(self.m)
        )

    def core_copies(self, z):
        d, s = place()
        core = lax.rem(d, 2)
        lead = (slice(None),) * self.m
        send, recv, local = self.sems["core"]
        copies = [
            remote(
                self.grad.at[lead + (1 - core, z)],
                self.core_in.at[lead + (z,)],
                send.at[z],
                recv.at[z],
                xor(d, 1),
                s,
            )
        ]
        if self.local:
            copies.append(
                pltpu.make_async_copy(
                    self.grad.at[lead + (core, z)],
                    self.own(lead, z, slice(None)),
                    local.at[z],
                )
            )
        return copies

    def core_start(self, z):
        for c in self.core_copies(z):
            c.start()

    def core_add(self, z):
        for c in self.core_copies(z):
            c.wait()

        @pl.loop(0, 1 << self.m)
        def _(n):
            lead = tuple(
                lax.rem(lax.div(n, 1 << (self.m - 1 - dim)), 2) for dim in range(self.m)
            )
            target = self.own(lead, z, slice(None))
            target[...] = target[...] + self.core_in[lead + (z,)]

    def step_copy(self, z, h, step):
        d, s = place()
        order = self.orders[h]
        send, recv = self.sems["step"]
        cols = pl.ds(h * self.cols, self.cols)
        return remote(
            self.own(self.index(order[:step], order[step]), z, cols),
            self.step_in[h][step].at[z],
            send.at[z, h, step],
            recv.at[z, h, step],
            xor(d, 1 << self.bits[order[step]]),
            s,
        )

    def mine_at(self, z):
        return self.own(self.mine(), z, slice(None))

    def z_copy(self, z):
        d, s = place()
        send, recv = self.sems["z"]
        return remote(self.mine_at(z), self.z_in.at[s], send.at[z], recv.at[s], d, z)

    def event(self, z, t):
        for h in range(2):
            if t:
                self.step_copy(z, h, t - 1).wait()
                order = self.orders[h]
                cols = pl.ds(h * self.cols, self.cols)
                free = [dim for dim in range(self.m) if dim not in order[:t]]
                for n in range(1 << len(free)):
                    bits = [(n >> (len(free) - 1 - i)) & 1 for i in range(len(free))]
                    lead = tuple(
                        bits[free.index(dim)] if dim in free else self.my(dim)
                        for dim in range(self.m)
                    )
                    target = self.own(lead, z, cols)
                    target[...] = target[...] + self.step_in[h][t - 1][(z, *bits)]
            if t < self.m:
                self.step_copy(z, h, t).start()
        if t == self.m and self.z_in is not None:
            _, s = place()

            @pl.when(z != s)
            def _():
                self.z_copy(z).start()

    def total(self):
        d, s = place()
        send, recv = self.sems["z"]
        for off in range(1, self.n_seq):
            origin = lax.rem(s + off, self.n_seq)
            remote(
                self.mine_at(s),
                self.z_in.at[origin],
                send.at[origin],
                recv.at[origin],
                d,
                origin,
            ).wait_recv()
        total = self.mine_at(s)[...].astype(F32)
        for off in range(1, self.n_seq):
            total += self.z_in[lax.rem(s + off, self.n_seq)].astype(F32)
        return total

    def sent(self):
        _, s = place()
        for z in range(self.n_seq):

            @pl.when(z != s)
            def _():
                self.z_copy(z).wait_send()


def spread(k, dims):
    idx = []
    for n in dims[::-1]:
        idx.append(k % n if isinstance(k, int) else lax.rem(k, n))
        k = k // n if isinstance(k, int) else lax.div(k, n)
    return tuple(idx[::-1])


GELU_A = math.sqrt(2.0 / math.pi)
GELU_B = 0.044715 * GELU_A


def gelu_both(u):
    square = u * u
    half = 0.5 * jnp.tanh(u * (GELU_B * square + GELU_A)) + 0.5
    value = u * half
    slope = half + value * (1.0 - half) * (6.0 * GELU_B * square + 2.0 * GELU_A)
    return value, slope


class RowReturn:
    def __init__(self, src, dst, send, recv, rows, n_seq):
        self.src, self.dst, self.send, self.recv = src, dst, send, recv
        self.rows, self.n_seq = rows, n_seq
        d, s = place()
        self.first = lax.rem(d, 2)
        self.mine = s - self.first
        self.active = (self.mine >= 0) & (self.mine < rows)

    def local(self):
        _, s = place()
        return pltpu.make_async_copy(
            self.src.at[s], self.dst.at[self.mine], self.send.at[0]
        )

    def remote(self, off):
        d, s = place()
        to = lax.rem(s + off, self.n_seq)
        return remote(
            self.src.at[to],
            self.dst.at[self.mine],
            self.send.at[off],
            self.recv.at[self.mine],
            d,
            to,
        )

    def start(self, offs=None):
        @pl.when(self.active)
        def _():
            for off in range(self.n_seq) if offs is None else offs:
                if off:
                    self.remote(off).start()
                else:
                    self.local().start()

    def finish(self):
        d, s = place()

        @pl.when(self.active)
        def _():
            self.local().wait()
            for off in range(1, self.n_seq):
                self.remote(off).wait_send()

        for i in range(self.rows):

            @pl.when(self.first + i != s)
            def _():
                remote(
                    self.src.at[0],
                    self.dst.at[i],
                    self.send.at[0],
                    self.recv.at[i],
                    d,
                    self.first + i,
                ).wait_recv()


def middle_kernel(n_dp, n_seq, *refs):
    mixed_h, tok_h, cot_h, rest_h, group_h, mod = refs[:6]
    out_o, mid_h, gmixed_h, grad_h, down_h, gm = refs[6:12]
    m = n_dp.bit_length() - 2
    (
        wo,
        wu,
        wd,
        slabs,
        mixed,
        tok,
        cot,
        act,
        slope,
        normed,
        g_mlp,
        g_attn,
        turned,
        out,
        attn,
        mlp,
        sems,
        cot_send,
        cot_recv,
        row_send,
        row_recv,
        c_send,
        c_recv,
        s_send,
        s_recv,
        tiles,
        tile_sem,
        x_send,
        x_recv,
        own_sem,
        core_in,
        *steps,
    ) = refs[12:]
    d, s = place()
    rows = cot_h.shape[0]
    length = cot_h.shape[1]
    seq_len, width = mixed.shape
    hidden = wu.shape[1]
    depth = slabs.shape[-2]
    lead = slabs.shape[:-2]
    count = math.prod(lead)
    everything = (slice(None),) * len(lead)
    ways = hidden // width
    down = width + hidden
    first = lax.rem(d, 2)
    mine = s - first
    active = (mine >= 0) & (mine < rows)
    ins = [
        pltpu.make_async_copy(*args, sems.at[i])
        for i, args in enumerate(
            (
                (rest_h.at[:, pl.ds(0, width)], wo),
                (mixed_h, mixed),
                (tok_h, tok),
                (rest_h.at[:, pl.ds(width, hidden)], wu),
            )
        )
    ]
    for c in ins:
        c.start()
    greet(n_dp, n_seq)
    core = lax.rem(d, 2)
    sums = GradReduce(
        slabs,
        lambda idx, z, cols: slabs.at[tuple(idx) + (core, z, slice(None), cols)],
        False,
        core_in,
        (steps[:m], steps[m:]),
        None,
        {"core": (c_send, c_recv, None), "step": (s_send, s_recv)},
        n_dp,
        n_seq,
    )

    def slab_at(e, z):
        bits = [lax.rem(lax.div(e, 1 << b), 2) for b in range(len(lead) - 1)]
        return slabs.at[tuple(bits[::-1]) + (z,)]

    gather = WeightGather(
        None, slab_at, None, None, (x_send, x_recv), hidden, n_dp, n_seq
    )
    group_own = [
        pltpu.make_async_copy(group_h.at[z], slab_at(d, z), own_sem.at[z])
        for z in range(n_seq)
    ]
    for z in range(n_seq):
        gather.x_start(z, group_h.at[z])
        group_own[z].start()

    def cot_remote(i):
        return remote(
            cot_h.at[i], cot.at[s], cot_send.at[i], cot_recv.at[s], d, first + i
        )

    def cot_local(i):
        return pltpu.make_async_copy(cot_h.at[i], cot.at[s], cot_send.at[i])

    def cot_each(near, far):
        for i in range(rows):
            pl.when(first + i == s)(functools.partial(near, i))
            pl.when(first + i != s)(functools.partial(far, i))

    cot_each(lambda i: cot_local(i).start(), lambda i: cot_remote(i).start())

    @pl.when(jnp.logical_not(active))
    def _():
        cot[...] = jnp.zeros_like(cot)

    for c in ins:
        c.wait()

    shift = mod[3:4, :]
    gain = mod[7:8, :]
    scale = 1.0 + mod[4:5, :]
    gate_a = mod[2:3, :]
    gate_m = mod[5:6, :]
    gm[...] = jnp.zeros_like(gm)
    chunk = 1024
    block = 2 * length
    blocks = [(pl.ds(r * block, block), pl.ds(r * 2, 2)) for r in range(n_seq // 2)]
    three = (2, length, width)

    def middle_of(at):
        return tok[at, :].astype(F32) + gate_a * attn[at, :]

    half = n_seq // 2
    gather_events = [[(z, 1) for z in range(half)], [(z, 1) for z in range(half, n_seq)]]
    gather_events += [
        [(z, t) for z in range(n_seq)] for t in range(2, gather.steps + 1)
    ]
    for at, _ in blocks:
        attn[at, :] = dot(mixed[at, :], wo[...], ((1,), (0,)))
        normal, _ = normalise(middle_of(at))
        normed[at, :] = (normal * (gain * scale) + shift).astype(BF16)

        @pl.loop(0, hidden // chunk)
        def _(c):
            cols = pl.ds(pl.multiple_of(c * chunk, chunk), chunk)
            value, steep = gelu_both(dot(normed[at, :], wu[:, cols], ((1,), (0,))))
            act[at, cols] = value.astype(BF16)
            slope[at, cols] = steep.astype(BF16)

        if gather_events:
            for z, t in gather_events.pop(0):
                gather.passing(z, t)

    def turn(left):
        for r in range(seq_len // 256):
            at = pl.ds(r * 256, 256)
            turned[:, at] = jnp.transpose(left[at, :])

    turn(normed)
    for events in gather_events:
        for z, t in events:
            gather.passing(z, t)
    for z in range(n_seq):
        gather.x_sent(z)
        group_own[z].wait()
    group = 16 // math.gcd(16, depth * ways)

    @pl.loop(0, count // group)
    def _(i):
        parts = [
            slabs[spread(i * group + j, lead) + (slice(None), pl.ds(k * width, width))]
            for j in range(group)
            for k in range(ways)
        ]
        n = group * depth * ways
        wd[pl.ds(pl.multiple_of(i * n, n), n), :] = jnp.concatenate(parts, 0)

    for at, two in blocks:
        mlp_out = dot(act[at, :], wd[...], ((1,), (0,)))
        mlp[at, :] = mlp_out.astype(BF16)
        out[two] = (middle_of(at) + gate_m * mlp_out).astype(BF16).reshape(three)
    returned = RowReturn(out, out_o, row_send, row_recv, rows, n_seq)

    cot_each(lambda i: cot_local(i).wait(), lambda i: None)

    @pl.when(active)
    def _():
        for off in range(1, n_seq):
            origin = lax.rem(s + off, n_seq)
            remote(
                cot_h.at[0],
                cot.at[origin],
                cot_send.at[0],
                cot_recv.at[origin],
                d,
                origin,
            ).wait_recv()

    for at, two in blocks:
        grad = cot[two].reshape(block, width).astype(F32)
        g_mlp[at, :] = (grad * gate_m).astype(BF16)
        gm[5:6, :] += jnp.sum(grad * mlp[at, :].astype(F32), 0, keepdims=True)

    several = math.lcm(128, depth * ways) // (depth * ways)

    @pl.loop(0, count // several)
    def _(i):
        n = several * depth * ways
        at = pl.ds(pl.multiple_of(i * n, n), n)
        g = dot(act[:, at], g_mlp[...], ((0,), (0,)))
        for j in range(several):
            for k in range(ways):
                row = (j * ways + k) * depth
                slabs[
                    spread(i * several + j, lead) + (slice(None), pl.ds(k * width, width))
                ] = g[row : row + depth].astype(BF16)

    returned.start()
    for z in range(n_seq):
        sums.core_start(z)
    todo = [[("add", z) for z in range(n_seq)] + [(z, 0) for z in range(n_seq)]]
    todo += [[(z, t) for z in range(n_seq)] for t in range(1, m + 1)]

    def proceed():
        for z, t in todo.pop(0) if todo else []:
            if z == "add":
                sums.core_add(t)
            else:
                sums.event(z, t)

    for b, (at, two) in enumerate(blocks):
        grad = cot[two].reshape(block, width).astype(F32)

        @pl.loop(0, hidden // chunk)
        def _(c):
            cols = pl.ds(pl.multiple_of(c * chunk, chunk), chunk)
            g_act = dot(g_mlp[at, :], wd[cols, :], ((1,), (1,)))
            slope[at, cols] = (g_act * slope[at, cols].astype(F32)).astype(BF16)

        e = dot(slope[at, :], wu[...], ((1,), (1,)))
        if b == 0:
            proceed()
        gm[3:4, :] += jnp.sum(e, 0, keepdims=True)
        normal, rstd = normalise(middle_of(at))
        weighted = jnp.sum(e * normal, 0, keepdims=True)
        gm[4:5, :] += weighted * gain
        gm[7:8, :] += weighted * scale
        h = e * (gain * scale)
        mean_h = jnp.mean(h, -1, keepdims=True)
        mean_hz = jnp.mean(h * normal, -1, keepdims=True)
        g_mid = grad + (h - mean_h - normal * mean_hz) * rstd
        mlp[at, :] = g_mid.astype(BF16)
        gm[2:3, :] += jnp.sum(g_mid * attn[at, :], 0, keepdims=True)
        g_attn[at, :] = (g_mid * gate_a).astype(BF16)
        g_mixed = dot(g_attn[at, :], wo[...], ((1,), (1,)))
        cot[two] = g_mixed.astype(BF16).reshape(three)
    proceed()

    outs = [
        pltpu.make_async_copy(*args, sems.at[i])
        for i, args in enumerate(((mlp, mid_h), (cot, gmixed_h)))
    ]
    for c in outs:
        c.start()

    tile = 256

    def tile_copy(slot, col):
        return pltpu.make_async_copy(
            tiles.at[slot],
            grad_h.at[everything + (slice(None), pl.ds(col, tile))],
            tile_sem.at[slot],
        )

    def weight_grad(right, start, n, busy):
        @pl.loop(0, n // tile)
        def _(c):
            col = pl.multiple_of(c * tile, tile)
            slot = lax.rem(c, 2)
            g = dot(turned[...], right[:, pl.ds(col, tile)], ((1,), (0,)))

            @pl.when((c >= 2) | busy)
            def _():
                tile_copy(slot, 0).wait()

            for i in range(count):
                tiles[(slot,) + spread(i, lead)] = g[
                    i * depth : (i + 1) * depth
                ].astype(BF16)
            tile_copy(slot, pl.multiple_of(start + col, tile)).start()

    weight_grad(slope, width, hidden, False)
    proceed()
    turn(mixed)
    weight_grad(g_attn, 0, width, True)
    while todo:
        proceed()
    reduced = []
    for z in range(n_seq):
        reduced.append(
            pltpu.make_async_copy(sums.mine_at(z), down_h.at[z], c_send.at[z])
        )
        reduced[-1].start()
    for slot in range(2):
        tile_copy(slot, 0).wait()
    for c in outs + reduced:
        c.wait()
    cot_each(lambda i: None, lambda i: cot_remote(i).wait_send())
    returned.finish()


def middle_call(n_dp, n_seq, mixed, tok, cot, rest, group, mod, width, hidden):
    seq_len = mixed.shape[0]
    rows, length = cot.shape[:2]
    depth, wide = rest.shape[-2:]
    m = n_dp.bit_length() - 2
    lead = (2,) * m
    split = lead + (2, n_seq)
    struct = jax.ShapeDtypeStruct
    dma = pltpu.SemaphoreType.DMA
    row = pltpu.VMEM((seq_len, width), BF16)
    cut = pltpu.VMEM((n_seq, length, width), BF16)
    full = pltpu.VMEM((seq_len, hidden), BF16)
    steps = [
        pltpu.VMEM((n_seq,) + (2,) * (m - 1 - step) + (depth, hidden // 2), BF16)
        for _ in range(2)
        for step in range(m)
    ]
    out, mid, g_mixed, grads, down, gm = pl.pallas_call(
        functools.partial(middle_kernel, n_dp, n_seq),
        out_shape=[
            struct(cot.shape, BF16),
            struct((seq_len, width), BF16),
            struct((n_seq, length, width), BF16),
            struct(split + (depth, width + hidden), BF16),
            struct((n_seq, depth, hidden), BF16),
            struct(mod.shape, F32),
        ],
        in_specs=[ANY] * 5 + [VMEM],
        out_specs=[ANY] * 5 + [VMEM],
        scratch_shapes=[
            pltpu.VMEM((width, width), BF16),
            pltpu.VMEM((width, hidden), BF16),
            pltpu.VMEM((hidden, width), BF16),
            pltpu.VMEM(split + (depth, hidden), BF16),
            row,
            row,
            cut,
            full,
            full,
            row,
            row,
            row,
            pltpu.VMEM((width, seq_len), BF16),
            cut,
            pltpu.VMEM((seq_len, width), F32),
            row,
            dma((6,)),
            dma((rows,)),
            dma((n_seq,)),
            dma((n_seq,)),
            dma((rows,)),
            dma((n_seq,)),
            dma((n_seq,)),
            dma((n_seq, 2, m)),
            dma((n_seq, 2, m)),
            pltpu.VMEM((2,) + split + (depth, 256), BF16),
            dma((2,)),
            dma((n_seq, 2, n_dp)),
            dma((n_seq, 2, n_dp)),
            dma((n_seq,)),
            pltpu.VMEM(lead + (n_seq, depth, hidden), BF16),
            *steps,
        ],
        compiler_params=pltpu.CompilerParams(
            collective_id=2, has_side_effects=True, vmem_limit_bytes=VMEM_LIMIT
        ),
    )(
        mixed,
        tok,
        cot,
        rest.reshape(width, wide),
        group,
        mod,
    )
    return out, mid, g_mixed.reshape(seq_len, width), grads, down, gm


def split3(x):
    high = x.astype(BF16)
    x = x - high.astype(F32)
    middle = x.astype(BF16)
    low = (x - middle.astype(F32)).astype(BF16)
    return high, middle, low


def back_kernel(n_dp, n_seq, rows, hidden, *refs):
    grad_rest, down_h, wq_h, packed_h, mixed_h, grad_mixed_h, normed_h = refs[:7]
    lse, docs, cos, sin, tok, grad_mid, mod, gm_in = refs[7:15]
    gq_o, go_o, gu_o, gd_o = refs[15:19]
    dtok_o, gmod_o = refs[19:21]
    refs = refs[21:]
    m = n_dp.bit_length() - 2
    chunks = 3
    sets = []
    for _ in range(1 + chunks):
        acc, core_in, z_in = refs[:3]
        steps = (refs[3 : 3 + m], refs[3 + m : 3 + 2 * m])
        sets.append((acc, core_in, steps, z_in))
        refs = refs[3 + 2 * m :]
    (
        down_in,
        w,
        qkv,
        normed_t,
        grad_qkv,
        dtok,
        q2,
        k2,
        v2,
        g2,
        dq2,
        keys_t,
        gmod,
        qkv_sem,
        w_sem,
        row_send,
        row_recv,
        g_send,
        g_recv,
        gd_send,
        gd_recv,
        c_send,
        c_recv,
        c_local,
        s_send,
        s_recv,
        z_send,
        z_recv,
        down_send,
        down_recv,
    ) = refs
    d, s = place()
    length, width = dtok.shape[1:]
    depth = gq_o.shape[0]
    seq_len = length * n_seq
    pairs = width // 128
    first = lax.rem(d, 2)
    mine = s - first
    active = (mine >= 0) & (mine < rows)
    core = lax.rem(d, 2)

    def pair_copies(p, slot):
        return [
            pltpu.make_async_copy(
                packed_h.at[kind * pairs + p], qkv.at[slot, kind], qkv_sem.at[slot, kind]
            )
            for kind in range(3)
        ] + [
            pltpu.make_async_copy(
                src.at[:, pl.ds(pl.multiple_of(p * 128, 128), 128)],
                qkv.at[slot, kind],
                qkv_sem.at[slot, kind],
            )
            for kind, src in ((3, mixed_h), (4, grad_mixed_h))
        ]

    for c in pair_copies(0, 0):
        c.start()
    normed_copy = pltpu.make_async_copy(normed_h, dtok, w_sem.at[1])
    normed_copy.start()
    greet(n_dp, n_seq)

    def reducer(i, grad, own, local):
        acc, core_in, steps, z_in = sets[i]
        sems = {
            "core": (c_send.at[i], c_recv.at[i], c_local.at[i]),
            "step": (s_send.at[i], s_recv.at[i]),
            "z": (z_send.at[i], z_recv.at[i]),
        }
        return GradReduce(grad, own, local, core_in, steps, z_in, sems, n_dp, n_seq)

    acc_r = sets[0][0]
    rest = reducer(
        0,
        grad_rest,
        lambda lead, z, cols: acc_r.at[tuple(lead) + (z, slice(None), cols)],
        True,
    )

    def chunk_reducer(c):
        stage = sets[1 + c][0]
        return reducer(
            1 + c,
            stage,
            lambda lead, z, cols: stage.at[tuple(lead) + (core, z, slice(None), cols)],
            False,
        )

    parts = [chunk_reducer(c) for c in range(chunks)]
    order = [0, n_seq - 1] + list(range(1, n_seq - 1))
    for z in order:
        rest.core_start(z)

    def down_copy(z):
        return remote(
            down_h.at[z], down_in.at[s], down_send.at[z], down_recv.at[s], d, z
        )

    down_own = pltpu.make_async_copy(down_h.at[s], down_in.at[s], down_send.at[s])
    down_own.start()
    for z in range(n_seq):

        @pl.when(z != s)
        def _():
            down_copy(z).start()

    w_copy = pltpu.make_async_copy(wq_h, w, w_sem.at[0])
    w_copy.start()
    returned = RowReturn(dtok, dtok_o, row_send, row_recv, rows, n_seq)

    normed_copy.wait()
    for r in range(n_seq):
        normed_t[:, pl.ds(r * length, length)] = jnp.transpose(dtok[r])

    def weight_chunk(c):
        stage = sets[1 + c][0]
        n = width // chunks
        lead = stage.shape[:-2]
        for kind in range(3):
            g = dot(
                normed_t[...],
                grad_qkv[:, kind * width + c * n : kind * width + (c + 1) * n],
                ((1,), (0,)),
            )
            for i in range(n_dp * n_seq):
                k, idx = i, []
                for size in lead[::-1]:
                    idx.append(k % size)
                    k //= size
                stage[tuple(idx[::-1]) + (slice(None), pl.ds(kind * n, n))] = g[
                    i * depth : (i + 1) * depth
                ].astype(BF16)
        for z in range(n_seq):
            parts[c].core_start(z)

    def chunk_event(c, t):
        for z in range(n_seq):
            if t == 0:
                parts[c].core_add(z)
            parts[c].event(z, t)

    def run(what, *args):
        if what == "add":
            rest.core_add(order[args[0]])
        elif what == "rest":
            rest.event(order[args[0]], args[1])
        elif what == "grad":
            weight_chunk(*args)
        else:
            chunk_event(*args)

    run("add", 0)
    run("rest", 0, 0)
    run("add", 1)
    run("rest", 1, 0)
    slots = {
        0: [("add", 2), ("add", 3)],
        1: [("rest", 0, 1), ("rest", 2, 0)],
        2: [("rest", 1, 1), ("rest", 3, 0)],
        3: [("rest", 0, 2), ("grad", 0)],
        4: [("rest", 2, 1), ("rest", 1, 2), ("chunk", 0, 0)],
        5: [("rest", 3, 1)],
        6: [("rest", 2, 2), ("chunk", 0, 1)],
        7: [("rest", 3, 2), ("grad", 1)],
        8: [("chunk", 0, 2), ("chunk", 1, 0)],
        10: [("chunk", 1, 1)],
        11: [("chunk", 1, 2)],
    }
    tail = [[], [("grad", 2)], [], [("chunk", 2, 0)]]
    block = seq_len // 2
    lane = lax.broadcasted_iota(jnp.int32, (seq_len, 128), 1)
    if m != 2:
        slots, tail = {3: [("grad", 0)], 7: [("grad", 1)], 11: [("grad", 2)]}, []

    @pl.loop(0, pairs)
    def _(p):
        now = lax.rem(p, 2)

        @pl.when(p + 1 < pairs)
        def _():
            for c in pair_copies(p + 1, 1 - now):
                c.start()

        for c in pair_copies(p, now):
            c.wait()
        queries, keys, values = qkv[now, 0], qkv[now, 1], qkv[now, 2]
        at_p = pl.ds(pl.multiple_of(p * 128, 128), 128)
        grads = qkv[now, 4]
        product = grads.astype(F32) * qkv[now, 3].astype(F32)
        nothing = jnp.zeros_like(grads)
        keys_t[...] = jnp.transpose(keys)
        for j in range(2):
            own = lanes_of(j, grads.shape)
            base = HEAD_DIM * (1 - j) + 8

            def with_terms(x, other, column):
                for n, term in enumerate(split3(column)):
                    other = jnp.where(lane == base + n, term, other)
                return jnp.where(own, x, other)

            inner = jnp.sum(jnp.where(own, product, 0.0), -1, keepdims=True)
            stat = jnp.sum(jnp.where(lane == 2 * p + j, lse[...], 0.0), -1, keepdims=True)
            g2[j] = with_terms(grads, nothing, -inner)
            q2[j] = with_terms(queries, docs[1], -stat)
            k2[j] = jnp.where(own, keys, docs[0])
            v2[j] = jnp.where(own, values, docs[0])
        for i in range(seq_len // block):
            at = pl.ds(i * block, block)
            dvs, dks = [], []
            for j in range(2):
                probs = jnp.exp2(dot(k2[j, at, :], q2[j], ((1,), (1,))))
                ds = probs * dot(v2[j, at, :], g2[j], ((1,), (1,)))
                ds = ds.astype(BF16)
                dvs.append(dot(probs.astype(BF16), grads, ((1,), (0,))))
                dks.append(dot(ds, queries, ((1,), (0,))))
                dq = dot(keys_t[:, at], ds, ((1,), (0,)))
                if i == 0:
                    dq2[j] = dq
                else:
                    dq2[j] += dq
            here = lanes_of(0, dvs[0].shape)
            dk = jnp.where(here, dks[0], dks[1]) * (1.0 / LOG2E)
            grad_qkv[at, pl.ds(pl.multiple_of(width + p * 128, 128), 128)] = (
                dk * cos[at, :] + swap_halves(dk * sin[at, :])
            ).astype(BF16)
            grad_qkv[at, pl.ds(pl.multiple_of(2 * width + p * 128, 128), 128)] = jnp.where(
                here, dvs[0], dvs[1]
            ).astype(BF16)
            if i == seq_len // block - 1:
                row = lax.broadcasted_iota(jnp.int32, dq2.shape[1:], 0)
                dq = jnp.where(row < HEAD_DIM, dq2[0], dq2[1])
                dq = jnp.transpose(dq) * (1.0 / math.sqrt(HEAD_DIM))
                grad_qkv[:, at_p] = (dq * cos[...] + swap_halves(dq * sin[...])).astype(
                    BF16
                )
            for slot, events in slots.items():
                if slot % 2 != i:
                    continue

                @pl.when(p == slot // 2)
                def _():
                    for e in events:
                        run(*e)

    w_copy.wait()
    gain = mod[6:7, :]
    scale = 1.0 + mod[1:2, :]
    gmod[...] = gm_in[...]
    offs = [n_seq // 2] + [off for off in range(1, n_seq) if off != n_seq // 2] + [0]
    for r, off in enumerate(offs):
        to = lax.rem(s + off, n_seq)
        at = pl.ds(pl.multiple_of(to * length, length), length)
        e = dot(grad_qkv[at, :], w[...], ((1,), (1,)))
        normal, rstd = normalise(tok[at, :].astype(F32))
        gmod[0:1, :] += jnp.sum(e, 0, keepdims=True)
        weighted = jnp.sum(e * normal, 0, keepdims=True)
        gmod[1:2, :] += weighted * gain
        gmod[6:7, :] += weighted * scale
        h = e * (gain * scale)
        mean_h = jnp.mean(h, -1, keepdims=True)
        mean_hz = jnp.mean(h * normal, -1, keepdims=True)
        dtok[to] = (grad_mid[at, :] + (h - mean_h - normal * mean_hz) * rstd).astype(BF16)
        if r == 0:
            returned.start([off])
        if r < len(tail):
            for e in tail[r]:
                run(*e)

    own_row = pltpu.make_async_copy(gmod, gmod_o.at[d, mine], g_send.at[0])

    def group_copy(off):
        return remote(
            gmod,
            gmod_o.at[d, mine],
            g_send.at[off],
            g_recv.at[s],
            d,
            lax.rem(s + off, n_seq),
        )

    @pl.when(active)
    def _():
        own_row.start()
        for off in range(1, n_seq):
            group_copy(off).start()

    if m != 2:
        for n in range(n_seq):
            if n > 1:
                run("add", n)
                run("rest", n, 0)
        for t in range(1, m + 1):
            for n in range(n_seq):
                run("rest", n, t)
        for c in range(chunks):
            for t in range(m + 1):
                run("chunk", c, t)
    returned.start(offs[1:])
    if m == 2:
        run("chunk", 2, 1)
        run("chunk", 2, 2)

    @pl.when(active)
    def _():
        own_row.wait()

    for i in range(rows):
        owner = first + i

        @pl.when(owner != s)
        def _():
            remote(
                gmod, gmod_o.at[d, i], g_send.at[0], g_recv.at[owner], d, owner
            ).wait_recv()

    def dp_copy(off):
        return remote(
            gmod_o.at[d], gmod_o.at[d], gd_send.at[off], gd_recv.at[off], xor(d, off), s
        )

    for off in range(1, n_dp):
        dp_copy(off).start()

    total = rest.total()
    go_o[...] = total[:, :width]
    gu_o[...] = total[:, width : width + hidden]
    down_own.wait()
    for off in range(1, n_seq):
        origin = lax.rem(s + off, n_seq)
        remote(
            down_h.at[s],
            down_in.at[origin],
            down_send.at[origin],
            down_recv.at[origin],
            d,
            origin,
        ).wait_recv()
    total = down_in[0].astype(F32)
    for z in range(1, n_seq):
        total += down_in[z].astype(F32)
    for i in range(hidden // width):
        gd_o[i * depth : (i + 1) * depth, :] = total[:, i * width : (i + 1) * width]
    n = width // chunks
    for c in range(chunks):
        total = parts[c].total()
        for kind in range(3):
            gq_o[:, kind * width + c * n : kind * width + (c + 1) * n] = total[
                :, kind * n : (kind + 1) * n
            ]

    for off in range(1, n_dp):
        e = xor(d, off)
        dp_copy(off).wait_send()
        remote(
            gmod_o.at[e], gmod_o.at[e], gd_send.at[off], gd_recv.at[off], e, s
        ).wait_recv()

    @pl.when(active)
    def _():
        for off in range(1, n_seq):
            group_copy(off).wait_send()

    returned.finish()
    for z in range(n_seq):

        @pl.when(z != s)
        def _():
            down_copy(z).wait_send()

    rest.sent()
    for p in parts:
        p.sent()


def back(n_dp, n_seq, rows, hidden, grad_rest, grad_down, hbm_args, vmem_args):
    dma = pltpu.SemaphoreType.DMA
    struct = jax.ShapeDtypeStruct
    m = n_dp.bit_length() - 2
    lead = (2,) * m
    length, width = hbm_args[-1].shape[1:]
    seq_len = length * n_seq
    depth, wide = grad_rest.shape[-2:]
    gmod = vmem_args[-1]
    chunks = 3
    outs = [
        struct((depth, 3 * width), F32),
        struct((depth, width), F32),
        struct((depth, hidden), F32),
        struct((depth * hidden // width, width), F32),
        struct((rows, length, width), BF16),
        struct((n_dp, rows) + gmod.shape, F32),
    ]

    def reduce_scratch(n, acc):
        slabs = [
            pltpu.VMEM(acc + (n_seq, depth, n), BF16),
            pltpu.VMEM(lead + (n_seq, depth, n), BF16),
            pltpu.VMEM((n_seq, depth, n), BF16),
        ]
        for _ in range(2):
            for step in range(m):
                slabs.append(
                    pltpu.VMEM(
                        (n_seq,) + (2,) * (m - 1 - step) + (depth, n // 2), BF16
                    )
                )
        return slabs

    scratch = reduce_scratch(wide, lead)
    for _ in range(chunks):
        scratch += reduce_scratch(3 * width // chunks, lead + (2,))
    count = 1 + chunks
    scratch += (
        [
            pltpu.VMEM(grad_down.shape, BF16),
            pltpu.VMEM((width, 3 * width), BF16),
            pltpu.VMEM((2, 5, seq_len, 128), BF16),
            pltpu.VMEM((width, seq_len), BF16),
            pltpu.VMEM((seq_len, 3 * width), BF16),
            pltpu.VMEM((n_seq, length, width), BF16),
        ]
        + [pltpu.VMEM((2, seq_len, 128), BF16)] * 4
        + [
            pltpu.VMEM((2, 128, seq_len), F32),
            pltpu.VMEM((128, seq_len), BF16),
            pltpu.VMEM(gmod.shape, F32),
            dma((2, 5)),
            dma((2,)),
            dma((n_seq,)),
            dma((rows,)),
            dma((n_seq,)),
            dma((n_seq,)),
            dma((n_dp,)),
            dma((n_dp,)),
            dma((count, n_seq)),
            dma((count, n_seq)),
            dma((count, n_seq)),
            dma((count, n_seq, 2, m)),
            dma((count, n_seq, 2, m)),
            dma((count, n_seq)),
            dma((count, n_seq)),
            dma((n_seq,)),
            dma((n_seq,)),
        ]
    )
    return pl.pallas_call(
        functools.partial(back_kernel, n_dp, n_seq, rows, hidden),
        out_shape=outs,
        in_specs=[ANY] * (2 + len(hbm_args)) + [VMEM] * len(vmem_args),
        out_specs=[VMEM] * 4 + [ANY] * 2,
        scratch_shapes=scratch,
        compiler_params=pltpu.CompilerParams(
            collective_id=1, has_side_effects=True, vmem_limit_bytes=VMEM_LIMIT
        ),
    )(grad_rest, grad_down, *hbm_args, *vmem_args)


def last_kernel(emb, gmods, *refs):
    count = len(refs) // 2 - 1
    grads = refs[:count]
    gwm_o, sum_o, *grads_o = refs[count:]
    n_dp, rows, _, width = gmods.shape
    depth = gwm_o.shape[0]
    features = jnp.transpose(emb[...].reshape(n_dp * 8, 128))[:depth]
    total = gmods[0, 0]
    for k in range(n_dp * rows):
        if k:
            total += gmods[k // rows, k % rows]
    sum_o[...] = total
    for p in range(6):
        acc = jnp.zeros((depth, width), F32)
        for k in range(n_dp * rows):
            e, i = k // rows, k % rows
            acc += features[:, e * 8 + i : e * 8 + i + 1] * gmods[e, i, p : p + 1, :]
        gwm_o[:, p * width : (p + 1) * width] = acc
    for g, o in zip(grads, grads_o):
        o[...] = g[...]


def last_call(emb, gmods, results, depth):
    width = gmods.shape[-1]
    struct = jax.ShapeDtypeStruct
    n = len(results)
    return pl.pallas_call(
        last_kernel,
        out_shape=[struct((depth, 6 * width), F32), struct((8, width), F32)]
        + [struct(g.shape, g.dtype) for g in results],
        in_specs=[VMEM] * (2 + n),
        out_specs=[VMEM] * (2 + n),
        compiler_params=pltpu.CompilerParams(vmem_limit_bytes=VMEM_LIMIT),
    )(emb, gmods, *results)


def rotary_tables(seq_len):
    half = HEAD_DIM // 2
    freq = np.exp(np.float32(-math.log(10000.0)) * np.arange(half, dtype=np.float32) / np.float32(half))
    angles = np.arange(seq_len, dtype=np.float32)[:, None] * freq.astype(np.float32)[None, :]
    cos = np.tile(np.cos(angles), (1, 4)).astype(np.float32)
    sin = np.sin(angles)
    sin = np.concatenate([-sin, sin, -sin, sin], 1).astype(np.float32)
    return jnp.asarray(cos), jnp.asarray(sin)


def time_embed(step_ids, model_dim):
    half_dim = model_dim // 2
    frequency = jnp.exp(-math.log(10000.0) * jnp.arange(half_dim, dtype=jnp.float32) / half_dim)
    angles = step_ids.astype(jnp.float32)[:, None] * frequency[None, :]
    return jnp.concatenate([jnp.cos(angles), jnp.sin(angles)], axis=-1)


def shards(
    n_dp,
    n_seq,
    tokens,
    segments,
    timesteps,
    w_mod,
    b_mod,
    gain_attn,
    w_qkv,
    w_out,
    gain_mlp,
    w_up,
    w_down,
    cotangent,
):
    rows, length, width = tokens.shape
    seq_len = length * n_seq
    hidden = w_up.shape[1]
    d, s = place()
    me = d * n_seq + s
    depth = w_mod.shape[0]
    cos, sin = rotary_tables(seq_len)

    emb = time_embed(timesteps, width).astype(BF16).astype(F32)
    emb = emb.reshape(rows, n_dp, n_seq, depth)
    emb = lax.dynamic_index_in_dim(emb, s, 2, keepdims=False).transpose(1, 0, 2)
    emb = jnp.pad(emb, ((0, 0), (0, 8 - rows), (0, 128 - depth)))
    n = n_dp * n_seq

    def in_place(vector):
        size = vector.shape[0]
        here = lax.broadcasted_iota(jnp.int32, (n, size), 0) == me
        return jnp.where(here, vector.astype(F32)[None, :], 0.0).reshape(-1, width)

    base = jnp.concatenate([in_place(v) for v in (b_mod, gain_attn, gain_mlp)], 0)
    seg = jnp.broadcast_to(segments[:, None, :], (rows, 8, length))

    down = [w_down[i * depth : (i + 1) * depth] for i in range(hidden // width)]
    tok, docs, normed_a, packed, wq, rest, group, mod, emb, mixed, lse = front(
        n_dp,
        n_seq,
        tokens,
        seg,
        emb,
        (w_qkv, jnp.concatenate([w_out, w_up], 1), jnp.concatenate(down, 1)),
        w_mod,
        base,
        cos,
        sin,
    )
    tok = tok.reshape(seq_len, width)
    out, grad_mid, grad_mixed, grad_rest, grad_down, gm_in = middle_call(
        n_dp, n_seq, mixed, tok, cotangent, rest, group, mod, width, hidden
    )
    g_wqkv, g_wout, g_wup, g_wdown, d_tok, gmods = back(
        n_dp,
        n_seq,
        rows,
        hidden,
        grad_rest,
        grad_down,
        (
            wq.reshape(width, 3 * width),
            packed,
            mixed,
            grad_mixed,
            normed_a.reshape(n_seq, length, width),
        ),
        (lse, docs, cos, sin, tok, grad_mid, mod, gm_in),
    )
    g_w_mod, summed, out, d_tok, g_wqkv, g_wout, g_wup, g_wdown = last_call(
        emb, gmods, (out, d_tok, g_wqkv, g_wout, g_wup, g_wdown), depth
    )
    summed = summed.reshape(8 * width)

    def own_part(vector, n):
        return lax.dynamic_slice_in_dim(vector, me * n, n, 0)

    return (
        out,
        d_tok,
        g_w_mod,
        own_part(summed[: 6 * width], b_mod.shape[0]),
        own_part(summed[6 * width : 7 * width], gain_attn.shape[0]),
        g_wqkv,
        g_wout,
        own_part(summed[7 * width :], gain_mlp.shape[0]),
        g_wup,
        g_wdown,
    )


def solution(mesh):
    both = P(("dp", "seq"))
    wide = P(("dp", "seq"), None)
    tokens = P("dp", "seq", None)
    return jax.shard_map(
        functools.partial(shards, mesh.shape["dp"], mesh.shape["seq"]),
        mesh=mesh,
        in_specs=(
            tokens,
            P("dp", "seq"),
            P("dp"),
            wide,
            both,
            both,
            wide,
            wide,
            both,
            wide,
            wide,
            tokens,
        ),
        out_specs=(tokens, tokens, wide, both, both, wide, wide, both, wide, wide),
        check_vma=False,
    )
```
